128 devices in a mesh: graph: 8 (over z, core), feat: 16 (over y, x).
Axes of the slice: x: 4, y: 4, z: 4, core: 2. Of those that a mesh axis runs over, the one named last changes fastest.
Arguments:
- node_features: bfloat16 [131072, 1024], P('graph', 'feat'), may hold values from -6 to 6
- proj_weight: bfloat16 [1024, 512], P('feat'), may hold values from -0.1875 to 0.1875
- relation_weight: bfloat16 [2, 512, 512], replicated, may hold values from -0.25 to 0.25
- att_source: float32 [2, 512], replicated, may hold values from -8 to 8
- att_target: float32 [2, 512], replicated, may hold values from -8 to 8
- edge_mask: int32 [1024, 12, 128, 128], P(('graph', 'feat')), may hold values from 0 to 1, as said below
- relation_ids: int32 [1024, 12], P(('graph', 'feat')), may hold values from 0 to 1
- send_blocks: int32 [128, 8, 4], P(('graph', 'feat')), may hold values from 0 to 7, as said below
- source_slots: int32 [1024, 12], P(('graph', 'feat')), may hold values from 0 to 31
Outputs:
- layer_out: bfloat16 [131072, 512], P(('graph', 'feat'))
The draws below stay inside these ranges and needn't reach their ends.
Inputs may be any that keep to these rules, and one draw needn't show every extreme that they name: `edge_mask`: every target row i has an edge at list position 0 to row i of that source block. `send_blocks`: the 4 entries of one device's list to one graph index are distinct block numbers of that device.
All inputs are finite; a program needn't handle non-finite values.
Results may differ from the reference program's by a relative error of at most 0.034.
Values may be sent and summed in bfloat16 or wider, within the bound.
No kernel may reach another device: no remote copies, remote signals or barrier semaphores. Data moves between devices by JAX's collectives and lax.ppermute only.
A program may use at most 128 MiB of HBM per device.

```python
import jax
import jax.numpy as jnp
from jax import lax

DIN = 1024
HID = 512
HEADS = 4
BR = 128
REL = 2
BLK_DEV = 8
KSRC = 12
CAP = 4
BLOCKS = 1024
NODES = 131072
N_GRAPH = 8
N_FEAT = 16
DEVICES = 128


def draw_att_source(key, part):
    key = jax.random.fold_in(key, 11)
    return jnp.clip(0.18 * jax.random.normal(key, (REL, HID), jnp.float32), -8.0, 8.0)


def draw_att_target(key, part):
    key = jax.random.fold_in(key, 12)
    return jnp.clip(0.18 * jax.random.normal(key, (REL, HID), jnp.float32), -8.0, 8.0)


def draw_edge_mask(key, part):
    key = jax.random.fold_in(key, 13)
    coins = jax.random.randint(key, (BLOCKS, KSRC, BR, BR), 0, KSRC * BR)
    first = (jnp.arange(KSRC) == 0)[None, :, None, None]
    diagonal = (jnp.arange(BR)[:, None] == jnp.arange(BR)[None, :])[None, None]
    return ((coins < 16) | first & diagonal).astype(jnp.int32)


def draw_send_blocks(key, part):
    key = jax.random.fold_in(key, 14)
    keys = jax.random.split(key, DEVICES * N_GRAPH)
    orders = jax.vmap(lambda single: jax.random.permutation(single, BLK_DEV))(keys)
    return orders[:, :CAP].reshape(DEVICES, N_GRAPH, CAP).astype(jnp.int32)


def place_ends(drawn, stream_key, least, high):
    place = [jax.random.randint(jax.random.fold_in(stream_key, axis), (), 0, length) for axis, length in enumerate(drawn.shape)]
    longest = drawn.shape.index(max(drawn.shape))
    beside = place[:longest] + [(place[longest] + 1) % drawn.shape[longest]] + place[longest + 1:]
    return drawn.at[tuple(place)].set(least).at[tuple(beside)].set(high)


def levels(stream_key, dims, pieces, least, largest):
    loudness = 1.0
    for position, blocks in pieces:
        steps = jax.random.uniform(jax.random.fold_in(jax.random.fold_in(stream_key, 6), position), (blocks,), jnp.float32, least / len(pieces), largest / len(pieces))
        loudness = loudness * jnp.repeat(jnp.exp(steps), dims[position] // blocks).reshape((-1,) + (1,) * (len(dims) - 1 - position))
    return loudness


def normal_values(key, dims, deviation, most, pieces=(), kind=jnp.bfloat16):
    values = deviation * jax.random.normal(key, dims, jnp.float32)
    if pieces:
        values = values * levels(key, dims, pieces, -0.22, 0.18)
    return jnp.clip(values, -most, most).astype(kind)


def setup_inputs(seed: int = 0) -> dict:
    seeds = jax.random.split(jax.random.key(seed), 10)
    node_features = normal_values(seeds[0], (NODES, DIN), 1.0, 6.0, ((0, 8), (1, 16)))
    proj_weight = normal_values(seeds[1], (DIN, HID), DIN ** -0.5, 0.1875, ((0, 16),))
    relation_weight = normal_values(seeds[2], (REL, HID, HID), HID ** -0.5, 0.25)
    att_source = draw_att_source(jax.random.fold_in(seeds[9], 71), 0)
    att_target = draw_att_target(jax.random.fold_in(seeds[9], 71), 0)
    edge_mask = draw_edge_mask(jax.random.fold_in(seeds[9], 71), 0)
    relation_ids = place_ends(jax.random.randint(seeds[6], (BLOCKS, KSRC), 0, REL), jax.random.fold_in(seeds[6], 1), 0, REL - 1).astype(jnp.int32)
    send_blocks = draw_send_blocks(jax.random.fold_in(seeds[9], 71), 0)
    source_slots = place_ends(jax.random.randint(seeds[8], (BLOCKS, KSRC), 0, N_GRAPH * CAP), jax.random.fold_in(seeds[8], 1), 0, (N_GRAPH * CAP) - 1).astype(jnp.int32)
    return dict(node_features=node_features, proj_weight=proj_weight, relation_weight=relation_weight, att_source=att_source, att_target=att_target, edge_mask=edge_mask, relation_ids=relation_ids, send_blocks=send_blocks, source_slots=source_slots)


def attend(target_scores, source_scores, live, values, own):
    heads_count = target_scores.shape[1]
    width = values.shape[2]
    lists = target_scores.shape[0]
    rows = target_scores.shape[2]
    lhs = jnp.transpose(target_scores, (1, 2, 0))
    rhs = jnp.transpose(source_scores, (1, 0, 2))
    raw = lhs[:, :, :, None] + rhs[:, None, :, :]
    leaky = jnp.where(raw > 0, raw, 0.2 * raw)
    usable = (jnp.transpose(live, (1, 0, 2)) > 0)[None]
    masked = jnp.where(usable, leaky, -jnp.inf)
    highest = jnp.max(masked, axis=(2, 3), keepdims=True)
    prob = jnp.exp(masked - highest)
    total = jnp.sum(prob, axis=(2, 3))
    weights = prob.astype(jnp.bfloat16).reshape(heads_count, rows, lists * values.shape[1])
    stacked = values.reshape(lists * values.shape[1], heads_count, width // heads_count)
    summed = jnp.einsum("hix,xhd->hid", weights.astype(jnp.float32), stacked.astype(jnp.float32))
    summed = summed / total[:, :, None]
    mixed = jnp.transpose(summed, (1, 0, 2)).reshape(rows, width) + own.astype(jnp.float32)
    return jax.nn.elu(mixed).astype(jnp.bfloat16)


def reference(node_features, proj_weight, relation_weight, att_source, att_target, edge_mask, relation_ids, send_blocks, source_slots):
    head_width = HID // HEADS
    hidden = jnp.dot(node_features, proj_weight, preferred_element_type=jnp.float32).astype(jnp.bfloat16)
    blocks = hidden.reshape(BLOCKS, BR, HID)
    values_all = jnp.stack([jnp.dot(hidden, relation_weight[r], preferred_element_type=jnp.float32).astype(jnp.bfloat16) for r in range(REL)]).reshape(REL, BLOCKS, BR, HID)
    src_heads = values_all.astype(jnp.float32).reshape(REL, BLOCKS, BR, HEADS, head_width)
    source_all = jnp.sum(src_heads * att_source.reshape(REL, 1, 1, HEADS, head_width), axis=-1)
    source_all = jnp.transpose(source_all, (0, 1, 3, 2))
    device_ids = jnp.arange(DEVICES, dtype=jnp.int32)[:, None, None]
    peer_ids = jnp.arange(N_GRAPH, dtype=jnp.int32)[None, :, None]
    slot_ids = jnp.arange(CAP, dtype=jnp.int32)[None, None, :]
    sender = peer_ids * N_FEAT + device_ids % N_FEAT
    frontier = sender * BLK_DEV + send_blocks[sender, device_ids // N_FEAT, slot_ids]
    frontier = frontier.reshape(DEVICES, N_GRAPH * CAP).astype(jnp.int32)
    att_heads = att_target.reshape(REL, HEADS, head_width)

    def one_block(index):
        rels = relation_ids[index]
        sources = frontier[index // BLK_DEV][source_slots[index]]
        chosen = values_all[rels, sources]
        source_scores = source_all[rels, sources]
        own = blocks[index]
        own_heads = own.astype(jnp.float32).reshape(BR, HEADS, head_width)
        target_scores = jnp.sum(own_heads[None] * att_heads[rels][:, None], axis=-1)
        target_scores = jnp.transpose(target_scores, (0, 2, 1))
        return attend(target_scores, source_scores, edge_mask[index], chosen, own)

    result = lax.map(one_block, jnp.arange(BLOCKS, dtype=jnp.int32))
    return result.reshape(NODES, HID)
```

```python
import functools

import jax
import jax.numpy as jnp
from jax import lax
from jax.experimental import pallas as pl
from jax.experimental.pallas import tpu as pltpu
from jax.sharding import PartitionSpec as P

HEADS = 4
LOG2E = 1.4426950408889634
F32 = jnp.float32
BF16 = jnp.bfloat16


def three_parts(x):
    hi = lax.reduce_precision(x, 8, 7)
    rest = x - hi
    mid = lax.reduce_precision(rest, 8, 7)
    return hi.astype(BF16), mid.astype(BF16), (rest - mid).astype(BF16)


def transform_kernel(hid_ref, rw_ref, src_ref, val_ref, score_ref):
    hid = hid_ref[0]
    rows, width = hid.shape
    blocks = val_ref.shape[1]
    relations = rw_ref.shape[0]
    for r in range(relations):
        moved = jnp.dot(hid, rw_ref[r], preferred_element_type=F32).astype(BF16)
        val_ref[0, :, r] = moved.reshape(blocks, rows // blocks, width)
    raw = lax.dot_general(src_ref[...], hid, (((1,), (1,)), ((), ())), preferred_element_type=F32)
    score = raw[0:8] + raw[8:16] + raw[16:24]
    block = rows // blocks
    for c in range(blocks):
        score_ref[0, c] = score[:, c * block : (c + 1) * block]


def transform(frontier, relation_weight, src_vectors):
    peers, cap, block, width = frontier.shape
    relations = relation_weight.shape[0]
    return pl.pallas_call(
        transform_kernel,
        grid=(peers,),
        in_specs=[
            pl.BlockSpec((1, cap * block, width), lambda p: (p, 0, 0)),
            pl.BlockSpec((relations, width, width), lambda p: (0, 0, 0)),
            pl.BlockSpec(src_vectors.shape, lambda p: (0, 0)),
        ],
        out_specs=[
            pl.BlockSpec((1, cap, relations, block, width), lambda p: (p, 0, 0, 0, 0)),
            pl.BlockSpec((1, cap, 8, block), lambda p: (p, 0, 0, 0)),
        ],
        out_shape=[
            jax.ShapeDtypeStruct((peers, cap, relations, block, width), BF16),
            jax.ShapeDtypeStruct((peers, cap, 8, block), F32),
        ],
        compiler_params=pltpu.CompilerParams(vmem_limit_bytes=48 * 1024 * 1024),
        name="transform",
    )(frontier.reshape(peers, cap * block, width), relation_weight, src_vectors)


def attend_kernel(
    rel_ref, slot_ref, own_ref, mask_ref, val_ref, score_ref, tgt_ref, out_ref, tb_ref, log_ref, prob_ref, cat_ref, den_ref
):
    b = pl.program_id(0)
    lists, rows, cols = mask_ref.shape[1:]
    chunk = 32
    own = own_ref[...]
    target = jnp.dot(own, tgt_ref[0], preferred_element_type=F32)
    target += jnp.dot(own, tgt_ref[1], preferred_element_type=F32)
    target += jnp.dot(own, tgt_ref[2], preferred_element_type=F32)
    for r in range(tb_ref.shape[0]):
        for h in range(HEADS):
            c = r * HEADS + h
            tb_ref[r, h] = jnp.broadcast_to(target[:, c : c + 1], (rows, cols))
    rels = [rel_ref[b, k] for k in range(lists)]
    slots = [slot_ref[b, k] for k in range(lists)]
    for k in range(lists):
        cat_ref[k * cols : (k + 1) * cols, :] = val_ref[slots[k], rels[k]]
    for i in range(0, rows, chunk):
        here = slice(i, i + chunk)
        top = [jnp.full((chunk, cols), -jnp.inf, F32) for _ in range(HEADS)]
        for k in range(lists):
            used = mask_ref[0, k, here, :] > 0
            for h in range(HEADS):
                source = score_ref[slots[k], pl.ds(rels[k] * HEADS + h, 1), :]
                raw = tb_ref[rels[k], h, here, :] + source
                logit = jnp.where(used, jnp.maximum(raw, 0.2 * raw), -jnp.inf)
                log_ref[h, k, here, :] = logit
                top[h] = jnp.maximum(top[h], logit)
        for h in range(HEADS):
            highest = jnp.broadcast_to(jnp.max(top[h], axis=1, keepdims=True), (chunk, cols))
            total = jnp.zeros((chunk, cols), F32)
            for k in range(lists):
                prob = jnp.exp2(log_ref[h, k, here, :] - highest)
                total += prob
                prob_ref[h, here, k * cols : (k + 1) * cols] = prob.astype(BF16)
            den_ref[h, here, :] = jnp.broadcast_to(jnp.sum(total, axis=1, keepdims=True), (chunk, cols))
    for h in range(HEADS):
        lanes = slice(h * cols, (h + 1) * cols)
        summed = jnp.dot(prob_ref[h], cat_ref[:, lanes], preferred_element_type=F32)
        mixed = summed / den_ref[h] + own[:, lanes].astype(F32)
        out_ref[:, lanes] = jnp.where(mixed > 0, mixed, jnp.exp(jnp.minimum(mixed, 0.0)) - 1.0).astype(BF16)


def attend(hidden, edge_mask, relation_ids, source_slots, values, scores, tgt_vectors):
    blocks, lists, rows, cols = edge_mask.shape
    width = hidden.shape[1]
    slots, relations = values.shape[:2]
    return pl.pallas_call(
        attend_kernel,
        grid_spec=pltpu.PrefetchScalarGridSpec(
            num_scalar_prefetch=2,
            grid=(blocks,),
            in_specs=[
                pl.BlockSpec((rows, width), lambda b, *_: (b, 0)),
                pl.BlockSpec((1, lists, rows, cols), lambda b, *_: (b, 0, 0, 0)),
                pl.BlockSpec(values.shape, lambda b, *_: (0, 0, 0, 0)),
                pl.BlockSpec(scores.shape, lambda b, *_: (0, 0, 0)),
                pl.BlockSpec(tgt_vectors.shape, lambda b, *_: (0, 0, 0)),
            ],
            out_specs=pl.BlockSpec((rows, width), lambda b, *_: (b, 0)),
            scratch_shapes=[
                pltpu.VMEM((relations, HEADS, rows, cols), F32),
                pltpu.VMEM((HEADS, lists, rows, cols), F32),
                pltpu.VMEM((HEADS, rows, lists * cols), BF16),
                pltpu.VMEM((lists * cols, width), BF16),
                pltpu.VMEM((HEADS, rows, cols), F32),
            ],
        ),
        out_shape=jax.ShapeDtypeStruct(hidden.shape, BF16),
        compiler_params=pltpu.CompilerParams(vmem_limit_bytes=56 * 1024 * 1024),
        name="attend",
    )(relation_ids, source_slots, hidden, edge_mask, values, scores, tgt_vectors)


def score_vectors(relation_weight, att_source, att_target):
    relations, width = att_source.shape
    head_width = width // HEADS
    split = att_source.reshape(relations, HEADS, head_width)
    moved = jnp.einsum(
        "rche,rhe->rhc",
        relation_weight.astype(F32).reshape(relations, width, HEADS, head_width),
        split,
        precision=lax.Precision.HIGHEST,
        preferred_element_type=F32,
    ).reshape(relations * HEADS, width)
    src = jnp.concatenate(three_parts(moved * LOG2E) + (jnp.zeros((8, width), BF16),), axis=0)
    own_head = (jnp.arange(width)[:, None] // head_width) == (jnp.arange(relations * HEADS)[None, :] % HEADS)
    spread = jnp.repeat(att_target.T, HEADS, axis=1)
    tgt = jnp.where(own_head, spread, 0.0) * LOG2E
    tgt = jnp.pad(tgt, ((0, 0), (0, 128 - relations * HEADS)))
    return src, jnp.stack(three_parts(tgt))


def shards(
    node_features,
    proj_weight,
    relation_weight,
    att_source,
    att_target,
    edge_mask,
    relation_ids,
    send_blocks,
    source_slots,
):
    block_rows = edge_mask.shape[-1]
    local_blocks = edge_mask.shape[0]
    rows_local = local_blocks * block_rows
    depth, width = proj_weight.shape
    n_feat = lax.axis_size("feat")
    src_vectors, tgt_vectors = score_vectors(relation_weight, att_source, att_target)
    slices = node_features.T.reshape(depth, n_feat, rows_local).transpose(1, 0, 2)
    weights = jnp.broadcast_to(proj_weight[None], (n_feat, depth, width))
    got = lax.all_to_all(jnp.concatenate([slices, weights], axis=2), "feat", 0, 0, tiled=True)
    got = got.reshape(n_feat * depth, rows_local + width)
    hidden = lax.dot_general(
        got[:, :rows_local], got[:, rows_local:], (((0,), (0,)), ((), ())), preferred_element_type=F32
    ).astype(BF16)
    blocks = hidden.reshape(local_blocks, block_rows, width)
    frontier = lax.all_to_all(blocks[send_blocks[0]], "graph", split_axis=0, concat_axis=0, tiled=True)
    values, scores = transform(frontier, relation_weight, src_vectors)
    slots = values.shape[0] * values.shape[1]
    values = values.reshape((slots,) + values.shape[2:])
    scores = scores.reshape((slots,) + scores.shape[2:])
    return attend(hidden, edge_mask, relation_ids, source_slots, values, scores, tgt_vectors)


def solution(mesh):
    placed = (
        P("graph", "feat"),
        P("feat", None),
        P(),
        P(),
        P(),
        P(("graph", "feat"), None, None, None),
        P(("graph", "feat"), None),
        P(("graph", "feat"), None, None),
        P(("graph", "feat"), None),
    )
    return jax.shard_map(
        shards, mesh=mesh, in_specs=placed, out_specs=P(("graph", "feat"), None), check_vma=False
    )
```

```python
import functools

import jax
import jax.numpy as jnp
from jax import lax
from jax.experimental import pallas as pl
from jax.experimental.pallas import tpu as pltpu
from jax.sharding import PartitionSpec as P

HEADS = 4
CAP = 4
LOG2E = 1.4426950408889634
F32 = jnp.float32
BF16 = jnp.bfloat16


def three_parts(x):
    hi = lax.reduce_precision(x, 8, 7)
    rest = x - hi
    mid = lax.reduce_precision(rest, 8, 7)
    return hi.astype(BF16), mid.astype(BF16), (rest - mid).astype(BF16)


def transform_kernel(bounds, first, idx_ref, *refs):
    n_pieces = sum(len(pieces) for pieces in bounds)
    pieces = refs[:n_pieces]
    rw_ref, src_ref = refs[n_pieces : n_pieces + 2]
    val_ref, score_ref, hid_ref, sem = refs[-4:]
    sources = len(bounds)
    blocks, relations, block = val_ref.shape[1:4]
    now = pl.program_id(0)

    def copy(piece, row, slot, c):
        return pltpu.make_async_copy(
            piece.at[pl.ds(row, block)], hid_ref.at[slot, pl.ds(c * block, block)], sem.at[slot, c]
        )

    def fetch(source):
        begin = sum(len(p) for p in bounds[:source])
        for c in range(blocks):
            wanted = idx_ref[first + source, c]
            for n, (low, high) in enumerate(bounds[source]):

                @pl.when((wanted >= low) & (wanted < high))
                def _():
                    row = pl.multiple_of((wanted - low) * block, block)
                    copy(pieces[begin + n], row, source % 2, c).start()

    @pl.when(now == 0)
    def _():
        fetch(0)

    for source in range(1, sources):

        @pl.when(now == source - 1)
        def _():
            fetch(source)

    slot = lax.rem(now, 2)
    for c in range(blocks):
        copy(pieces[0], 0, slot, c).wait()
    hid = hid_ref[slot]
    for r in range(relations):
        moved = jnp.dot(hid, rw_ref[r], preferred_element_type=F32).astype(BF16)
        val_ref[0, :, r] = moved.reshape(blocks, block, moved.shape[1])
    raw = lax.dot_general(src_ref[...], hid, (((1,), (1,)), ((), ())), preferred_element_type=F32)
    score = raw[0:8] + raw[8:16] + raw[16:24]
    for c in range(blocks):
        score_ref[0, c] = score[:, c * block : (c + 1) * block]


def transform(sources, first, index, relation_weight, src_vectors, block, values, scores):
    bounds = tuple(tuple((low, high) for _, low, high in pieces) for pieces in sources)
    arrays = [array for pieces in sources for array, _, _ in pieces]
    peers, cap = index.shape
    relations, width = relation_weight.shape[:2]
    anywhere = pl.BlockSpec(memory_space=pl.ANY)
    at = len(arrays) + 1 + 2
    kept = () if values is None else (values, scores)
    return pl.pallas_call(
        functools.partial(transform_kernel, bounds, first),
        grid_spec=pltpu.PrefetchScalarGridSpec(
            num_scalar_prefetch=1,
            grid=(len(sources),),
            in_specs=[anywhere] * len(arrays)
            + [
                pl.BlockSpec((relations, width, width), lambda p, *_: (0, 0, 0)),
                pl.BlockSpec(src_vectors.shape, lambda p, *_: (0, 0)),
            ]
            + [anywhere] * len(kept),
            out_specs=[
                pl.BlockSpec((1, cap, relations, block, width), lambda p, *_: (p + first, 0, 0, 0, 0)),
                pl.BlockSpec((1, cap, 8, block), lambda p, *_: (p + first, 0, 0, 0)),
            ],
            scratch_shapes=[pltpu.VMEM((2, cap * block, width), BF16), pltpu.SemaphoreType.DMA((2, cap))],
        ),
        out_shape=[
            jax.ShapeDtypeStruct((peers, cap, relations, block, width), BF16),
            jax.ShapeDtypeStruct((peers, cap, 8, block), F32),
        ],
        input_output_aliases={at + n: n for n in range(len(kept))},
        compiler_params=pltpu.CompilerParams(vmem_limit_bytes=48 * 1024 * 1024),
        name="transform",
    )(index, *arrays, relation_weight, src_vectors, *kept)


def attend_kernel(
    rel_ref, slot_ref, own_ref, mask_ref, val_ref, score_ref, tgt_ref, out_ref, tb_ref, log_ref, prob_ref, cats_ref, den_ref, sem
):
    b = pl.program_id(0)
    lists, rows, cols = mask_ref.shape[1:]
    chunk = 32

    def copy(block, slot, k):
        return pltpu.make_async_copy(
            val_ref.at[slot_ref[block, k], rel_ref[block, k]], cats_ref.at[slot, pl.ds(k * cols, cols)], sem.at[slot, k]
        )

    @pl.when(b == 0)
    def _():
        for k in range(lists):
            copy(0, 0, k).start()

    @pl.when(b + 1 < pl.num_programs(0))
    def _():
        for k in range(lists):
            copy(b + 1, lax.rem(b + 1, 2), k).start()

    half = lax.rem(b, 2)
    own = own_ref[...]
    target = jnp.dot(own, tgt_ref[0], preferred_element_type=F32)
    target += jnp.dot(own, tgt_ref[1], preferred_element_type=F32)
    target += jnp.dot(own, tgt_ref[2], preferred_element_type=F32)
    for r in range(tb_ref.shape[0]):
        for h in range(HEADS):
            c = r * HEADS + h
            tb_ref[r, h] = jnp.broadcast_to(target[:, c : c + 1], (rows, cols))
    rels = [rel_ref[b, k] for k in range(lists)]
    slots = [slot_ref[b, k] for k in range(lists)]
    for i in range(0, rows, chunk):
        here = slice(i, i + chunk)
        top = [jnp.full((chunk, cols), -jnp.inf, F32) for _ in range(HEADS)]
        for k in range(lists):
            used = mask_ref[0, k, here, :] > 0
            for h in range(HEADS):
                source = score_ref[slots[k], pl.ds(rels[k] * HEADS + h, 1), :]
                raw = tb_ref[rels[k], h, here, :] + source
                logit = jnp.where(used, jnp.maximum(raw, 0.2 * raw), -jnp.inf)
                log_ref[h, k, here, :] = logit
                top[h] = jnp.maximum(top[h], logit)
        for h in range(HEADS):
            highest = jnp.broadcast_to(jnp.max(top[h], axis=1, keepdims=True), (chunk, cols))
            total = jnp.zeros((chunk, cols), F32)
            for k in range(lists):
                prob = jnp.exp2(log_ref[h, k, here, :] - highest)
                total += prob
                prob_ref[h, here, k * cols : (k + 1) * cols] = prob.astype(BF16)
            den_ref[h, here, :] = jnp.broadcast_to(jnp.sum(total, axis=1, keepdims=True), (chunk, cols))
    for k in range(lists):
        copy(b, half, k).wait()
    for h in range(HEADS):
        lanes = slice(h * cols, (h + 1) * cols)
        summed = jnp.dot(prob_ref[h], cats_ref[half, :, lanes], preferred_element_type=F32)
        mixed = summed / den_ref[h] + own[:, lanes].astype(F32)
        out_ref[:, lanes] = jnp.where(mixed > 0, mixed, jnp.exp(jnp.minimum(mixed, 0.0)) - 1.0).astype(BF16)


def attend(hidden, edge_mask, relation_ids, source_slots, values, scores, tgt_vectors):
    blocks, lists, rows, cols = edge_mask.shape
    width = hidden.shape[1]
    slots, relations = values.shape[:2]
    return pl.pallas_call(
        attend_kernel,
        grid_spec=pltpu.PrefetchScalarGridSpec(
            num_scalar_prefetch=2,
            grid=(blocks,),
            in_specs=[
                pl.BlockSpec((rows, width), lambda b, *_: (b, 0)),
                pl.BlockSpec((1, lists, rows, cols), lambda b, *_: (b, 0, 0, 0)),
                pl.BlockSpec(memory_space=pl.ANY),
                pl.BlockSpec(scores.shape, lambda b, *_: (0, 0, 0)),
                pl.BlockSpec(tgt_vectors.shape, lambda b, *_: (0, 0, 0)),
            ],
            out_specs=pl.BlockSpec((rows, width), lambda b, *_: (b, 0)),
            scratch_shapes=[
                pltpu.VMEM((relations, HEADS, rows, cols), F32),
                pltpu.VMEM((HEADS, lists, rows, cols), F32),
                pltpu.VMEM((HEADS, rows, lists * cols), BF16),
                pltpu.VMEM((2, lists * cols, width), BF16),
                pltpu.VMEM((HEADS, rows, cols), F32),
                pltpu.SemaphoreType.DMA((2, lists)),
            ],
        ),
        out_shape=jax.ShapeDtypeStruct(hidden.shape, BF16),
        compiler_params=pltpu.CompilerParams(vmem_limit_bytes=56 * 1024 * 1024),
        name="attend",
    )(relation_ids, source_slots, hidden, edge_mask, values, scores, tgt_vectors)


def score_vectors(relation_weight, att_source, att_target):
    relations, width = att_source.shape
    head_width = width // HEADS
    split = att_source.reshape(relations, HEADS, head_width)
    moved = jnp.einsum(
        "rche,rhe->rhc",
        relation_weight.astype(F32).reshape(relations, width, HEADS, head_width),
        split,
        precision=lax.Precision.HIGHEST,
        preferred_element_type=F32,
    ).reshape(relations * HEADS, width)
    src = jnp.concatenate(three_parts(moved * LOG2E) + (jnp.zeros((8, width), BF16),), axis=0)
    own_head = (jnp.arange(width)[:, None] // head_width) == (jnp.arange(relations * HEADS)[None, :] % HEADS)
    spread = jnp.repeat(att_target.T, HEADS, axis=1)
    tgt = jnp.where(own_head, spread, 0.0) * LOG2E
    tgt = jnp.pad(tgt, ((0, 0), (0, 128 - relations * HEADS)))
    return src, jnp.stack(three_parts(tgt))


def shards(
    node_features,
    proj_weight,
    relation_weight,
    att_source,
    att_target,
    edge_mask,
    relation_ids,
    send_blocks,
    source_slots,
):
    block_rows = edge_mask.shape[-1]
    local_blocks = edge_mask.shape[0]
    rows_local = local_blocks * block_rows
    depth, width = proj_weight.shape
    n_feat = lax.axis_size("feat")
    n_graph = lax.axis_size("graph")
    depth_z = n_graph // 2
    place = lax.axis_index("graph")
    core, level = lax.rem(place, 2), place // 2

    def send(x, levels, cores=0):
        pairs = [(p, (p + 2 * levels) % n_graph ^ cores) for p in range(n_graph)]
        return lax.ppermute(x, "graph", pairs)

    cut = 3
    parts = ((0, cut), (cut, local_blocks))
    features = node_features.T.reshape(depth, n_feat, local_blocks, block_rows)

    def slices(low, high):
        return features[:, :, low:high].reshape(depth, n_feat, (high - low) * block_rows).transpose(1, 0, 2)

    half = width // 2
    share = lax.dynamic_slice(proj_weight, (0, core * half), (depth, half))
    share = jnp.broadcast_to(share[None], (n_feat, depth, half))
    got = lax.all_to_all(jnp.concatenate([slices(*parts[0]), share], axis=2), "feat", 0, 0, tiled=True)
    got = got.reshape(n_feat * depth, cut * block_rows + half)
    later = lax.all_to_all(slices(*parts[1]), "feat", 0, 0, tiled=True)
    later = later.reshape(n_feat * depth, (local_blocks - cut) * block_rows)
    mine = got[:, cut * block_rows :]
    other = send(mine, 0, 1)
    whole = jnp.where(core == 0, jnp.concatenate([mine, other], axis=1), jnp.concatenate([other, mine], axis=1))

    src_vectors, tgt_vectors = score_vectors(relation_weight, att_source, att_target)
    tables = lax.all_gather(send_blocks[0], "graph")[:, place]
    relative = jnp.arange(n_graph)
    index = tables[2 * lax.rem(level - relative // 2 + depth_z, depth_z) + (relative % 2 ^ core)]
    peer = source_slots // CAP
    distance = lax.rem(level - peer // 2 + depth_z, depth_z)
    slots = (2 * distance + (peer % 2 ^ core)) * CAP + source_slots % CAP

    hidden = []
    sources = [[] for _ in range(n_graph)]
    for (low, high), x in zip(parts, (got[:, : cut * block_rows], later)):
        part = lax.dot_general(x, whole, (((0,), (0,)), ((), ())), preferred_element_type=F32).astype(BF16)
        hidden.append(part)
        middle = (high - low + (low == 0)) // 2
        split = middle * block_rows
        up, down = send(part, 1), send(part, -1)
        arrived = (
            (0, part, low, high),
            (1, up, low, high),
            (3, down, low, high),
            (2, send(up[:split], 1), low, low + middle),
            (2, send(down[split:], -1), low + middle, high),
        )
        for steps, array, first, end in arrived:
            sources[2 * steps].append((array, first, end))
            sources[2 * steps + 1].append((send(array, 0, 1), first, end))

    values = scores = None
    index = index.astype(jnp.int32)
    for group in ((0, 1), (2, 3), (6, 7), (4, 5)):
        values, scores = transform(
            [sources[s] for s in group], group[0], index, relation_weight, src_vectors, block_rows, values, scores
        )
    total = n_graph * CAP
    values = values.reshape((total,) + values.shape[2:])
    scores = scores.reshape((total,) + scores.shape[2:])
    hidden = jnp.concatenate(hidden, axis=0)
    return attend(hidden, edge_mask, relation_ids, slots, values, scores, tgt_vectors)


def solution(mesh):
    placed = (
        P("graph", "feat"),
        P("feat", None),
        P(),
        P(),
        P(),
        P(("graph", "feat"), None, None, None),
        P(("graph", "feat"), None),
        P(("graph", "feat"), None, None),
        P(("graph", "feat"), None),
    )
    return jax.shard_map(
        shards, mesh=mesh, in_specs=placed, out_specs=P(("graph", "feat"), None), check_vma=False
    )
```

```python
import functools

import jax
import jax.numpy as jnp
from jax import lax
from jax.experimental import pallas as pl
from jax.experimental.pallas import tpu as pltpu
from jax.sharding import PartitionSpec as P

HEADS = 4
CAP = 4
LOG2E = 1.4426950408889634
F32 = jnp.float32
BF16 = jnp.bfloat16


def arrange_kernel(x_ref, out_ref, sem):
    peers, _, rows = out_ref.shape
    copies = [
        pltpu.make_async_copy(x_ref.at[:, pl.ds(q * rows, rows)], out_ref.at[q], sem.at[q]) for q in range(peers)
    ]
    for c in copies:
        c.start()
    for c in copies:
        c.wait()


def arrange(features, peers):
    depth, columns = features.shape
    return pl.pallas_call(
        arrange_kernel,
        in_specs=[pl.BlockSpec(memory_space=pltpu.HBM)],
        out_specs=pl.BlockSpec(memory_space=pltpu.HBM),
        out_shape=jax.ShapeDtypeStruct((peers, depth, columns // peers), BF16),
        scratch_shapes=[pltpu.SemaphoreType.DMA((peers,))],
        name="arrange",
    )(features)


def project_kernel(row_ref, x_ref, mine_ref, other_ref, out_ref, w_ref, sem):
    pieces, part = mine_ref.shape[:2]

    @pl.when(pl.program_id(0) == 0)
    def _():
        copies = []
        for n in range(pieces):
            for which, ref in enumerate((mine_ref, other_ref)):
                row = pl.multiple_of(row_ref[which, n], part)
                copies.append(pltpu.make_async_copy(ref.at[n], w_ref.at[pl.ds(row, part)], sem.at[which, n]))
        for c in copies:
            c.start()
        for c in copies:
            c.wait()

    out_ref[...] = lax.dot_general(
        x_ref[...], w_ref[...], (((0,), (0,)), ((), ())), preferred_element_type=F32
    ).astype(BF16)


def project(x, mine, other, place):
    depth, rows = x.shape
    pieces, part, width = mine.shape
    step = rows // 4
    return pl.pallas_call(
        project_kernel,
        grid_spec=pltpu.PrefetchScalarGridSpec(
            num_scalar_prefetch=1,
            grid=(rows // step,),
            in_specs=[
                pl.BlockSpec((depth, step), lambda i, *_: (0, i)),
                pl.BlockSpec(memory_space=pl.ANY),
                pl.BlockSpec(memory_space=pl.ANY),
            ],
            out_specs=pl.BlockSpec((step, width), lambda i, *_: (i, 0)),
            scratch_shapes=[pltpu.VMEM((depth, width), BF16), pltpu.SemaphoreType.DMA((2, pieces))],
        ),
        out_shape=jax.ShapeDtypeStruct((rows, width), BF16),
        compiler_params=pltpu.CompilerParams(vmem_limit_bytes=32 * 1024 * 1024),
        name="project",
    )(place, x, mine, other)


def three_parts(x):
    hi = lax.reduce_precision(x, 8, 7)
    rest = x - hi
    mid = lax.reduce_precision(rest, 8, 7)
    return hi.astype(BF16), mid.astype(BF16), (rest - mid).astype(BF16)


def transform_kernel(bounds, first, idx_ref, *refs):
    n_pieces = sum(len(pieces) for pieces in bounds)
    pieces = refs[:n_pieces]
    rw_ref, src_ref = refs[n_pieces : n_pieces + 2]
    val_ref, score_ref, hid_ref, sem = refs[-4:]
    sources = len(bounds)
    blocks, relations, block = val_ref.shape[1:4]
    now = pl.program_id(0)

    def copy(piece, row, slot, c):
        return pltpu.make_async_copy(
            piece.at[pl.ds(row, block)], hid_ref.at[slot, pl.ds(c * block, block)], sem.at[slot, c]
        )

    def fetch(source):
        begin = sum(len(p) for p in bounds[:source])
        for c in range(blocks):
            wanted = idx_ref[first + source, c]
            for n, (low, high) in enumerate(bounds[source]):

                @pl.when((wanted >= low) & (wanted < high))
                def _():
                    row = pl.multiple_of((wanted - low) * block, block)
                    copy(pieces[begin + n], row, source % 2, c).start()

    @pl.when(now == 0)
    def _():
        fetch(0)

    for source in range(1, sources):

        @pl.when(now == source - 1)
        def _():
            fetch(source)

    slot = lax.rem(now, 2)
    for c in range(blocks):
        copy(pieces[0], 0, slot, c).wait()
    hid = hid_ref[slot]
    for r in range(relations):
        moved = jnp.dot(hid, rw_ref[r], preferred_element_type=F32).astype(BF16)
        val_ref[0, :, r] = moved.reshape(blocks, block, moved.shape[1])
    raw = lax.dot_general(src_ref[...], hid, (((1,), (1,)), ((), ())), preferred_element_type=F32)
    score = raw[0:8] + raw[8:16] + raw[16:24]
    for c in range(blocks):
        score_ref[0, c] = score[:, c * block : (c + 1) * block]


def transform(sources, first, index, relation_weight, src_vectors, block, values, scores):
    bounds = tuple(tuple((low, high) for _, low, high in pieces) for pieces in sources)
    arrays = [array for pieces in sources for array, _, _ in pieces]
    peers, cap = index.shape
    relations, width = relation_weight.shape[:2]
    anywhere = pl.BlockSpec(memory_space=pl.ANY)
    at = len(arrays) + 1 + 2
    kept = () if values is None else (values, scores)
    return pl.pallas_call(
        functools.partial(transform_kernel, bounds, first),
        grid_spec=pltpu.PrefetchScalarGridSpec(
            num_scalar_prefetch=1,
            grid=(len(sources),),
            in_specs=[anywhere] * len(arrays)
            + [
                pl.BlockSpec((relations, width, width), lambda p, *_: (0, 0, 0)),
                pl.BlockSpec(src_vectors.shape, lambda p, *_: (0, 0)),
            ]
            + [anywhere] * len(kept),
            out_specs=[
                pl.BlockSpec((1, cap, relations, block, width), lambda p, *_: (p + first, 0, 0, 0, 0)),
                pl.BlockSpec((1, cap, 8, block), lambda p, *_: (p + first, 0, 0, 0)),
            ],
            scratch_shapes=[pltpu.VMEM((2, cap * block, width), BF16), pltpu.SemaphoreType.DMA((2, cap))],
        ),
        out_shape=[
            jax.ShapeDtypeStruct((peers, cap, relations, block, width), BF16),
            jax.ShapeDtypeStruct((peers, cap, 8, block), F32),
        ],
        input_output_aliases={at + n: n for n in range(len(kept))},
        compiler_params=pltpu.CompilerParams(vmem_limit_bytes=48 * 1024 * 1024),
        name="transform",
    )(index, *arrays, relation_weight, src_vectors, *kept)


def attend_kernel(
    rel_ref, slot_ref, own_ref, mask_ref, val_ref, score_ref, tgt_ref, out_ref, tb_ref, log_ref, prob_ref, cats_ref, den_ref, sem
):
    b = pl.program_id(0)
    lists, rows, cols = mask_ref.shape[1:]
    chunk = 32

    def copy(block, slot, k):
        return pltpu.make_async_copy(
            val_ref.at[slot_ref[block, k], rel_ref[block, k]], cats_ref.at[slot, pl.ds(k * cols, cols)], sem.at[slot, k]
        )

    @pl.when(b == 0)
    def _():
        for k in range(lists):
            copy(0, 0, k).start()

    @pl.when(b + 1 < pl.num_programs(0))
    def _():
        for k in range(lists):
            copy(b + 1, lax.rem(b + 1, 2), k).start()

    half = lax.rem(b, 2)
    own = own_ref[...]
    target = jnp.dot(own, tgt_ref[0], preferred_element_type=F32)
    target += jnp.dot(own, tgt_ref[1], preferred_element_type=F32)
    target += jnp.dot(own, tgt_ref[2], preferred_element_type=F32)
    for r in range(tb_ref.shape[0]):
        for h in range(HEADS):
            c = r * HEADS + h
            tb_ref[r, h] = jnp.broadcast_to(target[:, c : c + 1], (rows, cols))
    rels = [rel_ref[b, k] for k in range(lists)]
    slots = [slot_ref[b, k] for k in range(lists)]
    for i in range(0, rows, chunk):
        here = slice(i, i + chunk)
        top = [jnp.full((chunk, cols), -jnp.inf, F32) for _ in range(HEADS)]
        for k in range(lists):
            used = mask_ref[0, k, here, :] > 0
            for h in range(HEADS):
                source = score_ref[slots[k], pl.ds(rels[k] * HEADS + h, 1), :]
                raw = tb_ref[rels[k], h, here, :] + source
                logit = jnp.where(used, jnp.maximum(raw, 0.2 * raw), -jnp.inf)
                log_ref[h, k, here, :] = logit
                top[h] = jnp.maximum(top[h], logit)
        for h in range(HEADS):
            highest = jnp.broadcast_to(jnp.max(top[h], axis=1, keepdims=True), (chunk, cols))
            total = jnp.zeros((chunk, cols), F32)
            for k in range(lists):
                prob = jnp.exp2(log_ref[h, k, here, :] - highest)
                total += prob
                prob_ref[h, here, k * cols : (k + 1) * cols] = prob.astype(BF16)
            den_ref[h, here, :] = jnp.broadcast_to(jnp.sum(total, axis=1, keepdims=True), (chunk, cols))
    for k in range(lists):
        copy(b, half, k).wait()
    for h in range(HEADS):
        lanes = slice(h * cols, (h + 1) * cols)
        summed = jnp.dot(prob_ref[h], cats_ref[half, :, lanes], preferred_element_type=F32)
        mixed = summed / den_ref[h] + own[:, lanes].astype(F32)
        out_ref[:, lanes] = jnp.where(mixed > 0, mixed, jnp.exp(jnp.minimum(mixed, 0.0)) - 1.0).astype(BF16)


def attend(hidden, edge_mask, relation_ids, source_slots, values, scores, tgt_vectors):
    blocks, lists, rows, cols = edge_mask.shape
    width = hidden.shape[1]
    slots, relations = values.shape[:2]
    return pl.pallas_call(
        attend_kernel,
        grid_spec=pltpu.PrefetchScalarGridSpec(
            num_scalar_prefetch=2,
            grid=(blocks,),
            in_specs=[
                pl.BlockSpec((rows, width), lambda b, *_: (b, 0)),
                pl.BlockSpec((1, lists, rows, cols), lambda b, *_: (b, 0, 0, 0)),
                pl.BlockSpec(memory_space=pl.ANY),
                pl.BlockSpec(scores.shape, lambda b, *_: (0, 0, 0)),
                pl.BlockSpec(tgt_vectors.shape, lambda b, *_: (0, 0, 0)),
            ],
            out_specs=pl.BlockSpec((rows, width), lambda b, *_: (b, 0)),
            scratch_shapes=[
                pltpu.VMEM((relations, HEADS, rows, cols), F32),
                pltpu.VMEM((HEADS, lists, rows, cols), F32),
                pltpu.VMEM((HEADS, rows, lists * cols), BF16),
                pltpu.VMEM((2, lists * cols, width), BF16),
                pltpu.VMEM((HEADS, rows, cols), F32),
                pltpu.SemaphoreType.DMA((2, lists)),
            ],
        ),
        out_shape=jax.ShapeDtypeStruct(hidden.shape, BF16),
        compiler_params=pltpu.CompilerParams(vmem_limit_bytes=56 * 1024 * 1024),
        name="attend",
    )(relation_ids, source_slots, hidden, edge_mask, values, scores, tgt_vectors)


def score_vectors(relation_weight, att_source, att_target):
    relations, width = att_source.shape
    head_width = width // HEADS
    split = att_source.reshape(relations, HEADS, head_width)
    moved = jnp.einsum(
        "rche,rhe->rhc",
        relation_weight.astype(F32).reshape(relations, width, HEADS, head_width),
        split,
        precision=lax.Precision.HIGHEST,
        preferred_element_type=F32,
    ).reshape(relations * HEADS, width)
    src = jnp.concatenate(three_parts(moved * LOG2E) + (jnp.zeros((8, width), BF16),), axis=0)
    own_head = (jnp.arange(width)[:, None] // head_width) == (jnp.arange(relations * HEADS)[None, :] % HEADS)
    spread = jnp.repeat(att_target.T, HEADS, axis=1)
    tgt = jnp.where(own_head, spread, 0.0) * LOG2E
    tgt = jnp.pad(tgt, ((0, 0), (0, 128 - relations * HEADS)))
    return src, jnp.stack(three_parts(tgt))


def shards(
    node_features,
    proj_weight,
    relation_weight,
    att_source,
    att_target,
    edge_mask,
    relation_ids,
    send_blocks,
    source_slots,
):
    block_rows = edge_mask.shape[-1]
    local_blocks = edge_mask.shape[0]
    rows_local = local_blocks * block_rows
    depth, width = proj_weight.shape
    n_feat = lax.axis_size("feat")
    n_graph = lax.axis_size("graph")
    levels = n_graph // 2
    side = 4
    place = lax.axis_index("graph")
    core, level = lax.rem(place, 2), place // 2

    def send(x, up, cores=0):
        pairs = [(p, (p + 2 * up) % n_graph ^ cores) for p in range(n_graph)]
        return lax.ppermute(x, "graph", pairs)

    def shift(x, right, ahead):
        pairs = [(q, (q // side + ahead) % side * side + (q + right) % side) for q in range(n_feat)]
        return lax.ppermute(x, "feat", pairs)

    outgoing = arrange(node_features.T, n_feat)
    got = lax.all_to_all(outgoing, "feat", 0, 0, tiled=True).reshape(n_feat * depth, rows_local)

    half = depth // 2
    share = lax.dynamic_slice(proj_weight, (core * half, 0), (half, width))
    row = jnp.stack([share] + [shift(share, d, 0) for d in range(1, side)])
    mine = jnp.concatenate([row] + [shift(row, 0, d) for d in range(1, side)])
    other = send(mine, 0, 1)
    here = lax.axis_index("feat")
    piece = jnp.arange(n_feat)
    owner = (here // side - piece // side + side) % side * side + (here - piece + n_feat) % side
    begins = (owner * depth + jnp.stack([core, 1 - core])[:, None] * half).astype(jnp.int32)

    tables = jnp.stack([send_blocks[0]] + [send(send_blocks[0], d) for d in range(1, levels)])
    tables = jnp.stack([tables, send(tables, 0, 1)], axis=1)
    order = jnp.array([0, 1, 3, 2])
    index = tables[order, :, place].reshape(n_graph, CAP)
    peer = source_slots // CAP
    distance = (level - peer // 2 + levels) % levels
    slots = (2 * (distance ^ (distance >> 1)) + (peer % 2 ^ core)) * CAP + source_slots % CAP
    src_vectors, tgt_vectors = score_vectors(relation_weight, att_source, att_target)

    hidden = project(got, mine, other, begins)
    middle = local_blocks // 2
    split = middle * block_rows
    up, down = send(hidden, 1), send(hidden, -1)
    far = (send(up[:split], 1), send(down[split:], -1))
    groups = []
    for arrived in (
        (((hidden, 0, local_blocks),),),
        (((up, 0, local_blocks),), ((down, 0, local_blocks),)),
        (((far[0], 0, middle), (far[1], middle, local_blocks)),),
    ):
        group = []
        for pieces in arrived:
            group.append(pieces)
            group.append([(send(x, 0, 1), low, high) for x, low, high in pieces])
        groups.append(group)
    values = scores = None
    first = 0
    for group in groups:
        values, scores = transform(group, first, index, relation_weight, src_vectors, block_rows, values, scores)
        first += len(group)
    total = n_graph * CAP
    values = values.reshape((total,) + values.shape[2:])
    scores = scores.reshape((total,) + scores.shape[2:])
    return attend(hidden, edge_mask, relation_ids, slots, values, scores, tgt_vectors)


def solution(mesh):
    placed = (
        P("graph", "feat"),
        P("feat", None),
        P(),
        P(),
        P(),
        P(("graph", "feat"), None, None, None),
        P(("graph", "feat"), None),
        P(("graph", "feat"), None, None),
        P(("graph", "feat"), None),
    )
    return jax.shard_map(
        shards, mesh=mesh, in_specs=placed, out_specs=P(("graph", "feat"), None), check_vma=False
    )
```

```python
import functools

import jax
import jax.numpy as jnp
from jax import lax
from jax.experimental import pallas as pl
from jax.experimental.pallas import tpu as pltpu
from jax.sharding import PartitionSpec as P

HEADS = 4
CAP = 4
LOG2E = 1.4426950408889634
F32 = jnp.float32
BF16 = jnp.bfloat16


def arrange_kernel(core_ref, x_ref, w_ref, out_ref):
    peers, _, columns = out_ref.shape
    half = w_ref.shape[1]
    rows = columns - half
    for q in range(peers):
        out_ref[q, :, :rows] = x_ref[:, q * rows : (q + 1) * rows]
        out_ref[q, :, rows:] = w_ref[...]


def arrange(features, weight, core, peers):
    depth, columns = features.shape
    half = weight.shape[1] // 2
    rows = columns // peers
    step = 4
    return pl.pallas_call(
        arrange_kernel,
        grid_spec=pltpu.PrefetchScalarGridSpec(
            num_scalar_prefetch=1,
            grid=(peers // step,),
            in_specs=[
                pl.BlockSpec((depth, step * rows), lambda i, core_ref: (0, i)),
                pl.BlockSpec((depth, half), lambda i, core_ref: (0, core_ref[0])),
            ],
            out_specs=pl.BlockSpec((step, depth, rows + half), lambda i, core_ref: (i, 0, 0)),
        ),
        out_shape=jax.ShapeDtypeStruct((peers, depth, rows + half), BF16),
        name="arrange",
    )(core.reshape(1), features, weight)


def three_parts(x):
    hi = lax.reduce_precision(x, 8, 7)
    rest = x - hi
    mid = lax.reduce_precision(rest, 8, 7)
    return hi.astype(BF16), mid.astype(BF16), (rest - mid).astype(BF16)


def transform_kernel(bounds, first, idx_ref, *refs):
    n_pieces = sum(len(pieces) for pieces in bounds)
    pieces = refs[:n_pieces]
    rw_ref, src_ref = refs[n_pieces : n_pieces + 2]
    val_ref, score_ref, hid_ref, sem = refs[-4:]
    sources = len(bounds)
    blocks, relations, block = val_ref.shape[1:4]
    now = pl.program_id(0)

    def copy(piece, row, slot, c):
        return pltpu.make_async_copy(
            piece.at[pl.ds(row, block)], hid_ref.at[slot, pl.ds(c * block, block)], sem.at[slot, c]
        )

    def fetch(source):
        begin = sum(len(p) for p in bounds[:source])
        for c in range(blocks):
            wanted = idx_ref[first + source, c]
            for n, (low, high) in enumerate(bounds[source]):

                @pl.when((wanted >= low) & (wanted < high))
                def _():
                    row = pl.multiple_of((wanted - low) * block, block)
                    copy(pieces[begin + n], row, source % 2, c).start()

    @pl.when(now == 0)
    def _():
        fetch(0)

    for source in range(1, sources):

        @pl.when(now == source - 1)
        def _():
            fetch(source)

    slot = lax.rem(now, 2)
    for c in range(blocks):
        copy(pieces[0], 0, slot, c).wait()
    hid = hid_ref[slot]
    for r in range(relations):
        moved = jnp.dot(hid, rw_ref[r], preferred_element_type=F32).astype(BF16)
        val_ref[0, :, r] = moved.reshape(blocks, block, moved.shape[1])
    raw = lax.dot_general(src_ref[...], hid, (((1,), (1,)), ((), ())), preferred_element_type=F32)
    score = raw[0:8] + raw[8:16] + raw[16:24]
    for c in range(blocks):
        score_ref[0, c] = score[:, c * block : (c + 1) * block]


def transform(sources, first, index, relation_weight, src_vectors, block, values, scores):
    bounds = tuple(tuple((low, high) for _, low, high in pieces) for pieces in sources)
    arrays = [array for pieces in sources for array, _, _ in pieces]
    peers, cap = index.shape
    relations, width = relation_weight.shape[:2]
    anywhere = pl.BlockSpec(memory_space=pl.ANY)
    at = len(arrays) + 1 + 2
    kept = () if values is None else (values, scores)
    return pl.pallas_call(
        functools.partial(transform_kernel, bounds, first),
        grid_spec=pltpu.PrefetchScalarGridSpec(
            num_scalar_prefetch=1,
            grid=(len(sources),),
            in_specs=[anywhere] * len(arrays)
            + [
                pl.BlockSpec((relations, width, width), lambda p, *_: (0, 0, 0)),
                pl.BlockSpec(src_vectors.shape, lambda p, *_: (0, 0)),
            ]
            + [anywhere] * len(kept),
            out_specs=[
                pl.BlockSpec((1, cap, relations, block, width), lambda p, *_: (p + first, 0, 0, 0, 0)),
                pl.BlockSpec((1, cap, 8, block), lambda p, *_: (p + first, 0, 0, 0)),
            ],
            scratch_shapes=[pltpu.VMEM((2, cap * block, width), BF16), pltpu.SemaphoreType.DMA((2, cap))],
        ),
        out_shape=[
            jax.ShapeDtypeStruct((peers, cap, relations, block, width), BF16),
            jax.ShapeDtypeStruct((peers, cap, 8, block), F32),
        ],
        input_output_aliases={at + n: n for n in range(len(kept))},
        compiler_params=pltpu.CompilerParams(vmem_limit_bytes=48 * 1024 * 1024),
        name="transform",
    )(index, *arrays, relation_weight, src_vectors, *kept)


def attend_kernel(
    rel_ref, slot_ref, own_ref, mask_ref, val_ref, score_ref, tgt_ref, out_ref, tb_ref, log_ref, prob_ref, cats_ref, den_ref, sem
):
    b = pl.program_id(0)
    lists, rows, cols = mask_ref.shape[1:]
    chunk = 32

    def copy(block, slot, k):
        return pltpu.make_async_copy(
            val_ref.at[slot_ref[block, k], rel_ref[block, k]], cats_ref.at[slot, pl.ds(k * cols, cols)], sem.at[slot, k]
        )

    @pl.when(b == 0)
    def _():
        for k in range(lists):
            copy(0, 0, k).start()

    @pl.when(b + 1 < pl.num_programs(0))
    def _():
        for k in range(lists):
            copy(b + 1, lax.rem(b + 1, 2), k).start()

    half = lax.rem(b, 2)
    own = own_ref[...]
    target = jnp.dot(own, tgt_ref[0], preferred_element_type=F32)
    target += jnp.dot(own, tgt_ref[1], preferred_element_type=F32)
    target += jnp.dot(own, tgt_ref[2], preferred_element_type=F32)
    for r in range(tb_ref.shape[0]):
        for h in range(HEADS):
            c = r * HEADS + h
            tb_ref[r, h] = jnp.broadcast_to(target[:, c : c + 1], (rows, cols))
    rels = [rel_ref[b, k] for k in range(lists)]
    slots = [slot_ref[b, k] for k in range(lists)]
    for i in range(0, rows, chunk):
        here = slice(i, i + chunk)
        top = [jnp.full((chunk, cols), -jnp.inf, F32) for _ in range(HEADS)]
        for k in range(lists):
            used = mask_ref[0, k, here, :] > 0
            for h in range(HEADS):
                source = score_ref[slots[k], pl.ds(rels[k] * HEADS + h, 1), :]
                raw = tb_ref[rels[k], h, here, :] + source
                logit = jnp.where(used, jnp.maximum(raw, 0.2 * raw), -jnp.inf)
                log_ref[h, k, here, :] = logit
                top[h] = jnp.maximum(top[h], logit)
        for h in range(HEADS):
            highest = jnp.broadcast_to(jnp.max(top[h], axis=1, keepdims=True), (chunk, cols))
            total = jnp.zeros((chunk, cols), F32)
            for k in range(lists):
                prob = jnp.exp2(log_ref[h, k, here, :] - highest)
                total += prob
                prob_ref[h, here, k * cols : (k + 1) * cols] = prob.astype(BF16)
            den_ref[h, here, :] = jnp.broadcast_to(jnp.sum(total, axis=1, keepdims=True), (chunk, cols))
    for k in range(lists):
        copy(b, half, k).wait()
    for h in range(HEADS):
        lanes = slice(h * cols, (h + 1) * cols)
        summed = jnp.dot(prob_ref[h], cats_ref[half, :, lanes], preferred_element_type=F32)
        mixed = summed / den_ref[h] + own[:, lanes].astype(F32)
        out_ref[:, lanes] = jnp.where(mixed > 0, mixed, jnp.exp(jnp.minimum(mixed, 0.0)) - 1.0).astype(BF16)


def attend(hidden, edge_mask, relation_ids, source_slots, values, scores, tgt_vectors):
    blocks, lists, rows, cols = edge_mask.shape
    width = hidden.shape[1]
    slots, relations = values.shape[:2]
    return pl.pallas_call(
        attend_kernel,
        grid_spec=pltpu.PrefetchScalarGridSpec(
            num_scalar_prefetch=2,
            grid=(blocks,),
            in_specs=[
                pl.BlockSpec((rows, width), lambda b, *_: (b, 0)),
                pl.BlockSpec((1, lists, rows, cols), lambda b, *_: (b, 0, 0, 0)),
                pl.BlockSpec(memory_space=pl.ANY),
                pl.BlockSpec(scores.shape, lambda b, *_: (0, 0, 0)),
                pl.BlockSpec(tgt_vectors.shape, lambda b, *_: (0, 0, 0)),
            ],
            out_specs=pl.BlockSpec((rows, width), lambda b, *_: (b, 0)),
            scratch_shapes=[
                pltpu.VMEM((relations, HEADS, rows, cols), F32),
                pltpu.VMEM((HEADS, lists, rows, cols), F32),
                pltpu.VMEM((HEADS, rows, lists * cols), BF16),
                pltpu.VMEM((2, lists * cols, width), BF16),
                pltpu.VMEM((HEADS, rows, cols), F32),
                pltpu.SemaphoreType.DMA((2, lists)),
            ],
        ),
        out_shape=jax.ShapeDtypeStruct(hidden.shape, BF16),
        compiler_params=pltpu.CompilerParams(vmem_limit_bytes=56 * 1024 * 1024),
        name="attend",
    )(relation_ids, source_slots, hidden, edge_mask, values, scores, tgt_vectors)


def score_vectors(relation_weight, att_source, att_target):
    relations, width = att_source.shape
    head_width = width // HEADS
    split = att_source.reshape(relations, HEADS, head_width)
    moved = jnp.einsum(
        "rche,rhe->rhc",
        relation_weight.astype(F32).reshape(relations, width, HEADS, head_width),
        split,
        precision=lax.Precision.HIGHEST,
        preferred_element_type=F32,
    ).reshape(relations * HEADS, width)
    src = jnp.concatenate(three_parts(moved * LOG2E) + (jnp.zeros((8, width), BF16),), axis=0)
    own_head = (jnp.arange(width)[:, None] // head_width) == (jnp.arange(relations * HEADS)[None, :] % HEADS)
    spread = jnp.repeat(att_target.T, HEADS, axis=1)
    tgt = jnp.where(own_head, spread, 0.0) * LOG2E
    tgt = jnp.pad(tgt, ((0, 0), (0, 128 - relations * HEADS)))
    return src, jnp.stack(three_parts(tgt))


def shards(
    node_features,
    proj_weight,
    relation_weight,
    att_source,
    att_target,
    edge_mask,
    relation_ids,
    send_blocks,
    source_slots,
):
    block_rows = edge_mask.shape[-1]
    local_blocks = edge_mask.shape[0]
    rows_local = local_blocks * block_rows
    depth, width = proj_weight.shape
    n_feat = lax.axis_size("feat")
    n_graph = lax.axis_size("graph")
    levels = n_graph // 2
    place = lax.axis_index("graph")
    core, level = lax.rem(place, 2), place // 2

    def send(x, up, cores=0):
        pairs = [(p, (p + 2 * up) % n_graph ^ cores) for p in range(n_graph)]
        return lax.ppermute(x, "graph", pairs)

    outgoing = arrange(node_features.T, proj_weight, core, n_feat)
    got = lax.all_to_all(outgoing, "feat", 0, 0, tiled=True).reshape(n_feat * depth, rows_local + width // 2)

    tables = jnp.stack([send_blocks[0]] + [send(send_blocks[0], d) for d in range(1, levels)])
    tables = jnp.stack([tables, send(tables, 0, 1)], axis=1)
    order = jnp.array([0, 1, 3, 2])
    index = tables[order, :, place].reshape(n_graph, CAP)
    peer = source_slots // CAP
    distance = (level - peer // 2 + levels) % levels
    slots = (2 * (distance ^ (distance >> 1)) + (peer % 2 ^ core)) * CAP + source_slots % CAP
    src_vectors, tgt_vectors = score_vectors(relation_weight, att_source, att_target)

    got, src_vectors, tgt_vectors, index, slots = lax.optimization_barrier(
        (got, src_vectors, tgt_vectors, index, slots)
    )
    mine = got[:, rows_local:]
    other = send(mine, 0, 1)
    whole = jnp.where(core == 0, jnp.concatenate([mine, other], axis=1), jnp.concatenate([other, mine], axis=1))
    hidden = lax.dot_general(
        got[:, :rows_local], whole, (((0,), (0,)), ((), ())), preferred_element_type=F32
    ).astype(BF16)

    def both(pieces):
        return [pieces, [(send(x, 0, 1), low, high) for x, low, high in pieces]]

    def spread(group, first, kept):
        return transform(group, first, index, relation_weight, src_vectors, block_rows, *kept)

    middle = local_blocks // 2
    split = middle * block_rows
    up, down = send(hidden, 1), send(hidden, -1)
    done = spread(both([(hidden, 0, local_blocks)]), 0, (None, None))
    up, down, done = lax.optimization_barrier((up, down, done))
    far_up, far_down = send(up[:split], 1), send(down[split:], -1)
    done = spread(both([(up, 0, local_blocks)]) + both([(down, 0, local_blocks)]), 2, done)
    far_up, far_down, done = lax.optimization_barrier((far_up, far_down, done))
    values, scores = spread(both([(far_up, 0, middle), (far_down, middle, local_blocks)]), 6, done)
    total = n_graph * CAP
    values = values.reshape((total,) + values.shape[2:])
    scores = scores.reshape((total,) + scores.shape[2:])
    return attend(hidden, edge_mask, relation_ids, slots, values, scores, tgt_vectors)


def solution(mesh):
    placed = (
        P("graph", "feat"),
        P("feat", None),
        P(),
        P(),
        P(),
        P(("graph", "feat"), None, None, None),
        P(("graph", "feat"), None),
        P(("graph", "feat"), None, None),
        P(("graph", "feat"), None),
    )
    return jax.shard_map(
        shards, mesh=mesh, in_specs=placed, out_specs=P(("graph", "feat"), None), check_vma=False
    )
```

```python
import functools

import jax
import jax.numpy as jnp
from jax import lax
from jax.experimental import pallas as pl
from jax.experimental.pallas import tpu as pltpu
from jax.sharding import PartitionSpec as P

HEADS = 4
CAP = 4
LOG2E = 1.4426950408889634
F32 = jnp.float32
BF16 = jnp.bfloat16


def arrange_kernel(low, high, core_ref, x_ref, w_ref, out_ref):
    peers, _, columns = out_ref.shape
    total = x_ref.shape[1] // peers
    rows = high - low
    for q in range(peers):
        out_ref[q, :, :rows] = x_ref[:, q * total + low : q * total + high]
        if columns > rows:
            out_ref[q, :, rows:] = w_ref[...]


def arrange(features, weight, core, peers, low, high, half):
    depth, columns = features.shape
    rows = columns // peers
    step = 4
    return pl.pallas_call(
        functools.partial(arrange_kernel, low, high),
        grid_spec=pltpu.PrefetchScalarGridSpec(
            num_scalar_prefetch=1,
            grid=(peers // step,),
            in_specs=[
                pl.BlockSpec((depth, step * rows), lambda i, core_ref: (0, i)),
                pl.BlockSpec((depth, weight.shape[1] // 2), lambda i, core_ref: (0, core_ref[0])),
            ],
            out_specs=pl.BlockSpec((step, depth, high - low + half), lambda i, core_ref: (i, 0, 0)),
        ),
        out_shape=jax.ShapeDtypeStruct((peers, depth, high - low + half), BF16),
        name="arrange",
    )(core.reshape(1), features, weight)


def three_parts(x):
    hi = lax.reduce_precision(x, 8, 7)
    rest = x - hi
    mid = lax.reduce_precision(rest, 8, 7)
    return hi.astype(BF16), mid.astype(BF16), (rest - mid).astype(BF16)


def transform_kernel(bounds, first, idx_ref, *refs):
    n_pieces = sum(len(pieces) for pieces in bounds)
    pieces = refs[:n_pieces]
    rw_ref, src_ref = refs[n_pieces : n_pieces + 2]
    val_ref, score_ref, hid_ref, sem = refs[-4:]
    sources = len(bounds)
    blocks, relations, block = val_ref.shape[1:4]
    now = pl.program_id(0)

    def copy(piece, row, slot, c):
        return pltpu.make_async_copy(
            piece.at[pl.ds(row, block)], hid_ref.at[slot, pl.ds(c * block, block)], sem.at[slot, c]
        )

    def fetch(source):
        begin = sum(len(p) for p in bounds[:source])
        for c in range(blocks):
            wanted = idx_ref[first + source, c]
            for n, (low, high) in enumerate(bounds[source]):

                @pl.when((wanted >= low) & (wanted < high))
                def _():
                    row = pl.multiple_of((wanted - low) * block, block)
                    copy(pieces[begin + n], row, source % 2, c).start()

    @pl.when(now == 0)
    def _():
        fetch(0)

    for source in range(1, sources):

        @pl.when(now == source - 1)
        def _():
            fetch(source)

    slot = lax.rem(now, 2)
    for c in range(blocks):
        copy(pieces[0], 0, slot, c).wait()
    hid = hid_ref[slot]
    for r in range(relations):
        moved = jnp.dot(hid, rw_ref[r], preferred_element_type=F32).astype(BF16)
        val_ref[0, :, r] = moved.reshape(blocks, block, moved.shape[1])
    raw = lax.dot_general(src_ref[...], hid, (((1,), (1,)), ((), ())), preferred_element_type=F32)
    score = raw[0:8] + raw[8:16] + raw[16:24]
    for c in range(blocks):
        score_ref[0, c] = score[:, c * block : (c + 1) * block]


def transform(sources, first, index, relation_weight, src_vectors, block, values, scores):
    bounds = tuple(tuple((low, high) for _, low, high in pieces) for pieces in sources)
    arrays = [array for pieces in sources for array, _, _ in pieces]
    peers, cap = index.shape
    relations, width = relation_weight.shape[:2]
    anywhere = pl.BlockSpec(memory_space=pl.ANY)
    at = len(arrays) + 1 + 2
    kept = () if values is None else (values, scores)
    return pl.pallas_call(
        functools.partial(transform_kernel, bounds, first),
        grid_spec=pltpu.PrefetchScalarGridSpec(
            num_scalar_prefetch=1,
            grid=(len(sources),),
            in_specs=[anywhere] * len(arrays)
            + [
                pl.BlockSpec((relations, width, width), lambda p, *_: (0, 0, 0)),
                pl.BlockSpec(src_vectors.shape, lambda p, *_: (0, 0)),
            ]
            + [anywhere] * len(kept),
            out_specs=[
                pl.BlockSpec((1, cap, relations, block, width), lambda p, *_: (p + first, 0, 0, 0, 0)),
                pl.BlockSpec((1, cap, 8, block), lambda p, *_: (p + first, 0, 0, 0)),
            ],
            scratch_shapes=[pltpu.VMEM((2, cap * block, width), BF16), pltpu.SemaphoreType.DMA((2, cap))],
        ),
        out_shape=[
            jax.ShapeDtypeStruct((peers, cap, relations, block, width), BF16),
            jax.ShapeDtypeStruct((peers, cap, 8, block), F32),
        ],
        input_output_aliases={at + n: n for n in range(len(kept))},
        compiler_params=pltpu.CompilerParams(vmem_limit_bytes=48 * 1024 * 1024),
        name="transform",
    )(index, *arrays, relation_weight, src_vectors, *kept)


def attend_kernel(
    rel_ref, slot_ref, own_ref, mask_ref, val_ref, score_ref, tgt_ref, out_ref, tb_ref, log_ref, prob_ref, cats_ref, den_ref, sem
):
    b = pl.program_id(0)
    lists, rows, cols = mask_ref.shape[1:]
    chunk = 32

    def copy(block, slot, k):
        return pltpu.make_async_copy(
            val_ref.at[slot_ref[block, k], rel_ref[block, k]], cats_ref.at[slot, pl.ds(k * cols, cols)], sem.at[slot, k]
        )

    @pl.when(b == 0)
    def _():
        for k in range(lists):
            copy(0, 0, k).start()

    @pl.when(b + 1 < pl.num_programs(0))
    def _():
        for k in range(lists):
            copy(b + 1, lax.rem(b + 1, 2), k).start()

    half = lax.rem(b, 2)
    own = own_ref[...]
    target = jnp.dot(own, tgt_ref[0], preferred_element_type=F32)
    target += jnp.dot(own, tgt_ref[1], preferred_element_type=F32)
    target += jnp.dot(own, tgt_ref[2], preferred_element_type=F32)
    for r in range(tb_ref.shape[0]):
        for h in range(HEADS):
            c = r * HEADS + h
            tb_ref[r, h] = jnp.broadcast_to(target[:, c : c + 1], (rows, cols))
    rels = [rel_ref[b, k] for k in range(lists)]
    slots = [slot_ref[b, k] for k in range(lists)]
    for i in range(0, rows, chunk):
        here = slice(i, i + chunk)
        top = [jnp.full((chunk, cols), -jnp.inf, F32) for _ in range(HEADS)]
        for k in range(lists):
            used = mask_ref[0, k, here, :] > 0
            for h in range(HEADS):
                source = score_ref[slots[k], pl.ds(rels[k] * HEADS + h, 1), :]
                raw = tb_ref[rels[k], h, here, :] + source
                logit = jnp.where(used, jnp.maximum(raw, 0.2 * raw), -jnp.inf)
                log_ref[h, k, here, :] = logit
                top[h] = jnp.maximum(top[h], logit)
        for h in range(HEADS):
            highest = jnp.broadcast_to(jnp.max(top[h], axis=1, keepdims=True), (chunk, cols))
            total = jnp.zeros((chunk, cols), F32)
            for k in range(lists):
                prob = jnp.exp2(log_ref[h, k, here, :] - highest)
                total += prob
                prob_ref[h, here, k * cols : (k + 1) * cols] = prob.astype(BF16)
            den_ref[h, here, :] = jnp.broadcast_to(jnp.sum(total, axis=1, keepdims=True), (chunk, cols))
    for k in range(lists):
        copy(b, half, k).wait()
    for h in range(HEADS):
        lanes = slice(h * cols, (h + 1) * cols)
        summed = jnp.dot(prob_ref[h], cats_ref[half, :, lanes], preferred_element_type=F32)
        mixed = summed / den_ref[h] + own[:, lanes].astype(F32)
        out_ref[:, lanes] = jnp.where(mixed > 0, mixed, jnp.exp(jnp.minimum(mixed, 0.0)) - 1.0).astype(BF16)


def attend(hidden, edge_mask, relation_ids, source_slots, values, scores, tgt_vectors):
    blocks, lists, rows, cols = edge_mask.shape
    width = hidden.shape[1]
    slots, relations = values.shape[:2]
    return pl.pallas_call(
        attend_kernel,
        grid_spec=pltpu.PrefetchScalarGridSpec(
            num_scalar_prefetch=2,
            grid=(blocks,),
            in_specs=[
                pl.BlockSpec((rows, width), lambda b, *_: (b, 0)),
                pl.BlockSpec((1, lists, rows, cols), lambda b, *_: (b, 0, 0, 0)),
                pl.BlockSpec(memory_space=pl.ANY),
                pl.BlockSpec(scores.shape, lambda b, *_: (0, 0, 0)),
                pl.BlockSpec(tgt_vectors.shape, lambda b, *_: (0, 0, 0)),
            ],
            out_specs=pl.BlockSpec((rows, width), lambda b, *_: (b, 0)),
            scratch_shapes=[
                pltpu.VMEM((relations, HEADS, rows, cols), F32),
                pltpu.VMEM((HEADS, lists, rows, cols), F32),
                pltpu.VMEM((HEADS, rows, lists * cols), BF16),
                pltpu.VMEM((2, lists * cols, width), BF16),
                pltpu.VMEM((HEADS, rows, cols), F32),
                pltpu.SemaphoreType.DMA((2, lists)),
            ],
        ),
        out_shape=jax.ShapeDtypeStruct(hidden.shape, BF16),
        compiler_params=pltpu.CompilerParams(vmem_limit_bytes=56 * 1024 * 1024),
        name="attend",
    )(relation_ids, source_slots, hidden, edge_mask, values, scores, tgt_vectors)


def score_vectors(relation_weight, att_source, att_target):
    relations, width = att_source.shape
    head_width = width // HEADS
    split = att_source.reshape(relations, HEADS, head_width)
    moved = jnp.einsum(
        "rche,rhe->rhc",
        relation_weight.astype(F32).reshape(relations, width, HEADS, head_width),
        split,
        precision=lax.Precision.HIGHEST,
        preferred_element_type=F32,
    ).reshape(relations * HEADS, width)
    src = jnp.concatenate(three_parts(moved * LOG2E) + (jnp.zeros((8, width), BF16),), axis=0)
    own_head = (jnp.arange(width)[:, None] // head_width) == (jnp.arange(relations * HEADS)[None, :] % HEADS)
    spread = jnp.repeat(att_target.T, HEADS, axis=1)
    tgt = jnp.where(own_head, spread, 0.0) * LOG2E
    tgt = jnp.pad(tgt, ((0, 0), (0, 128 - relations * HEADS)))
    return src, jnp.stack(three_parts(tgt))


def shards(
    node_features,
    proj_weight,
    relation_weight,
    att_source,
    att_target,
    edge_mask,
    relation_ids,
    send_blocks,
    source_slots,
):
    block_rows = edge_mask.shape[-1]
    local_blocks = edge_mask.shape[0]
    rows_local = local_blocks * block_rows
    depth, width = proj_weight.shape
    n_feat = lax.axis_size("feat")
    n_graph = lax.axis_size("graph")
    levels = n_graph // 2
    place = lax.axis_index("graph")
    core, level = lax.rem(place, 2), place // 2

    def send(x, up, cores=0):
        pairs = [(p, (p + 2 * up) % n_graph ^ cores) for p in range(n_graph)]
        return lax.ppermute(x, "graph", pairs)

    cut = local_blocks // 2
    rows_a, half = cut * block_rows, width // 2
    features = node_features.T
    got = lax.all_to_all(
        arrange(features, proj_weight, core, n_feat, 0, rows_a, half), "feat", 0, 0, tiled=True
    ).reshape(n_feat * depth, rows_a + half)
    outgoing = arrange(features, proj_weight, core, n_feat, rows_a, rows_local, 0)
    got, outgoing = lax.optimization_barrier((got, outgoing))
    later = lax.all_to_all(outgoing, "feat", 0, 0, tiled=True).reshape(n_feat * depth, rows_local - rows_a)

    tables = jnp.stack([send_blocks[0]] + [send(send_blocks[0], d) for d in range(1, levels)])
    tables = jnp.stack([tables, send(tables, 0, 1)], axis=1)
    order = jnp.array([0, 1, 3, 2])
    index = tables[order, :, place].reshape(n_graph, CAP)
    peer = source_slots // CAP
    distance = (level - peer // 2 + levels) % levels
    slots = (2 * (distance ^ (distance >> 1)) + (peer % 2 ^ core)) * CAP + source_slots % CAP
    src_vectors, tgt_vectors = score_vectors(relation_weight, att_source, att_target)

    got, src_vectors, tgt_vectors, index, slots = lax.optimization_barrier(
        (got, src_vectors, tgt_vectors, index, slots)
    )
    mine = got[:, rows_a:]
    other = send(mine, 0, 1)
    whole = jnp.where(core == 0, jnp.concatenate([mine, other], axis=1), jnp.concatenate([other, mine], axis=1))

    def project(x):
        return lax.dot_general(x, whole, (((0,), (0,)), ((), ())), preferred_element_type=F32).astype(BF16)

    def both(pieces):
        return [pieces, [(send(x, 0, 1), low, high) for x, low, high in pieces]]

    def spread(group, first, kept):
        return transform(group, first, index, relation_weight, src_vectors, block_rows, *kept)

    def ring(part):
        return send(part, 1), send(part, -1)

    def forward(up, down):
        middle = up.shape[0] // 2
        return send(up[:middle], 1), send(down[middle:], -1)

    a = project(got[:, :rows_a])
    up_a, down_a = ring(a)
    later, up_a, down_a = lax.optimization_barrier((later, up_a, down_a))
    far_a = forward(up_a, down_a)
    b = project(later)
    up_b, down_b = ring(b)
    done = spread(both([(a, 0, cut), (b, cut, local_blocks)]), 0, (None, None))
    up_b, down_b, done = lax.optimization_barrier((up_b, down_b, done))
    far_b = forward(up_b, down_b)
    done = spread(
        both([(up_a, 0, cut), (up_b, cut, local_blocks)]) + both([(down_a, 0, cut), (down_b, cut, local_blocks)]), 2, done
    )
    far_b, done = lax.optimization_barrier((far_b, done))
    quarter = cut // 2
    far = [(x, n * quarter, (n + 1) * quarter) for n, x in enumerate(far_a + far_b)]
    values, scores = spread(both(far), 6, done)
    hidden = jnp.concatenate([a, b])
    total = n_graph * CAP
    values = values.reshape((total,) + values.shape[2:])
    scores = scores.reshape((total,) + scores.shape[2:])
    return attend(hidden, edge_mask, relation_ids, slots, values, scores, tgt_vectors)


def solution(mesh):
    placed = (
        P("graph", "feat"),
        P("feat", None),
        P(),
        P(),
        P(),
        P(("graph", "feat"), None, None, None),
        P(("graph", "feat"), None),
        P(("graph", "feat"), None, None),
        P(("graph", "feat"), None),
    )
    return jax.shard_map(
        shards, mesh=mesh, in_specs=placed, out_specs=P(("graph", "feat"), None), check_vma=False
    )
```

```python
import functools

import jax
import jax.numpy as jnp
from jax import lax
from jax.experimental import pallas as pl
from jax.experimental.pallas import tpu as pltpu
from jax.sharding import PartitionSpec as P

HEADS = 4
CAP = 4
LOG2E = 1.4426950408889634
F32 = jnp.float32
BF16 = jnp.bfloat16


def arrange_kernel(low, high, core_ref, x_ref, w_ref, out_ref):
    peers, _, columns = out_ref.shape
    total = x_ref.shape[1] // peers
    rows = high - low
    for q in range(peers):
        out_ref[q, :, :rows] = x_ref[:, q * total + low : q * total + high]
        if columns > rows:
            out_ref[q, :, rows:] = w_ref[...]


def arrange(features, weight, core, peers, low, high, half):
    depth, columns = features.shape
    rows = columns // peers
    step = 4
    return pl.pallas_call(
        functools.partial(arrange_kernel, low, high),
        grid_spec=pltpu.PrefetchScalarGridSpec(
            num_scalar_prefetch=1,
            grid=(peers // step,),
            in_specs=[
                pl.BlockSpec((depth, step * rows), lambda i, core_ref: (0, i)),
                pl.BlockSpec((depth, weight.shape[1] // 2), lambda i, core_ref: (0, core_ref[0])),
            ],
            out_specs=pl.BlockSpec((step, depth, high - low + half), lambda i, core_ref: (i, 0, 0)),
        ),
        out_shape=jax.ShapeDtypeStruct((peers, depth, high - low + half), BF16),
        name="arrange",
    )(core.reshape(1), features, weight)


def three_parts(x):
    hi = lax.reduce_precision(x, 8, 7)
    rest = x - hi
    mid = lax.reduce_precision(rest, 8, 7)
    return hi.astype(BF16), mid.astype(BF16), (rest - mid).astype(BF16)


def transform_kernel(bounds, first, idx_ref, *refs):
    n_pieces = sum(len(p) for p in bounds)
    pieces = refs[:n_pieces]
    rw_ref, src_ref = refs[n_pieces : n_pieces + 2]
    val_ref, score_ref, hid_ref, sem = refs[-4:]
    relations, block = val_ref.shape[1:3]
    cap = sem.shape[1]

    def copy(piece, row, source, c):
        return pltpu.make_async_copy(
            piece.at[pl.ds(row, block)], hid_ref.at[source, pl.ds(c * block, block)], sem.at[source, c]
        )

    begin = 0
    for source in range(len(bounds)):
        for c in range(cap):
            wanted = idx_ref[first + source, c]
            for n, (low, high) in enumerate(bounds[source]):

                @pl.when((wanted >= low) & (wanted < high))
                def _():
                    copy(pieces[begin + n], pl.multiple_of((wanted - low) * block, block), source, c).start()

        begin += len(bounds[source])
    for source in range(len(bounds)):
        for c in range(cap):
            copy(pieces[0], 0, source, c).wait()
        hid = hid_ref[source]
        at = (first + source) * cap
        for r in range(relations):
            moved = jnp.dot(hid, rw_ref[r], preferred_element_type=F32).astype(BF16)
            for c in range(cap):
                val_ref[at + c, r] = moved[c * block : (c + 1) * block]
        raw = lax.dot_general(src_ref[...], hid, (((1,), (1,)), ((), ())), preferred_element_type=F32)
        score = raw[0:8] + raw[8:16] + raw[16:24]
        for c in range(cap):
            score_ref[at + c] = score[:, c * block : (c + 1) * block]

def transform(sources, first, index, relation_weight, src_vectors, block, values, scores):
    bounds = tuple(tuple((low, high) for _, low, high in pieces) for pieces in sources)
    arrays = [array for pieces in sources for array, _, _ in pieces]
    peers, cap = index.shape
    relations, width = relation_weight.shape[:2]
    anywhere, inside = pl.BlockSpec(memory_space=pl.ANY), pl.BlockSpec(memory_space=pltpu.VMEM)
    kept = () if values is None else (values, scores)
    at = 1 + len(arrays) + 2
    return pl.pallas_call(
        functools.partial(transform_kernel, bounds, first),
        in_specs=[pl.BlockSpec(memory_space=pltpu.SMEM)] + [anywhere] * len(arrays) + [inside] * (2 + len(kept)),
        out_specs=[inside, inside],
        scratch_shapes=[
            pltpu.VMEM((len(bounds), cap * block, width), BF16),
            pltpu.SemaphoreType.DMA((len(bounds), cap)),
        ],
        out_shape=[
            jax.ShapeDtypeStruct((peers * cap, relations, block, width), BF16),
            jax.ShapeDtypeStruct((peers * cap, 8, block), F32),
        ],
        input_output_aliases={at + n: n for n in range(len(kept))},
        compiler_params=pltpu.CompilerParams(vmem_limit_bytes=24 * 1024 * 1024),
        name="transform",
    )(index, *arrays, relation_weight, src_vectors, *kept)


def cap_kernel(mask_ref, cap_ref):
    cap_ref[...] = jnp.where(mask_ref[...] > 0, jnp.inf, 0.0).astype(BF16)


def caps(edge_mask):
    shape = edge_mask.shape
    spec = pl.BlockSpec((1,) + shape[1:], lambda b: (b, 0, 0, 0))
    return pl.pallas_call(
        cap_kernel,
        grid=shape[:1],
        in_specs=[spec],
        out_specs=spec,
        out_shape=jax.ShapeDtypeStruct(shape, BF16),
        name="caps",
    )(edge_mask)


def attend_kernel(
    rel_ref, slot_ref, own_ref, cap_ref, tgt_ref, val_ref, score_ref, out_ref, u_ref, w_ref, prob_ref
):
    blocks, lists, rows, cols = cap_ref.shape
    relations = u_ref.shape[1]
    ones = jnp.ones((lists * cols, cols), BF16)

    def body(b, carry):
        own = own_ref[b]
        target = jnp.dot(own, tgt_ref[0], preferred_element_type=F32)
        target += jnp.dot(own, tgt_ref[1], preferred_element_type=F32)
        target += jnp.dot(own, tgt_ref[2], preferred_element_type=F32)
        rels = [rel_ref[b, k] for k in range(lists)]
        slots = [slot_ref[b, k] for k in range(lists)]

        def spread(r, h):
            return jnp.broadcast_to(target[:, r * HEADS + h : r * HEADS + h + 1], (rows, cols))

        def finish(h):
            lanes = slice(h * cols, (h + 1) * cols)
            value = jnp.concatenate([val_ref[slots[k], rels[k], :, lanes] for k in range(lists)], axis=0)
            summed = jnp.dot(prob_ref[h], jnp.concatenate([value, ones], axis=1), preferred_element_type=F32)
            total = summed[:, cols:]
            mixed = summed[:, :cols] / total + own[:, lanes].astype(F32)
            out_ref[b, :, lanes] = jnp.where(mixed > 0, mixed, jnp.exp(jnp.minimum(mixed, 0.0)) - 1.0).astype(BF16)
            return total

        reach = [jnp.full((8, cols), -jnp.inf, F32) for _ in range(relations)]
        for k in range(lists):
            source = score_ref[slots[k]]
            for r in range(relations):
                reach[r] = jnp.maximum(reach[r], jnp.where(rels[k] == r, source, -jnp.inf))
        for h in range(HEADS):
            bound = jnp.full((rows, cols), -jnp.inf, F32)
            for r in range(relations):
                c = r * HEADS + h
                most = spread(r, h) + jnp.max(reach[r][c : c + 1, :], axis=1, keepdims=True)
                bound = jnp.maximum(bound, jnp.maximum(most, 0.2 * most))
            for r in range(relations):
                u_ref[h, r] = spread(r, h) - bound
                w_ref[h, r] = 0.2 * spread(r, h) - bound
        least = jnp.full((rows, cols), jnp.inf, F32)
        for h in range(HEADS):
            for k in range(lists):
                source = score_ref[slots[k], pl.ds(rels[k] * HEADS + h, 1), :]
                logit = jnp.maximum(u_ref[h, rels[k]] + source, w_ref[h, rels[k]] + 0.2 * source)
                prob = jnp.exp2(logit).astype(BF16)
                prob_ref[h, :, k * cols : (k + 1) * cols] = jnp.minimum(prob, cap_ref[b, k])
        for h in range(HEADS):
            least = jnp.minimum(least, finish(h))

        @pl.when(jnp.logical_not(jnp.min(least) > 2.0**-90))
        def _():
            for h in range(HEADS):
                for r in range(relations):
                    u_ref[h, r] = spread(r, h)

                def raw(k):
                    r, slot = rel_ref[b, k], slot_ref[b, k]
                    x = u_ref[h, r] + score_ref[slot, pl.ds(r * HEADS + h, 1), :]
                    return jnp.where(cap_ref[b, k].astype(F32) > 0, jnp.maximum(x, 0.2 * x), -jnp.inf)

                w_ref[h, 0] = jnp.full((rows, cols), -jnp.inf, F32)

                def climb(k, carry):
                    w_ref[h, 0] = jnp.maximum(w_ref[h, 0], raw(k))
                    return carry

                lax.fori_loop(0, lists, climb, 0)
                w_ref[h, 0] = jnp.broadcast_to(jnp.max(w_ref[h, 0], axis=1, keepdims=True), (rows, cols))

                def weigh(k, carry):
                    at = pl.ds(pl.multiple_of(k * cols, cols), cols)
                    prob_ref[h, :, at] = jnp.exp2(raw(k) - w_ref[h, 0]).astype(BF16)
                    return carry

                lax.fori_loop(0, lists, weigh, 0)
                finish(h)

        return carry

    lax.fori_loop(0, blocks, body, 0)


def attend(hidden, cap, relation_ids, source_slots, values, scores, tgt_vectors):
    blocks, lists, rows, cols = cap.shape
    width = hidden.shape[1]
    relations = values.shape[1]
    scalars, inside = pl.BlockSpec(memory_space=pltpu.SMEM), pl.BlockSpec(memory_space=pltpu.VMEM)
    return pl.pallas_call(
        attend_kernel,
        in_specs=[scalars] * 2 + [inside] * 5,
        out_specs=inside,
        scratch_shapes=[
            pltpu.VMEM((HEADS, relations, rows, cols), F32),
            pltpu.VMEM((HEADS, relations, rows, cols), F32),
            pltpu.VMEM((HEADS, rows, lists * cols), BF16),
        ],
        out_shape=jax.ShapeDtypeStruct((blocks, rows, width), BF16),
        compiler_params=pltpu.CompilerParams(vmem_limit_bytes=24 * 1024 * 1024),
        name="attend",
    )(relation_ids, source_slots, hidden.reshape(blocks, rows, width), cap, tgt_vectors, values, scores).reshape(
        blocks * rows, width
    )


def score_vectors(relation_weight, att_source, att_target):
    relations, width = att_source.shape
    head_width = width // HEADS
    split = att_source.reshape(relations, HEADS, head_width)
    moved = jnp.einsum(
        "rche,rhe->rhc",
        relation_weight.astype(F32).reshape(relations, width, HEADS, head_width),
        split,
        precision=lax.Precision.HIGHEST,
        preferred_element_type=F32,
    ).reshape(relations * HEADS, width)
    src = jnp.concatenate(three_parts(moved * LOG2E) + (jnp.zeros((8, width), BF16),), axis=0)
    own_head = (jnp.arange(width)[:, None] // head_width) == (jnp.arange(relations * HEADS)[None, :] % HEADS)
    spread = jnp.repeat(att_target.T, HEADS, axis=1)
    tgt = jnp.where(own_head, spread, 0.0) * LOG2E
    tgt = jnp.pad(tgt, ((0, 0), (0, 128 - relations * HEADS)))
    return src, jnp.stack(three_parts(tgt))


def shards(
    node_features,
    proj_weight,
    relation_weight,
    att_source,
    att_target,
    edge_mask,
    relation_ids,
    send_blocks,
    source_slots,
):
    block_rows = edge_mask.shape[-1]
    local_blocks = edge_mask.shape[0]
    rows_local = local_blocks * block_rows
    depth, width = proj_weight.shape
    n_feat = lax.axis_size("feat")
    n_graph = lax.axis_size("graph")
    levels = n_graph // 2
    place = lax.axis_index("graph")
    core, level = lax.rem(place, 2), place // 2

    def send(x, up, cores=0):
        pairs = [(p, (p + 2 * up) % n_graph ^ cores) for p in range(n_graph)]
        return lax.ppermute(x, "graph", pairs)

    cut = local_blocks // 2
    rows_a, half = cut * block_rows, width // 2
    features = node_features.T
    got = lax.all_to_all(
        arrange(features, proj_weight, core, n_feat, 0, rows_a, half), "feat", 0, 0, tiled=True
    ).reshape(n_feat * depth, rows_a + half)
    outgoing = arrange(features, proj_weight, core, n_feat, rows_a, rows_local, 0)
    got, outgoing, send_blocks, cap = lax.optimization_barrier((got, outgoing, send_blocks, caps(edge_mask)))
    later = lax.all_to_all(outgoing, "feat", 0, 0, tiled=True).reshape(n_feat * depth, rows_local - rows_a)

    tables = jnp.stack([send_blocks[0]] + [send(send_blocks[0], d) for d in range(1, levels)])
    tables = jnp.stack([tables, send(tables, 0, 1)], axis=1)
    order = jnp.array([0, 1, 3, 2])
    index = tables[order, :, place].reshape(n_graph, CAP)
    peer = source_slots // CAP
    distance = (level - peer // 2 + levels) % levels
    slots = (2 * (distance ^ (distance >> 1)) + (peer % 2 ^ core)) * CAP + source_slots % CAP
    src_vectors, tgt_vectors = score_vectors(relation_weight, att_source, att_target)

    later, src_vectors, tgt_vectors, slots = lax.optimization_barrier((later, src_vectors, tgt_vectors, slots))
    mine = got[:, rows_a:]
    other = send(mine, 0, 1)
    whole = jnp.where(core == 0, jnp.concatenate([mine, other], axis=1), jnp.concatenate([other, mine], axis=1))

    def project(x):
        return lax.dot_general(x, whole, (((0,), (0,)), ((), ())), preferred_element_type=F32).astype(BF16)

    def both(pieces):
        return [pieces, [(send(x, 0, 1), low, high) for x, low, high in pieces]]

    def spread(group, first, kept):
        return transform(group, first, index, relation_weight, src_vectors, block_rows, *kept)

    def ring(part):
        return send(part, 1), send(part, -1)

    def forward(up, down):
        middle = up.shape[0] // 2
        return send(up[:middle], 1), send(down[middle:], -1)

    a = project(got[:, :rows_a])
    up_a, down_a = ring(a)
    far_a = forward(up_a, down_a)
    later, far_a = lax.optimization_barrier((later, far_a))
    b = project(later)
    up_b, down_b = ring(b)
    done = spread(both([(a, 0, cut), (b, cut, local_blocks)]), 0, (None, None))
    up_b, down_b, done = lax.optimization_barrier((up_b, down_b, done))
    far_b = forward(up_b, down_b)
    done = spread(
        both([(up_a, 0, cut), (up_b, cut, local_blocks)]) + both([(down_a, 0, cut), (down_b, cut, local_blocks)]), 2, done
    )
    far_b, done = lax.optimization_barrier((far_b, done))
    quarter = cut // 2
    far = [(x, n * quarter, (n + 1) * quarter) for n, x in enumerate(far_a + far_b)]
    values, scores = spread(both(far), 6, done)
    return attend(jnp.concatenate([a, b]), cap, relation_ids, slots, values, scores, tgt_vectors)


def solution(mesh):
    placed = (
        P("graph", "feat"),
        P("feat", None),
        P(),
        P(),
        P(),
        P(("graph", "feat"), None, None, None),
        P(("graph", "feat"), None),
        P(("graph", "feat"), None, None),
        P(("graph", "feat"), None),
    )
    return jax.shard_map(
        shards, mesh=mesh, in_specs=placed, out_specs=P(("graph", "feat"), None), check_vma=False
    )
```

```python
import functools

import jax
import jax.numpy as jnp
from jax import lax
from jax.experimental import pallas as pl
from jax.experimental.pallas import tpu as pltpu
from jax.sharding import PartitionSpec as P

HEADS = 4
CAP = 4
LOG2E = 1.4426950408889634
F32 = jnp.float32
BF16 = jnp.bfloat16


def arrange_kernel(low, high, core_ref, x_ref, w_ref, out_ref):
    peers, _, columns = out_ref.shape
    total = x_ref.shape[1] // peers
    rows = high - low
    for q in range(peers):
        out_ref[q, :, :rows] = x_ref[:, q * total + low : q * total + high]
        if columns > rows:
            out_ref[q, :, rows:] = w_ref[...]


def arrange(features, weight, core, peers, low, high, half):
    depth, columns = features.shape
    rows = columns // peers
    step = 4
    return pl.pallas_call(
        functools.partial(arrange_kernel, low, high),
        grid_spec=pltpu.PrefetchScalarGridSpec(
            num_scalar_prefetch=1,
            grid=(peers // step,),
            in_specs=[
                pl.BlockSpec((depth, step * rows), lambda i, core_ref: (0, i)),
                pl.BlockSpec((depth, weight.shape[1] // 2), lambda i, core_ref: (0, core_ref[0])),
            ],
            out_specs=pl.BlockSpec((step, depth, high - low + half), lambda i, core_ref: (i, 0, 0)),
        ),
        out_shape=jax.ShapeDtypeStruct((peers, depth, high - low + half), BF16),
        name="arrange",
    )(core.reshape(1), features, weight)


def three_parts(x):
    hi = lax.reduce_precision(x, 8, 7)
    rest = x - hi
    mid = lax.reduce_precision(rest, 8, 7)
    return hi.astype(BF16), mid.astype(BF16), (rest - mid).astype(BF16)


def transform_kernel(bounds, first, idx_ref, *refs):
    n_pieces = sum(len(p) for p in bounds)
    pieces = refs[:n_pieces]
    rw_ref, src_ref = refs[n_pieces : n_pieces + 2]
    val_ref, score_ref, hid_ref, sem = refs[-4:]
    relations, block = val_ref.shape[1:3]
    cap = sem.shape[1]

    def copy(piece, row, source, c):
        return pltpu.make_async_copy(
            piece.at[pl.ds(row, block)], hid_ref.at[source, pl.ds(c * block, block)], sem.at[source, c]
        )

    begin = 0
    for source in range(len(bounds)):
        for c in range(cap):
            wanted = idx_ref[first + source, c]
            for n, (low, high) in enumerate(bounds[source]):

                @pl.when((wanted >= low) & (wanted < high))
                def _():
                    copy(pieces[begin + n], pl.multiple_of((wanted - low) * block, block), source, c).start()

        begin += len(bounds[source])
    for source in range(len(bounds)):
        for c in range(cap):
            copy(pieces[0], 0, source, c).wait()
        hid = hid_ref[source]
        at = (first + source) * cap
        for r in range(relations):
            moved = jnp.dot(hid, rw_ref[r], preferred_element_type=F32).astype(BF16)
            for c in range(cap):
                val_ref[at + c, r] = moved[c * block : (c + 1) * block]
        raw = lax.dot_general(src_ref[...], hid, (((1,), (1,)), ((), ())), preferred_element_type=F32)
        score = raw[0:8] + raw[8:16] + raw[16:24]
        for c in range(cap):
            score_ref[at + c] = score[:, c * block : (c + 1) * block]

def transform(sources, first, index, relation_weight, src_vectors, block, values, scores):
    bounds = tuple(tuple((low, high) for _, low, high in pieces) for pieces in sources)
    arrays = [array for pieces in sources for array, _, _ in pieces]
    peers, cap = index.shape
    relations, width = relation_weight.shape[:2]
    anywhere, inside = pl.BlockSpec(memory_space=pl.ANY), pl.BlockSpec(memory_space=pltpu.VMEM)
    kept = () if values is None else (values, scores)
    at = 1 + len(arrays) + 2
    return pl.pallas_call(
        functools.partial(transform_kernel, bounds, first),
        in_specs=[pl.BlockSpec(memory_space=pltpu.SMEM)] + [anywhere] * len(arrays) + [inside] * (2 + len(kept)),
        out_specs=[inside, inside],
        scratch_shapes=[
            pltpu.VMEM((len(bounds), cap * block, width), BF16),
            pltpu.SemaphoreType.DMA((len(bounds), cap)),
        ],
        out_shape=[
            jax.ShapeDtypeStruct((peers * cap, relations, block, width), BF16),
            jax.ShapeDtypeStruct((peers * cap, 8, block), F32),
        ],
        input_output_aliases={at + n: n for n in range(len(kept))},
        compiler_params=pltpu.CompilerParams(vmem_limit_bytes=24 * 1024 * 1024),
        name="transform",
    )(index, *arrays, relation_weight, src_vectors, *kept)


def cap_kernel(mask_ref, cap_ref):
    cap_ref[...] = jnp.where(mask_ref[...] > 0, jnp.inf, 0.0).astype(BF16)


def caps(edge_mask):
    shape = edge_mask.shape
    spec = pl.BlockSpec((1,) + shape[1:], lambda b: (b, 0, 0, 0))
    return pl.pallas_call(
        cap_kernel,
        grid=shape[:1],
        in_specs=[spec],
        out_specs=spec,
        out_shape=jax.ShapeDtypeStruct(shape, BF16),
        name="caps",
    )(edge_mask)


def attend_kernel(
    rel_ref, slot_ref, own_ref, cap_ref, tgt_ref, val_ref, score_ref, out_ref, u_ref, w_ref, prob_ref
):
    blocks, lists, rows, cols = cap_ref.shape
    relations = u_ref.shape[1]
    ones = jnp.ones((lists * cols, cols), BF16)

    def body(b, carry):
        own = own_ref[b]
        target = jnp.dot(own, tgt_ref[0], preferred_element_type=F32)
        target += jnp.dot(own, tgt_ref[1], preferred_element_type=F32)
        target += jnp.dot(own, tgt_ref[2], preferred_element_type=F32)
        rels = [rel_ref[b, k] for k in range(lists)]
        slots = [slot_ref[b, k] for k in range(lists)]

        def spread(r, h):
            return jnp.broadcast_to(target[:, r * HEADS + h : r * HEADS + h + 1], (rows, cols))

        def finish(h):
            lanes = slice(h * cols, (h + 1) * cols)
            value = jnp.concatenate([val_ref[slots[k], rels[k], :, lanes] for k in range(lists)], axis=0)
            summed = jnp.dot(prob_ref[h], jnp.concatenate([value, ones], axis=1), preferred_element_type=F32)
            total = summed[:, cols:]
            mixed = summed[:, :cols] / total + own[:, lanes].astype(F32)
            out_ref[b, :, lanes] = jnp.where(mixed > 0, mixed, jnp.exp(jnp.minimum(mixed, 0.0)) - 1.0).astype(BF16)
            return total

        reach = [jnp.full((8, cols), -jnp.inf, F32) for _ in range(relations)]
        for k in range(lists):
            source = score_ref[slots[k]]
            for r in range(relations):
                reach[r] = jnp.maximum(reach[r], jnp.where(rels[k] == r, source, -jnp.inf))
        for h in range(HEADS):
            bound = jnp.full((rows, cols), -jnp.inf, F32)
            for r in range(relations):
                c = r * HEADS + h
                most = spread(r, h) + jnp.max(reach[r][c : c + 1, :], axis=1, keepdims=True)
                bound = jnp.maximum(bound, jnp.maximum(most, 0.2 * most))
            for r in range(relations):
                u_ref[h, r] = spread(r, h) - bound
                w_ref[h, r] = 0.2 * spread(r, h) - bound
        least = jnp.full((rows, cols), jnp.inf, F32)
        for h in range(HEADS):
            for k in range(lists):
                source = score_ref[slots[k], pl.ds(rels[k] * HEADS + h, 1), :]
                logit = jnp.maximum(u_ref[h, rels[k]] + source, w_ref[h, rels[k]] + 0.2 * source)
                prob = jnp.exp2(logit).astype(BF16)
                prob_ref[h, :, k * cols : (k + 1) * cols] = jnp.minimum(prob, cap_ref[b, k])
        for h in range(HEADS):
            least = jnp.minimum(least, finish(h))

        @pl.when(jnp.logical_not(jnp.min(least) > 2.0**-90))
        def _():
            for h in range(HEADS):
                for r in range(relations):
                    u_ref[h, r] = spread(r, h)

                def raw(k):
                    r, slot = rel_ref[b, k], slot_ref[b, k]
                    x = u_ref[h, r] + score_ref[slot, pl.ds(r * HEADS + h, 1), :]
                    return jnp.where(cap_ref[b, k].astype(F32) > 0, jnp.maximum(x, 0.2 * x), -jnp.inf)

                w_ref[h, 0] = jnp.full((rows, cols), -jnp.inf, F32)

                def climb(k, carry):
                    w_ref[h, 0] = jnp.maximum(w_ref[h, 0], raw(k))
                    return carry

                lax.fori_loop(0, lists, climb, 0)
                w_ref[h, 0] = jnp.broadcast_to(jnp.max(w_ref[h, 0], axis=1, keepdims=True), (rows, cols))

                def weigh(k, carry):
                    at = pl.ds(pl.multiple_of(k * cols, cols), cols)
                    prob_ref[h, :, at] = jnp.exp2(raw(k) - w_ref[h, 0]).astype(BF16)
                    return carry

                lax.fori_loop(0, lists, weigh, 0)
                finish(h)

        return carry

    lax.fori_loop(0, blocks, body, 0)


def attend(hidden, cap, relation_ids, source_slots, values, scores, tgt_vectors):
    blocks, lists, rows, cols = cap.shape
    width = hidden.shape[1]
    relations = values.shape[1]
    scalars, inside = pl.BlockSpec(memory_space=pltpu.SMEM), pl.BlockSpec(memory_space=pltpu.VMEM)
    return pl.pallas_call(
        attend_kernel,
        in_specs=[scalars] * 2 + [inside] * 5,
        out_specs=inside,
        scratch_shapes=[
            pltpu.VMEM((HEADS, relations, rows, cols), F32),
            pltpu.VMEM((HEADS, relations, rows, cols), F32),
            pltpu.VMEM((HEADS, rows, lists * cols), BF16),
        ],
        out_shape=jax.ShapeDtypeStruct((blocks, rows, width), BF16),
        compiler_params=pltpu.CompilerParams(vmem_limit_bytes=24 * 1024 * 1024),
        name="attend",
    )(relation_ids, source_slots, hidden.reshape(blocks, rows, width), cap, tgt_vectors, values, scores).reshape(
        blocks * rows, width
    )


def score_vectors(relation_weight, att_source, att_target):
    relations, width = att_source.shape
    head_width = width // HEADS
    split = att_source.reshape(relations, HEADS, head_width)
    moved = jnp.einsum(
        "rche,rhe->rhc",
        relation_weight.astype(F32).reshape(relations, width, HEADS, head_width),
        split,
        precision=lax.Precision.HIGHEST,
        preferred_element_type=F32,
    ).reshape(relations * HEADS, width)
    src = jnp.concatenate(three_parts(moved * LOG2E) + (jnp.zeros((8, width), BF16),), axis=0)
    own_head = (jnp.arange(width)[:, None] // head_width) == (jnp.arange(relations * HEADS)[None, :] % HEADS)
    spread = jnp.repeat(att_target.T, HEADS, axis=1)
    tgt = jnp.where(own_head, spread, 0.0) * LOG2E
    tgt = jnp.pad(tgt, ((0, 0), (0, 128 - relations * HEADS)))
    return src, jnp.stack(three_parts(tgt))


def shards(
    node_features,
    proj_weight,
    relation_weight,
    att_source,
    att_target,
    edge_mask,
    relation_ids,
    send_blocks,
    source_slots,
):
    block_rows = edge_mask.shape[-1]
    local_blocks = edge_mask.shape[0]
    rows_local = local_blocks * block_rows
    depth, width = proj_weight.shape
    n_feat = lax.axis_size("feat")
    n_graph = lax.axis_size("graph")
    levels = n_graph // 2
    place = lax.axis_index("graph")
    core, level = lax.rem(place, 2), place // 2

    def send(x, up, cores=0):
        pairs = [(p, (p + 2 * up) % n_graph ^ cores) for p in range(n_graph)]
        return lax.ppermute(x, "graph", pairs)

    half = width // 2
    features = node_features.T
    outgoing = arrange(features, proj_weight, core, n_feat, 0, rows_local, half)
    outgoing, send_blocks = lax.optimization_barrier((outgoing, send_blocks))
    got = lax.all_to_all(outgoing, "feat", 0, 0, tiled=True).reshape(n_feat * depth, rows_local + half)

    tables = jnp.stack([send_blocks[0]] + [send(send_blocks[0], d) for d in range(1, levels)])
    tables = jnp.stack([tables, send(tables, 0, 1)], axis=1)
    order = jnp.array([0, 1, 3, 2])
    index = tables[order, :, place].reshape(n_graph, CAP)
    peer = source_slots // CAP
    distance = (level - peer // 2 + levels) % levels
    slots = (2 * (distance ^ (distance >> 1)) + (peer % 2 ^ core)) * CAP + source_slots % CAP
    src_vectors, tgt_vectors = score_vectors(relation_weight, att_source, att_target)

    cap = caps(edge_mask)
    got, cap, src_vectors, tgt_vectors, slots, index = lax.optimization_barrier(
        (got, cap, src_vectors, tgt_vectors, slots, index)
    )

    mine = got[:, rows_local:]
    other = send(mine, 0, 1)
    whole = jnp.where(core == 0, jnp.concatenate([mine, other], axis=1), jnp.concatenate([other, mine], axis=1))
    hidden = lax.dot_general(
        got[:, :rows_local], whole, (((0,), (0,)), ((), ())), preferred_element_type=F32
    ).astype(BF16)

    def both(pieces):
        return [pieces, [(send(x, 0, 1), low, high) for x, low, high in pieces]]

    def spread(group, first, kept):
        return transform(group, first, index, relation_weight, src_vectors, block_rows, *kept)

    middle = local_blocks // 2
    split = middle * block_rows
    up, down = send(hidden, 1), send(hidden, -1)
    done = spread(both([(hidden, 0, local_blocks)]), 0, (None, None))
    up, down, done = lax.optimization_barrier((up, down, done))
    far_up, far_down = send(up[:split], 1), send(down[split:], -1)
    done = spread(both([(up, 0, local_blocks)]) + both([(down, 0, local_blocks)]), 2, done)
    far_up, far_down, done = lax.optimization_barrier((far_up, far_down, done))
    values, scores = spread(both([(far_up, 0, middle), (far_down, middle, local_blocks)]), 6, done)
    return attend(hidden, cap, relation_ids, slots, values, scores, tgt_vectors)


def solution(mesh):
    placed = (
        P("graph", "feat"),
        P("feat", None),
        P(),
        P(),
        P(),
        P(("graph", "feat"), None, None, None),
        P(("graph", "feat"), None),
        P(("graph", "feat"), None, None),
        P(("graph", "feat"), None),
    )
    return jax.shard_map(
        shards, mesh=mesh, in_specs=placed, out_specs=P(("graph", "feat"), None), check_vma=False
    )
```

```python
import functools

import jax
import jax.numpy as jnp
from jax import lax
from jax.experimental import pallas as pl
from jax.experimental.pallas import tpu as pltpu
from jax.sharding import PartitionSpec as P

HEADS = 4
CAP = 4
LOG2E = 1.4426950408889634
F32 = jnp.float32
BF16 = jnp.bfloat16


def arrange_kernel(low, high, core_ref, x_ref, w_ref, out_ref):
    peers, _, columns = out_ref.shape
    total = x_ref.shape[1] // peers
    rows = high - low
    for q in range(peers):
        out_ref[q, :, :rows] = x_ref[:, q * total + low : q * total + high]
        if columns > rows:
            out_ref[q, :, rows:] = w_ref[...]


def arrange(features, weight, core, peers, low, high, half):
    depth, columns = features.shape
    rows = columns // peers
    step = 4
    return pl.pallas_call(
        functools.partial(arrange_kernel, low, high),
        grid_spec=pltpu.PrefetchScalarGridSpec(
            num_scalar_prefetch=1,
            grid=(peers // step,),
            in_specs=[
                pl.BlockSpec((depth, step * rows), lambda i, core_ref: (0, i)),
                pl.BlockSpec((depth, weight.shape[1] // 2), lambda i, core_ref: (0, core_ref[0])),
            ],
            out_specs=pl.BlockSpec((step, depth, high - low + half), lambda i, core_ref: (i, 0, 0)),
        ),
        out_shape=jax.ShapeDtypeStruct((peers, depth, high - low + half), BF16),
        name="arrange",
    )(core.reshape(1), features, weight)


def three_parts(x):
    hi = lax.reduce_precision(x, 8, 7)
    rest = x - hi
    mid = lax.reduce_precision(rest, 8, 7)
    return hi.astype(BF16), mid.astype(BF16), (rest - mid).astype(BF16)


def transform_kernel(bounds, first, idx_ref, *refs):
    n_pieces = sum(len(p) for p in bounds)
    pieces = refs[:n_pieces]
    rw_ref, src_ref = refs[n_pieces : n_pieces + 2]
    val_ref, score_ref, hid_ref, sem = refs[-4:]
    relations, block = val_ref.shape[1:3]
    cap = sem.shape[1]

    def copy(piece, row, source, c):
        return pltpu.make_async_copy(
            piece.at[pl.ds(row, block)], hid_ref.at[source, pl.ds(c * block, block)], sem.at[source, c]
        )

    begin = 0
    for source in range(len(bounds)):
        for c in range(cap):
            wanted = idx_ref[first + source, c]
            for n, (low, high) in enumerate(bounds[source]):

                @pl.when((wanted >= low) & (wanted < high))
                def _():
                    copy(pieces[begin + n], pl.multiple_of((wanted - low) * block, block), source, c).start()

        begin += len(bounds[source])
    for source in range(len(bounds)):
        for c in range(cap):
            copy(pieces[0], 0, source, c).wait()
        hid = hid_ref[source]
        at = (first + source) * cap
        for r in range(relations):
            moved = jnp.dot(hid, rw_ref[r], preferred_element_type=F32).astype(BF16)
            for c in range(cap):
                val_ref[at + c, r] = moved[c * block : (c + 1) * block]
        raw = lax.dot_general(src_ref[...], hid, (((1,), (1,)), ((), ())), preferred_element_type=F32)
        score = raw[0:8] + raw[8:16] + raw[16:24]
        for c in range(cap):
            score_ref[at + c] = score[:, c * block : (c + 1) * block]

def transform(sources, first, index, relation_weight, src_vectors, block, values, scores):
    bounds = tuple(tuple((low, high) for _, low, high in pieces) for pieces in sources)
    arrays = [array for pieces in sources for array, _, _ in pieces]
    peers, cap = index.shape
    relations, width = relation_weight.shape[:2]
    anywhere, inside = pl.BlockSpec(memory_space=pl.ANY), pl.BlockSpec(memory_space=pltpu.VMEM)
    kept = () if values is None else (values, scores)
    at = 1 + len(arrays) + 2
    return pl.pallas_call(
        functools.partial(transform_kernel, bounds, first),
        in_specs=[pl.BlockSpec(memory_space=pltpu.SMEM)] + [anywhere] * len(arrays) + [inside] * (2 + len(kept)),
        out_specs=[inside, inside],
        scratch_shapes=[
            pltpu.VMEM((len(bounds), cap * block, width), BF16),
            pltpu.SemaphoreType.DMA((len(bounds), cap)),
        ],
        out_shape=[
            jax.ShapeDtypeStruct((peers * cap, relations, block, width), BF16),
            jax.ShapeDtypeStruct((peers * cap, 8, block), F32),
        ],
        input_output_aliases={at + n: n for n in range(len(kept))},
        compiler_params=pltpu.CompilerParams(vmem_limit_bytes=24 * 1024 * 1024),
        name="transform",
    )(index, *arrays, relation_weight, src_vectors, *kept)


def cap_kernel(mask_ref, cap_ref):
    cap_ref[...] = jnp.where(mask_ref[...] > 0, jnp.inf, 0.0).astype(BF16)


def caps(edge_mask):
    shape = edge_mask.shape
    spec = pl.BlockSpec((1,) + shape[1:], lambda b: (b, 0, 0, 0))
    return pl.pallas_call(
        cap_kernel,
        grid=shape[:1],
        in_specs=[spec],
        out_specs=spec,
        out_shape=jax.ShapeDtypeStruct(shape, BF16),
        name="caps",
    )(edge_mask)


def attend_kernel(
    rel_ref, slot_ref, own_ref, cap_ref, tgt_ref, val_ref, score_ref, out_ref, u_ref, w_ref, prob_ref
):
    blocks, lists, rows, cols = cap_ref.shape
    relations = u_ref.shape[1]
    ones = jnp.ones((lists * cols, cols), BF16)

    def body(b, carry):
        own = own_ref[b]
        target = jnp.dot(own, tgt_ref[0], preferred_element_type=F32)
        target += jnp.dot(own, tgt_ref[1], preferred_element_type=F32)
        target += jnp.dot(own, tgt_ref[2], preferred_element_type=F32)
        rels = [rel_ref[b, k] for k in range(lists)]
        slots = [slot_ref[b, k] for k in range(lists)]

        def spread(r, h):
            return jnp.broadcast_to(target[:, r * HEADS + h : r * HEADS + h + 1], (rows, cols))

        def finish(h):
            lanes = slice(h * cols, (h + 1) * cols)
            value = jnp.concatenate([val_ref[slots[k], rels[k], :, lanes] for k in range(lists)], axis=0)
            summed = jnp.dot(prob_ref[h], jnp.concatenate([value, ones], axis=1), preferred_element_type=F32)
            total = summed[:, cols:]
            mixed = summed[:, :cols] / total + own[:, lanes].astype(F32)
            out_ref[b, :, lanes] = jnp.where(mixed > 0, mixed, jnp.exp(jnp.minimum(mixed, 0.0)) - 1.0).astype(BF16)
            return total

        reach = [jnp.full((8, cols), -jnp.inf, F32) for _ in range(relations)]
        for k in range(lists):
            source = score_ref[slots[k]]
            for r in range(relations):
                reach[r] = jnp.maximum(reach[r], jnp.where(rels[k] == r, source, -jnp.inf))
        for h in range(HEADS):
            bound = jnp.full((rows, cols), -jnp.inf, F32)
            for r in range(relations):
                c = r * HEADS + h
                most = spread(r, h) + jnp.max(reach[r][c : c + 1, :], axis=1, keepdims=True)
                bound = jnp.maximum(bound, jnp.maximum(most, 0.2 * most))
            for r in range(relations):
                u_ref[h, r] = spread(r, h) - bound
                w_ref[h, r] = 0.2 * spread(r, h) - bound
        least = jnp.full((rows, cols), jnp.inf, F32)
        for h in range(HEADS):
            for k in range(lists):
                source = score_ref[slots[k], pl.ds(rels[k] * HEADS + h, 1), :]
                logit = jnp.maximum(u_ref[h, rels[k]] + source, w_ref[h, rels[k]] + 0.2 * source)
                prob = jnp.exp2(logit).astype(BF16)
                prob_ref[h, :, k * cols : (k + 1) * cols] = jnp.minimum(prob, cap_ref[b, k])
        for h in range(HEADS):
            least = jnp.minimum(least, finish(h))

        @pl.when(jnp.logical_not(jnp.min(least) > 2.0**-90))
        def _():
            for h in range(HEADS):
                for r in range(relations):
                    u_ref[h, r] = spread(r, h)

                def raw(k):
                    r, slot = rel_ref[b, k], slot_ref[b, k]
                    x = u_ref[h, r] + score_ref[slot, pl.ds(r * HEADS + h, 1), :]
                    return jnp.where(cap_ref[b, k].astype(F32) > 0, jnp.maximum(x, 0.2 * x), -jnp.inf)

                w_ref[h, 0] = jnp.full((rows, cols), -jnp.inf, F32)

                def climb(k, carry):
                    w_ref[h, 0] = jnp.maximum(w_ref[h, 0], raw(k))
                    return carry

                lax.fori_loop(0, lists, climb, 0)
                w_ref[h, 0] = jnp.broadcast_to(jnp.max(w_ref[h, 0], axis=1, keepdims=True), (rows, cols))

                def weigh(k, carry):
                    at = pl.ds(pl.multiple_of(k * cols, cols), cols)
                    prob_ref[h, :, at] = jnp.exp2(raw(k) - w_ref[h, 0]).astype(BF16)
                    return carry

                lax.fori_loop(0, lists, weigh, 0)
                finish(h)

        return carry

    lax.fori_loop(0, blocks, body, 0)


def attend(hidden, cap, relation_ids, source_slots, values, scores, tgt_vectors):
    blocks, lists, rows, cols = cap.shape
    width = hidden.shape[1]
    relations = values.shape[1]
    scalars, inside = pl.BlockSpec(memory_space=pltpu.SMEM), pl.BlockSpec(memory_space=pltpu.VMEM)
    return pl.pallas_call(
        attend_kernel,
        in_specs=[scalars] * 2 + [inside] * 5,
        out_specs=inside,
        scratch_shapes=[
            pltpu.VMEM((HEADS, relations, rows, cols), F32),
            pltpu.VMEM((HEADS, relations, rows, cols), F32),
            pltpu.VMEM((HEADS, rows, lists * cols), BF16),
        ],
        out_shape=jax.ShapeDtypeStruct((blocks, rows, width), BF16),
        compiler_params=pltpu.CompilerParams(vmem_limit_bytes=24 * 1024 * 1024),
        name="attend",
    )(relation_ids, source_slots, hidden.reshape(blocks, rows, width), cap, tgt_vectors, values, scores).reshape(
        blocks * rows, width
    )


def score_vectors(relation_weight, att_source, att_target):
    relations, width = att_source.shape
    head_width = width // HEADS
    split = att_source.reshape(relations, HEADS, head_width)
    moved = jnp.einsum(
        "rche,rhe->rhc",
        relation_weight.astype(F32).reshape(relations, width, HEADS, head_width),
        split,
        precision=lax.Precision.HIGHEST,
        preferred_element_type=F32,
    ).reshape(relations * HEADS, width)
    src = jnp.concatenate(three_parts(moved * LOG2E) + (jnp.zeros((8, width), BF16),), axis=0)
    own_head = (jnp.arange(width)[:, None] // head_width) == (jnp.arange(relations * HEADS)[None, :] % HEADS)
    spread = jnp.repeat(att_target.T, HEADS, axis=1)
    tgt = jnp.where(own_head, spread, 0.0) * LOG2E
    tgt = jnp.pad(tgt, ((0, 0), (0, 128 - relations * HEADS)))
    return src, jnp.stack(three_parts(tgt))


def shards(
    node_features,
    proj_weight,
    relation_weight,
    att_source,
    att_target,
    edge_mask,
    relation_ids,
    send_blocks,
    source_slots,
):
    block_rows = edge_mask.shape[-1]
    local_blocks = edge_mask.shape[0]
    rows_local = local_blocks * block_rows
    depth, width = proj_weight.shape
    n_feat = lax.axis_size("feat")
    n_graph = lax.axis_size("graph")
    levels = n_graph // 2
    place = lax.axis_index("graph")
    core, level = lax.rem(place, 2), place // 2

    def send(x, up, cores=0):
        pairs = [(p, (p + 2 * up) % n_graph ^ cores) for p in range(n_graph)]
        return lax.ppermute(x, "graph", pairs)

    half = width // 2
    features = node_features.T
    outgoing = arrange(features, proj_weight, core, n_feat, 0, rows_local, half)
    outgoing, send_blocks = lax.optimization_barrier((outgoing, send_blocks))
    got = lax.all_to_all(outgoing, "feat", 0, 0, tiled=True).reshape(n_feat * depth, rows_local + half)

    tables = jnp.stack([send_blocks[0]] + [send(send_blocks[0], d) for d in range(1, levels)])
    tables = jnp.stack([tables, send(tables, 0, 1)], axis=1)
    order = jnp.array([0, 1, 3, 2])
    index = tables[order, :, place].reshape(n_graph, CAP)
    peer = source_slots // CAP
    distance = (level - peer // 2 + levels) % levels
    slots = (2 * (distance ^ (distance >> 1)) + (peer % 2 ^ core)) * CAP + source_slots % CAP
    src_vectors, tgt_vectors = score_vectors(relation_weight, att_source, att_target)

    cap = caps(edge_mask)
    got, cap, src_vectors, tgt_vectors, slots, index = lax.optimization_barrier(
        (got, cap, src_vectors, tgt_vectors, slots, index)
    )

    mine = got[:, rows_local:]
    other = send(mine, 0, 1)
    whole = jnp.where(core == 0, jnp.concatenate([mine, other], axis=1), jnp.concatenate([other, mine], axis=1))
    hidden = lax.dot_general(
        got[:, :rows_local], whole, (((0,), (0,)), ((), ())), preferred_element_type=F32
    ).astype(BF16)

    def both(pieces):
        return [pieces, [(send(x, 0, 1), low, high) for x, low, high in pieces]]

    def spread(group, first, kept):
        return transform(group, first, index, relation_weight, src_vectors, block_rows, *kept)

    middle = local_blocks // 2
    split = middle * block_rows
    front, back = hidden[:split], hidden[split:]
    up_front, down_back = send(front, 1), send(back, -1)
    up_back, down_front = send(back, 1), send(front, -1)
    done = spread(both([(hidden, 0, local_blocks)]), 0, (None, None))
    up_front, down_back, done = lax.optimization_barrier((up_front, down_back, done))
    far_front, far_back = send(up_front, 1), send(down_back, -1)
    near = both([(up_front, 0, middle), (up_back, middle, local_blocks)])
    near += both([(down_front, 0, middle), (down_back, middle, local_blocks)])
    done = spread(near, 2, done)
    far_front, far_back, done = lax.optimization_barrier((far_front, far_back, done))
    values, scores = spread(both([(far_front, 0, middle), (far_back, middle, local_blocks)]), 6, done)
    return attend(hidden, cap, relation_ids, slots, values, scores, tgt_vectors)


def solution(mesh):
    placed = (
        P("graph", "feat"),
        P("feat", None),
        P(),
        P(),
        P(),
        P(("graph", "feat"), None, None, None),
        P(("graph", "feat"), None),
        P(("graph", "feat"), None, None),
        P(("graph", "feat"), None),
    )
    return jax.shard_map(
        shards, mesh=mesh, in_specs=placed, out_specs=P(("graph", "feat"), None), check_vma=False
    )
```

```python
import functools

import jax
import jax.numpy as jnp
from jax import lax
from jax.experimental import pallas as pl
from jax.experimental.pallas import tpu as pltpu
from jax.sharding import PartitionSpec as P

HEADS = 4
CAP = 4
LOG2E = 1.4426950408889634
F32 = jnp.float32
BF16 = jnp.bfloat16


def arrange_kernel(low, high, core_ref, x_ref, w_ref, out_ref):
    peers, _, columns = out_ref.shape
    total = x_ref.shape[1] // peers
    rows = high - low
    for q in range(peers):
        out_ref[q, :, :rows] = x_ref[:, q * total + low : q * total + high]
        if columns > rows:
            out_ref[q, :, rows:] = w_ref[...]


def arrange(features, weight, core, peers, low, high, half):
    depth, columns = features.shape
    rows = columns // peers
    step = 4
    return pl.pallas_call(
        functools.partial(arrange_kernel, low, high),
        grid_spec=pltpu.PrefetchScalarGridSpec(
            num_scalar_prefetch=1,
            grid=(peers // step,),
            in_specs=[
                pl.BlockSpec((depth, step * rows), lambda i, core_ref: (0, i)),
                pl.BlockSpec((depth, weight.shape[1] // 2), lambda i, core_ref: (0, core_ref[0])),
            ],
            out_specs=pl.BlockSpec((step, depth, high - low + half), lambda i, core_ref: (i, 0, 0)),
        ),
        out_shape=jax.ShapeDtypeStruct((peers, depth, high - low + half), BF16),
        name="arrange",
    )(core.reshape(1), features, weight)


def three_parts(x):
    hi = lax.reduce_precision(x, 8, 7)
    rest = x - hi
    mid = lax.reduce_precision(rest, 8, 7)
    return hi.astype(BF16), mid.astype(BF16), (rest - mid).astype(BF16)


def transform_kernel(bounds, first, idx_ref, *refs):
    n_pieces = sum(len(p) for p in bounds)
    pieces = refs[:n_pieces]
    rw_ref, src_ref = refs[n_pieces : n_pieces + 2]
    val_ref, score_ref, hid_ref, sem = refs[-4:]
    relations, block = val_ref.shape[1:3]
    cap = sem.shape[1]

    def copy(piece, row, source, c):
        return pltpu.make_async_copy(
            piece.at[pl.ds(row, block)], hid_ref.at[source, pl.ds(c * block, block)], sem.at[source, c]
        )

    begin = 0
    for source in range(len(bounds)):
        for c in range(cap):
            wanted = idx_ref[first + source, c]
            for n, (low, high) in enumerate(bounds[source]):

                @pl.when((wanted >= low) & (wanted < high))
                def _():
                    copy(pieces[begin + n], pl.multiple_of((wanted - low) * block, block), source, c).start()

        begin += len(bounds[source])
    for source in range(len(bounds)):
        for c in range(cap):
            copy(pieces[0], 0, source, c).wait()
        hid = hid_ref[source]
        at = (first + source) * cap
        for r in range(relations):
            moved = jnp.dot(hid, rw_ref[r], preferred_element_type=F32).astype(BF16)
            for c in range(cap):
                val_ref[at + c, r] = moved[c * block : (c + 1) * block]
        raw = lax.dot_general(src_ref[...], hid, (((1,), (1,)), ((), ())), preferred_element_type=F32)
        score = raw[0:8] + raw[8:16] + raw[16:24]
        for c in range(cap):
            score_ref[at + c] = score[:, c * block : (c + 1) * block]

def transform(sources, first, index, relation_weight, src_vectors, block, values, scores):
    bounds = tuple(tuple((low, high) for _, low, high in pieces) for pieces in sources)
    arrays = [array for pieces in sources for array, _, _ in pieces]
    peers, cap = index.shape
    relations, width = relation_weight.shape[:2]
    anywhere, inside = pl.BlockSpec(memory_space=pl.ANY), pl.BlockSpec(memory_space=pltpu.VMEM)
    kept = () if values is None else (values, scores)
    at = 1 + len(arrays) + 2
    return pl.pallas_call(
        functools.partial(transform_kernel, bounds, first),
        in_specs=[pl.BlockSpec(memory_space=pltpu.SMEM)] + [anywhere] * len(arrays) + [inside] * (2 + len(kept)),
        out_specs=[inside, inside],
        scratch_shapes=[
            pltpu.VMEM((len(bounds), cap * block, width), BF16),
            pltpu.SemaphoreType.DMA((len(bounds), cap)),
        ],
        out_shape=[
            jax.ShapeDtypeStruct((peers * cap, relations, block, width), BF16),
            jax.ShapeDtypeStruct((peers * cap, 8, block), F32),
        ],
        input_output_aliases={at + n: n for n in range(len(kept))},
        compiler_params=pltpu.CompilerParams(vmem_limit_bytes=24 * 1024 * 1024),
        name="transform",
    )(index, *arrays, relation_weight, src_vectors, *kept)


def cap_kernel(mask_ref, cap_ref):
    cap_ref[...] = jnp.where(mask_ref[...] > 0, jnp.inf, 0.0).astype(BF16)


def caps(edge_mask):
    shape = edge_mask.shape
    spec = pl.BlockSpec((1,) + shape[1:], lambda b: (b, 0, 0, 0))
    return pl.pallas_call(
        cap_kernel,
        grid=shape[:1],
        in_specs=[spec],
        out_specs=spec,
        out_shape=jax.ShapeDtypeStruct(shape, BF16),
        name="caps",
    )(edge_mask)


def attend_kernel(
    rel_ref, slot_ref, own_ref, cap_ref, tgt_ref, val_ref, score_ref, out_ref, u_ref, w_ref, prob_ref
):
    blocks, lists, rows, cols = cap_ref.shape
    relations = u_ref.shape[1]
    ones = jnp.ones((lists * cols, cols), BF16)

    def body(b, carry):
        own = own_ref[b]
        target = jnp.dot(own, tgt_ref[0], preferred_element_type=F32)
        target += jnp.dot(own, tgt_ref[1], preferred_element_type=F32)
        target += jnp.dot(own, tgt_ref[2], preferred_element_type=F32)
        rels = [rel_ref[b, k] for k in range(lists)]
        slots = [slot_ref[b, k] for k in range(lists)]

        def spread(r, h):
            return jnp.broadcast_to(target[:, r * HEADS + h : r * HEADS + h + 1], (rows, cols))

        def finish(h):
            lanes = slice(h * cols, (h + 1) * cols)
            value = jnp.concatenate([val_ref[slots[k], rels[k], :, lanes] for k in range(lists)], axis=0)
            summed = jnp.dot(prob_ref[h], jnp.concatenate([value, ones], axis=1), preferred_element_type=F32)
            total = summed[:, cols:]
            mixed = summed[:, :cols] / total + own[:, lanes].astype(F32)
            out_ref[b, :, lanes] = jnp.where(mixed > 0, mixed, jnp.exp(jnp.minimum(mixed, 0.0)) - 1.0).astype(BF16)
            return total

        reach = [jnp.full((8, cols), -jnp.inf, F32) for _ in range(relations)]
        for k in range(lists):
            source = score_ref[slots[k]]
            for r in range(relations):
                reach[r] = jnp.maximum(reach[r], jnp.where(rels[k] == r, source, -jnp.inf))
        for h in range(HEADS):
            bound = jnp.full((rows, cols), -jnp.inf, F32)
            for r in range(relations):
                c = r * HEADS + h
                most = spread(r, h) + jnp.max(reach[r][c : c + 1, :], axis=1, keepdims=True)
                bound = jnp.maximum(bound, jnp.maximum(most, 0.2 * most))
            for r in range(relations):
                u_ref[h, r] = spread(r, h) - bound
                w_ref[h, r] = 0.2 * spread(r, h) - bound
        least = jnp.full((rows, cols), jnp.inf, F32)
        for h in range(HEADS):
            for k in range(lists):
                source = score_ref[slots[k], pl.ds(rels[k] * HEADS + h, 1), :]
                logit = jnp.maximum(u_ref[h, rels[k]] + source, w_ref[h, rels[k]] + 0.2 * source)
                prob = jnp.exp2(logit).astype(BF16)
                prob_ref[h, :, k * cols : (k + 1) * cols] = jnp.minimum(prob, cap_ref[b, k])
        for h in range(HEADS):
            least = jnp.minimum(least, finish(h))

        @pl.when(jnp.logical_not(jnp.min(least) > 2.0**-90))
        def _():
            for h in range(HEADS):
                for r in range(relations):
                    u_ref[h, r] = spread(r, h)

                def raw(k):
                    r, slot = rel_ref[b, k], slot_ref[b, k]
                    x = u_ref[h, r] + score_ref[slot, pl.ds(r * HEADS + h, 1), :]
                    return jnp.where(cap_ref[b, k].astype(F32) > 0, jnp.maximum(x, 0.2 * x), -jnp.inf)

                w_ref[h, 0] = jnp.full((rows, cols), -jnp.inf, F32)

                def climb(k, carry):
                    w_ref[h, 0] = jnp.maximum(w_ref[h, 0], raw(k))
                    return carry

                lax.fori_loop(0, lists, climb, 0)
                w_ref[h, 0] = jnp.broadcast_to(jnp.max(w_ref[h, 0], axis=1, keepdims=True), (rows, cols))

                def weigh(k, carry):
                    at = pl.ds(pl.multiple_of(k * cols, cols), cols)
                    prob_ref[h, :, at] = jnp.exp2(raw(k) - w_ref[h, 0]).astype(BF16)
                    return carry

                lax.fori_loop(0, lists, weigh, 0)
                finish(h)

        return carry

    lax.fori_loop(0, blocks, body, 0)


def attend(hidden, cap, relation_ids, source_slots, values, scores, tgt_vectors):
    blocks, lists, rows, cols = cap.shape
    width = hidden.shape[1]
    relations = values.shape[1]
    scalars, inside = pl.BlockSpec(memory_space=pltpu.SMEM), pl.BlockSpec(memory_space=pltpu.VMEM)
    return pl.pallas_call(
        attend_kernel,
        in_specs=[scalars] * 2 + [inside] * 5,
        out_specs=inside,
        scratch_shapes=[
            pltpu.VMEM((HEADS, relations, rows, cols), F32),
            pltpu.VMEM((HEADS, relations, rows, cols), F32),
            pltpu.VMEM((HEADS, rows, lists * cols), BF16),
        ],
        out_shape=jax.ShapeDtypeStruct((blocks, rows, width), BF16),
        compiler_params=pltpu.CompilerParams(vmem_limit_bytes=24 * 1024 * 1024),
        name="attend",
    )(relation_ids, source_slots, hidden.reshape(blocks, rows, width), cap, tgt_vectors, values, scores).reshape(
        blocks * rows, width
    )


def score_vectors(relation_weight, att_source, att_target):
    relations, width = att_source.shape
    head_width = width // HEADS
    split = att_source.reshape(relations, HEADS, head_width)
    moved = jnp.einsum(
        "rche,rhe->rhc",
        relation_weight.astype(F32).reshape(relations, width, HEADS, head_width),
        split,
        precision=lax.Precision.HIGHEST,
        preferred_element_type=F32,
    ).reshape(relations * HEADS, width)
    src = jnp.concatenate(three_parts(moved * LOG2E) + (jnp.zeros((8, width), BF16),), axis=0)
    own_head = (jnp.arange(width)[:, None] // head_width) == (jnp.arange(relations * HEADS)[None, :] % HEADS)
    spread = jnp.repeat(att_target.T, HEADS, axis=1)
    tgt = jnp.where(own_head, spread, 0.0) * LOG2E
    tgt = jnp.pad(tgt, ((0, 0), (0, 128 - relations * HEADS)))
    return src, jnp.stack(three_parts(tgt))


def shards(
    node_features,
    proj_weight,
    relation_weight,
    att_source,
    att_target,
    edge_mask,
    relation_ids,
    send_blocks,
    source_slots,
):
    block_rows = edge_mask.shape[-1]
    local_blocks = edge_mask.shape[0]
    rows_local = local_blocks * block_rows
    depth, width = proj_weight.shape
    n_feat = lax.axis_size("feat")
    n_graph = lax.axis_size("graph")
    levels = n_graph // 2
    place = lax.axis_index("graph")
    core, level = lax.rem(place, 2), place // 2

    def send(x, up, cores=0):
        pairs = [(p, (p + 2 * up) % n_graph ^ cores) for p in range(n_graph)]
        return lax.ppermute(x, "graph", pairs)

    cut = local_blocks // 2
    rows_a, half = cut * block_rows, width // 2
    features = node_features.T
    got = lax.all_to_all(
        arrange(features, proj_weight, core, n_feat, 0, rows_a, half), "feat", 0, 0, tiled=True
    ).reshape(n_feat * depth, rows_a + half)
    outgoing = arrange(features, proj_weight, core, n_feat, rows_a, rows_local, 0)
    outgoing, send_blocks = lax.optimization_barrier((outgoing, send_blocks))

    tables = jnp.stack([send_blocks[0]] + [send(send_blocks[0], d) for d in range(1, levels)])
    tables = jnp.stack([tables, send(tables, 0, 1)], axis=1)
    order = jnp.array([0, 1, 3, 2])
    index = tables[order, :, place].reshape(n_graph, CAP)
    peer = source_slots // CAP
    distance = (level - peer // 2 + levels) % levels
    slots = (2 * (distance ^ (distance >> 1)) + (peer % 2 ^ core)) * CAP + source_slots % CAP
    src_vectors, tgt_vectors = score_vectors(relation_weight, att_source, att_target)

    got, outgoing, cap, src_vectors, tgt_vectors, slots, index = lax.optimization_barrier(
        (got, outgoing, caps(edge_mask), src_vectors, tgt_vectors, slots, index)
    )
    later = lax.all_to_all(outgoing, "feat", 0, 0, tiled=True).reshape(n_feat * depth, rows_local - rows_a)

    mine = got[:, rows_a:]
    other = send(mine, 0, 1)
    whole = jnp.where(core == 0, jnp.concatenate([mine, other], axis=1), jnp.concatenate([other, mine], axis=1))

    def project(x):
        return lax.dot_general(x, whole, (((0,), (0,)), ((), ())), preferred_element_type=F32).astype(BF16)

    def both(pieces):
        return [pieces, [(send(x, 0, 1), low, high) for x, low, high in pieces]]

    def spread(group, first, kept):
        return transform(group, first, index, relation_weight, src_vectors, block_rows, *kept)

    def ring(part):
        return send(part, 1), send(part, -1)

    def forward(up, down):
        middle = up.shape[0] // 2
        return send(up[:middle], 1), send(down[middle:], -1)

    a = project(got[:, :rows_a])
    up_a, down_a = ring(a)
    later, up_a, down_a = lax.optimization_barrier((later, up_a, down_a))
    far_a = forward(up_a, down_a)
    b = project(later)
    up_b, down_b = ring(b)
    done = spread(both([(a, 0, cut), (b, cut, local_blocks)]), 0, (None, None))
    up_b, down_b, done = lax.optimization_barrier((up_b, down_b, done))
    far_b = forward(up_b, down_b)
    done = spread(
        both([(up_a, 0, cut), (up_b, cut, local_blocks)]) + both([(down_a, 0, cut), (down_b, cut, local_blocks)]), 2, done
    )
    far_b, done = lax.optimization_barrier((far_b, done))
    quarter = cut // 2
    far = [(x, n * quarter, (n + 1) * quarter) for n, x in enumerate(far_a + far_b)]
    values, scores = spread(both(far), 6, done)
    return attend(jnp.concatenate([a, b]), cap, relation_ids, slots, values, scores, tgt_vectors)


def solution(mesh):
    placed = (
        P("graph", "feat"),
        P("feat", None),
        P(),
        P(),
        P(),
        P(("graph", "feat"), None, None, None),
        P(("graph", "feat"), None),
        P(("graph", "feat"), None, None),
        P(("graph", "feat"), None),
    )
    return jax.shard_map(
        shards, mesh=mesh, in_specs=placed, out_specs=P(("graph", "feat"), None), check_vma=False
    )
```

```python
import functools

import jax
import jax.numpy as jnp
from jax import lax
from jax.experimental import pallas as pl
from jax.experimental.pallas import tpu as pltpu
from jax.sharding import PartitionSpec as P

HEADS = 4
CAP = 4
LOG2E = 1.4426950408889634
F32 = jnp.float32
BF16 = jnp.bfloat16


def arrange_kernel(low, high, core_ref, x_ref, w_ref, out_ref):
    peers, _, columns = out_ref.shape
    total = x_ref.shape[1] // peers
    rows = high - low
    for q in range(peers):
        out_ref[q, :, :rows] = x_ref[:, q * total + low : q * total + high]
        if columns > rows:
            out_ref[q, :, rows:] = w_ref[...]


def arrange(features, weight, core, peers, low, high, half):
    depth, columns = features.shape
    rows = columns // peers
    step = 4
    return pl.pallas_call(
        functools.partial(arrange_kernel, low, high),
        grid_spec=pltpu.PrefetchScalarGridSpec(
            num_scalar_prefetch=1,
            grid=(peers // step,),
            in_specs=[
                pl.BlockSpec((depth, step * rows), lambda i, core_ref: (0, i)),
                pl.BlockSpec((depth, weight.shape[1] // 2), lambda i, core_ref: (0, core_ref[0])),
            ],
            out_specs=pl.BlockSpec((step, depth, high - low + half), lambda i, core_ref: (i, 0, 0)),
        ),
        out_shape=jax.ShapeDtypeStruct((peers, depth, high - low + half), BF16),
        name="arrange",
    )(core.reshape(1), features, weight)


def three_parts(x):
    hi = lax.reduce_precision(x, 8, 7)
    rest = x - hi
    mid = lax.reduce_precision(rest, 8, 7)
    return hi.astype(BF16), mid.astype(BF16), (rest - mid).astype(BF16)


def transform_kernel(bounds, first, idx_ref, *refs):
    n_pieces = sum(len(p) for p in bounds)
    pieces = refs[:n_pieces]
    rw_ref, src_ref = refs[n_pieces : n_pieces + 2]
    val_ref, score_ref, hid_ref, sem = refs[-4:]
    relations, block = val_ref.shape[1:3]
    cap = sem.shape[1]

    def copy(piece, row, source, c):
        return pltpu.make_async_copy(
            piece.at[pl.ds(row, block)], hid_ref.at[source, pl.ds(c * block, block)], sem.at[source, c]
        )

    begin = 0
    for source in range(len(bounds)):
        for c in range(cap):
            wanted = idx_ref[first + source, c]
            for n, (low, high) in enumerate(bounds[source]):

                @pl.when((wanted >= low) & (wanted < high))
                def _():
                    copy(pieces[begin + n], pl.multiple_of((wanted - low) * block, block), source, c).start()

        begin += len(bounds[source])
    for source in range(len(bounds)):
        for c in range(cap):
            copy(pieces[0], 0, source, c).wait()
        hid = hid_ref[source]
        at = (first + source) * cap
        for r in range(relations):
            moved = jnp.dot(hid, rw_ref[r], preferred_element_type=F32).astype(BF16)
            for c in range(cap):
                val_ref[at + c, r] = moved[c * block : (c + 1) * block]
        raw = lax.dot_general(src_ref[...], hid, (((1,), (1,)), ((), ())), preferred_element_type=F32)
        score = raw[0:8] + raw[8:16] + raw[16:24]
        for c in range(cap):
            score_ref[at + c] = score[:, c * block : (c + 1) * block]

def transform(sources, first, index, relation_weight, src_vectors, block, values, scores):
    bounds = tuple(tuple((low, high) for _, low, high in pieces) for pieces in sources)
    arrays = [array for pieces in sources for array, _, _ in pieces]
    peers, cap = index.shape
    relations, width = relation_weight.shape[:2]
    anywhere, inside = pl.BlockSpec(memory_space=pl.ANY), pl.BlockSpec(memory_space=pltpu.VMEM)
    kept = () if values is None else (values, scores)
    at = 1 + len(arrays) + 2
    return pl.pallas_call(
        functools.partial(transform_kernel, bounds, first),
        in_specs=[pl.BlockSpec(memory_space=pltpu.SMEM)] + [anywhere] * len(arrays) + [inside] * (2 + len(kept)),
        out_specs=[inside, inside],
        scratch_shapes=[
            pltpu.VMEM((len(bounds), cap * block, width), BF16),
            pltpu.SemaphoreType.DMA((len(bounds), cap)),
        ],
        out_shape=[
            jax.ShapeDtypeStruct((peers * cap, relations, block, width), BF16),
            jax.ShapeDtypeStruct((peers * cap, 8, block), F32),
        ],
        input_output_aliases={at + n: n for n in range(len(kept))},
        compiler_params=pltpu.CompilerParams(vmem_limit_bytes=24 * 1024 * 1024),
        name="transform",
    )(index, *arrays, relation_weight, src_vectors, *kept)


def cap_kernel(mask_ref, cap_ref):
    cap_ref[...] = jnp.where(mask_ref[...] > 0, jnp.inf, 0.0).astype(BF16)


def caps(edge_mask):
    shape = edge_mask.shape
    spec = pl.BlockSpec((1,) + shape[1:], lambda b: (b, 0, 0, 0))
    return pl.pallas_call(
        cap_kernel,
        grid=shape[:1],
        in_specs=[spec],
        out_specs=spec,
        out_shape=jax.ShapeDtypeStruct(shape, BF16),
        name="caps",
    )(edge_mask)


def attend_kernel(
    rel_ref, slot_ref, own_ref, cap_ref, tgt_ref, val_ref, score_ref, out_ref, u_ref, w_ref, prob_ref
):
    blocks, lists, rows, cols = cap_ref.shape
    relations = u_ref.shape[1]
    ones = jnp.ones((lists * cols, cols), BF16)

    def body(b, carry):
        own = own_ref[b]
        target = jnp.dot(own, tgt_ref[0], preferred_element_type=F32)
        target += jnp.dot(own, tgt_ref[1], preferred_element_type=F32)
        target += jnp.dot(own, tgt_ref[2], preferred_element_type=F32)
        rels = [rel_ref[b, k] for k in range(lists)]
        slots = [slot_ref[b, k] for k in range(lists)]

        def spread(r, h):
            return jnp.broadcast_to(target[:, r * HEADS + h : r * HEADS + h + 1], (rows, cols))

        def finish(h):
            lanes = slice(h * cols, (h + 1) * cols)
            value = jnp.concatenate([val_ref[slots[k], rels[k], :, lanes] for k in range(lists)], axis=0)
            summed = jnp.dot(prob_ref[h], jnp.concatenate([value, ones], axis=1), preferred_element_type=F32)
            total = summed[:, cols:]
            mixed = summed[:, :cols] / total + own[:, lanes].astype(F32)
            out_ref[b, :, lanes] = jnp.where(mixed > 0, mixed, jnp.exp(jnp.minimum(mixed, 0.0)) - 1.0).astype(BF16)
            return total

        reach = [jnp.full((8, cols), -jnp.inf, F32) for _ in range(relations)]
        for k in range(lists):
            source = score_ref[slots[k]]
            for r in range(relations):
                reach[r] = jnp.maximum(reach[r], jnp.where(rels[k] == r, source, -jnp.inf))
        for h in range(HEADS):
            bound = jnp.full((rows, cols), -jnp.inf, F32)
            for r in range(relations):
                c = r * HEADS + h
                most = spread(r, h) + jnp.max(reach[r][c : c + 1, :], axis=1, keepdims=True)
                bound = jnp.maximum(bound, jnp.maximum(most, 0.2 * most))
            for r in range(relations):
                u_ref[h, r] = spread(r, h) - bound
                w_ref[h, r] = 0.2 * spread(r, h) - bound
        least = jnp.full((rows, cols), jnp.inf, F32)
        for h in range(HEADS):
            for k in range(lists):
                source = score_ref[slots[k], pl.ds(rels[k] * HEADS + h, 1), :]
                logit = jnp.maximum(u_ref[h, rels[k]] + source, w_ref[h, rels[k]] + 0.2 * source)
                prob = jnp.exp2(logit).astype(BF16)
                prob_ref[h, :, k * cols : (k + 1) * cols] = jnp.minimum(prob, cap_ref[b, k])
        for h in range(HEADS):
            least = jnp.minimum(least, finish(h))

        @pl.when(jnp.logical_not(jnp.min(least) > 2.0**-90))
        def _():
            for h in range(HEADS):
                for r in range(relations):
                    u_ref[h, r] = spread(r, h)

                def raw(k):
                    r, slot = rel_ref[b, k], slot_ref[b, k]
                    x = u_ref[h, r] + score_ref[slot, pl.ds(r * HEADS + h, 1), :]
                    return jnp.where(cap_ref[b, k].astype(F32) > 0, jnp.maximum(x, 0.2 * x), -jnp.inf)

                w_ref[h, 0] = jnp.full((rows, cols), -jnp.inf, F32)

                def climb(k, carry):
                    w_ref[h, 0] = jnp.maximum(w_ref[h, 0], raw(k))
                    return carry

                lax.fori_loop(0, lists, climb, 0)
                w_ref[h, 0] = jnp.broadcast_to(jnp.max(w_ref[h, 0], axis=1, keepdims=True), (rows, cols))

                def weigh(k, carry):
                    at = pl.ds(pl.multiple_of(k * cols, cols), cols)
                    prob_ref[h, :, at] = jnp.exp2(raw(k) - w_ref[h, 0]).astype(BF16)
                    return carry

                lax.fori_loop(0, lists, weigh, 0)
                finish(h)

        return carry

    lax.fori_loop(0, blocks, body, 0)


def attend(hidden, cap, relation_ids, source_slots, values, scores, tgt_vectors):
    blocks, lists, rows, cols = cap.shape
    width = hidden.shape[1]
    relations = values.shape[1]
    scalars, inside = pl.BlockSpec(memory_space=pltpu.SMEM), pl.BlockSpec(memory_space=pltpu.VMEM)
    return pl.pallas_call(
        attend_kernel,
        in_specs=[scalars] * 2 + [inside] * 5,
        out_specs=inside,
        scratch_shapes=[
            pltpu.VMEM((HEADS, relations, rows, cols), F32),
            pltpu.VMEM((HEADS, relations, rows, cols), F32),
            pltpu.VMEM((HEADS, rows, lists * cols), BF16),
        ],
        out_shape=jax.ShapeDtypeStruct((blocks, rows, width), BF16),
        compiler_params=pltpu.CompilerParams(vmem_limit_bytes=24 * 1024 * 1024),
        name="attend",
    )(relation_ids, source_slots, hidden.reshape(blocks, rows, width), cap, tgt_vectors, values, scores).reshape(
        blocks * rows, width
    )


def score_vectors(relation_weight, att_source, att_target):
    relations, width = att_source.shape
    head_width = width // HEADS
    split = att_source.reshape(relations, HEADS, head_width)
    moved = jnp.einsum(
        "rche,rhe->rhc",
        relation_weight.astype(F32).reshape(relations, width, HEADS, head_width),
        split,
        precision=lax.Precision.HIGHEST,
        preferred_element_type=F32,
    ).reshape(relations * HEADS, width)
    src = jnp.concatenate(three_parts(moved * LOG2E) + (jnp.zeros((8, width), BF16),), axis=0)
    own_head = (jnp.arange(width)[:, None] // head_width) == (jnp.arange(relations * HEADS)[None, :] % HEADS)
    spread = jnp.repeat(att_target.T, HEADS, axis=1)
    tgt = jnp.where(own_head, spread, 0.0) * LOG2E
    tgt = jnp.pad(tgt, ((0, 0), (0, 128 - relations * HEADS)))
    return src, jnp.stack(three_parts(tgt))


def shards(
    node_features,
    proj_weight,
    relation_weight,
    att_source,
    att_target,
    edge_mask,
    relation_ids,
    send_blocks,
    source_slots,
):
    block_rows = edge_mask.shape[-1]
    local_blocks = edge_mask.shape[0]
    rows_local = local_blocks * block_rows
    depth, width = proj_weight.shape
    n_feat = lax.axis_size("feat")
    n_graph = lax.axis_size("graph")
    levels = n_graph // 2
    place = lax.axis_index("graph")
    core, level = lax.rem(place, 2), place // 2

    def send(x, up, cores=0):
        pairs = [(p, (p + 2 * up) % n_graph ^ cores) for p in range(n_graph)]
        return lax.ppermute(x, "graph", pairs)

    cut = local_blocks // 2
    rows_a, half = cut * block_rows, width // 2
    features = node_features.T
    first = arrange(features, proj_weight, core, n_feat, 0, rows_a, half)
    first, features = lax.optimization_barrier((first, features))
    got = lax.all_to_all(first, "feat", 0, 0, tiled=True).reshape(n_feat * depth, rows_a + half)
    outgoing = arrange(features, proj_weight, core, n_feat, rows_a, rows_local, 0)
    outgoing, send_blocks = lax.optimization_barrier((outgoing, send_blocks))

    tables = jnp.stack([send_blocks[0]] + [send(send_blocks[0], d) for d in range(1, levels)])
    tables = jnp.stack([tables, send(tables, 0, 1)], axis=1)
    order = jnp.array([0, 1, 3, 2])
    index = tables[order, :, place].reshape(n_graph, CAP)
    peer = source_slots // CAP
    distance = (level - peer // 2 + levels) % levels
    slots = (2 * (distance ^ (distance >> 1)) + (peer % 2 ^ core)) * CAP + source_slots % CAP
    src_vectors, tgt_vectors = score_vectors(relation_weight, att_source, att_target)

    got, outgoing, cap, src_vectors, tgt_vectors, slots, index = lax.optimization_barrier(
        (got, outgoing, caps(edge_mask), src_vectors, tgt_vectors, slots, index)
    )
    later = lax.all_to_all(outgoing, "feat", 0, 0, tiled=True).reshape(n_feat * depth, rows_local - rows_a)

    mine = got[:, rows_a:]
    other = send(mine, 0, 1)
    whole = jnp.where(core == 0, jnp.concatenate([mine, other], axis=1), jnp.concatenate([other, mine], axis=1))

    def project(x):
        return lax.dot_general(x, whole, (((0,), (0,)), ((), ())), preferred_element_type=F32).astype(BF16)

    def both(pieces):
        return [pieces, [(send(x, 0, 1), low, high) for x, low, high in pieces]]

    def spread(group, first, kept):
        return transform(group, first, index, relation_weight, src_vectors, block_rows, *kept)

    def ring(part):
        return send(part, 1), send(part, -1)

    def forward(up, down):
        middle = up.shape[0] // 2
        return send(up[:middle], 1), send(down[middle:], -1)

    a = project(got[:, :rows_a])
    up_a, down_a = ring(a)
    later, up_a, down_a = lax.optimization_barrier((later, up_a, down_a))
    far_a = forward(up_a, down_a)
    b = project(later)
    up_b, down_b = ring(b)
    done = spread(both([(a, 0, cut), (b, cut, local_blocks)]), 0, (None, None))
    up_b, down_b, far_a, done = lax.optimization_barrier((up_b, down_b, far_a, done))
    far_b = forward(up_b, down_b)
    done = spread(
        both([(up_a, 0, cut), (up_b, cut, local_blocks)]) + both([(down_a, 0, cut), (down_b, cut, local_blocks)]), 2, done
    )
    far_b, done = lax.optimization_barrier((far_b, done))
    quarter = cut // 2
    far = [(x, n * quarter, (n + 1) * quarter) for n, x in enumerate(far_a + far_b)]
    values, scores = spread(both(far), 6, done)
    return attend(jnp.concatenate([a, b]), cap, relation_ids, slots, values, scores, tgt_vectors)


def solution(mesh):
    placed = (
        P("graph", "feat"),
        P("feat", None),
        P(),
        P(),
        P(),
        P(("graph", "feat"), None, None, None),
        P(("graph", "feat"), None),
        P(("graph", "feat"), None, None),
        P(("graph", "feat"), None),
    )
    return jax.shard_map(
        shards, mesh=mesh, in_specs=placed, out_specs=P(("graph", "feat"), None), check_vma=False
    )
```

```python
import functools

import jax
import jax.numpy as jnp
from jax import lax
from jax.experimental import pallas as pl
from jax.experimental.pallas import tpu as pltpu
from jax.sharding import PartitionSpec as P

HEADS = 4
CAP = 4
LOG2E = 1.4426950408889634
F32 = jnp.float32
BF16 = jnp.bfloat16


def arrange_kernel(low, high, core_ref, x_ref, w_ref, out_ref):
    peers, _, columns = out_ref.shape
    total = x_ref.shape[1] // peers
    rows = high - low
    for q in range(peers):
        out_ref[q, :, :rows] = x_ref[:, q * total + low : q * total + high]
        if columns > rows:
            out_ref[q, :, rows:] = w_ref[...]


def arrange(features, weight, core, peers, low, high, half):
    depth, columns = features.shape
    rows = columns // peers
    step = 4
    return pl.pallas_call(
        functools.partial(arrange_kernel, low, high),
        grid_spec=pltpu.PrefetchScalarGridSpec(
            num_scalar_prefetch=1,
            grid=(peers // step,),
            in_specs=[
                pl.BlockSpec((depth, step * rows), lambda i, core_ref: (0, i)),
                pl.BlockSpec((depth, weight.shape[1] // 2), lambda i, core_ref: (0, core_ref[0])),
            ],
            out_specs=pl.BlockSpec((step, depth, high - low + half), lambda i, core_ref: (i, 0, 0)),
        ),
        out_shape=jax.ShapeDtypeStruct((peers, depth, high - low + half), BF16),
        name="arrange",
    )(core.reshape(1), features, weight)


def three_parts(x):
    hi = lax.reduce_precision(x, 8, 7)
    rest = x - hi
    mid = lax.reduce_precision(rest, 8, 7)
    return hi.astype(BF16), mid.astype(BF16), (rest - mid).astype(BF16)


def transform_kernel(bounds, first, idx_ref, *refs):
    n_pieces = sum(len(p) for p in bounds)
    pieces = refs[:n_pieces]
    rw_ref, src_ref = refs[n_pieces : n_pieces + 2]
    val_ref, score_ref, hid_ref, sem = refs[-4:]
    relations, block = val_ref.shape[1:3]
    cap = sem.shape[1]

    def copy(piece, row, source, c):
        return pltpu.make_async_copy(
            piece.at[pl.ds(row, block)], hid_ref.at[source, pl.ds(c * block, block)], sem.at[source, c]
        )

    begin = 0
    for source in range(len(bounds)):
        for c in range(cap):
            wanted = idx_ref[first + source, c]
            for n, (low, high) in enumerate(bounds[source]):

                @pl.when((wanted >= low) & (wanted < high))
                def _():
                    copy(pieces[begin + n], pl.multiple_of((wanted - low) * block, block), source, c).start()

        begin += len(bounds[source])
    for source in range(len(bounds)):
        for c in range(cap):
            copy(pieces[0], 0, source, c).wait()
        hid = hid_ref[source]
        at = (first + source) * cap
        for r in range(relations):
            moved = jnp.dot(hid, rw_ref[r], preferred_element_type=F32).astype(BF16)
            for c in range(cap):
                val_ref[at + c, r] = moved[c * block : (c + 1) * block]
        raw = lax.dot_general(src_ref[...], hid, (((1,), (1,)), ((), ())), preferred_element_type=F32)
        score = raw[0:8] + raw[8:16] + raw[16:24]
        for c in range(cap):
            score_ref[at + c] = score[:, c * block : (c + 1) * block]

def transform(sources, first, index, relation_weight, src_vectors, block, values, scores):
    bounds = tuple(tuple((low, high) for _, low, high in pieces) for pieces in sources)
    arrays = [array for pieces in sources for array, _, _ in pieces]
    peers, cap = index.shape
    relations, width = relation_weight.shape[:2]
    anywhere, inside = pl.BlockSpec(memory_space=pl.ANY), pl.BlockSpec(memory_space=pltpu.VMEM)
    kept = () if values is None else (values, scores)
    at = 1 + len(arrays) + 2
    return pl.pallas_call(
        functools.partial(transform_kernel, bounds, first),
        in_specs=[pl.BlockSpec(memory_space=pltpu.SMEM)] + [anywhere] * len(arrays) + [inside] * (2 + len(kept)),
        out_specs=[inside, inside],
        scratch_shapes=[
            pltpu.VMEM((len(bounds), cap * block, width), BF16),
            pltpu.SemaphoreType.DMA((len(bounds), cap)),
        ],
        out_shape=[
            jax.ShapeDtypeStruct((peers * cap, relations, block, width), BF16),
            jax.ShapeDtypeStruct((peers * cap, 8, block), F32),
        ],
        input_output_aliases={at + n: n for n in range(len(kept))},
        compiler_params=pltpu.CompilerParams(vmem_limit_bytes=24 * 1024 * 1024),
        name="transform",
    )(index, *arrays, relation_weight, src_vectors, *kept)


def cap_kernel(mask_ref, cap_ref):
    cap_ref[...] = jnp.where(mask_ref[...] > 0, jnp.inf, 0.0).astype(BF16)


def caps(edge_mask):
    shape = edge_mask.shape
    spec = pl.BlockSpec((1,) + shape[1:], lambda b: (b, 0, 0, 0))
    return pl.pallas_call(
        cap_kernel,
        grid=shape[:1],
        in_specs=[spec],
        out_specs=spec,
        out_shape=jax.ShapeDtypeStruct(shape, BF16),
        name="caps",
    )(edge_mask)


def attend_kernel(
    rel_ref, slot_ref, own_ref, cap_ref, tgt_ref, val_ref, score_ref, out_ref, u_ref, w_ref, prob_ref
):
    blocks, lists, rows, cols = cap_ref.shape
    relations = u_ref.shape[1]
    ones = jnp.ones((lists * cols, cols), BF16)

    def body(b, carry):
        own = own_ref[b]
        target = jnp.dot(own, tgt_ref[0], preferred_element_type=F32)
        target += jnp.dot(own, tgt_ref[1], preferred_element_type=F32)
        target += jnp.dot(own, tgt_ref[2], preferred_element_type=F32)
        rels = [rel_ref[b, k] for k in range(lists)]
        slots = [slot_ref[b, k] for k in range(lists)]

        def spread(r, h):
            return jnp.broadcast_to(target[:, r * HEADS + h : r * HEADS + h + 1], (rows, cols))

        def finish(h):
            lanes = slice(h * cols, (h + 1) * cols)
            value = jnp.concatenate([val_ref[slots[k], rels[k], :, lanes] for k in range(lists)], axis=0)
            summed = jnp.dot(prob_ref[h], jnp.concatenate([value, ones], axis=1), preferred_element_type=F32)
            total = summed[:, cols:]
            mixed = summed[:, :cols] / total + own[:, lanes].astype(F32)
            out_ref[b, :, lanes] = jnp.where(mixed > 0, mixed, jnp.exp(jnp.minimum(mixed, 0.0)) - 1.0).astype(BF16)
            return total

        reach = [jnp.full((8, cols), -jnp.inf, F32) for _ in range(relations)]
        for k in range(lists):
            source = score_ref[slots[k]]
            for r in range(relations):
                reach[r] = jnp.maximum(reach[r], jnp.where(rels[k] == r, source, -jnp.inf))
        for h in range(HEADS):
            bound = jnp.full((rows, cols), -jnp.inf, F32)
            for r in range(relations):
                c = r * HEADS + h
                most = spread(r, h) + jnp.max(reach[r][c : c + 1, :], axis=1, keepdims=True)
                bound = jnp.maximum(bound, jnp.maximum(most, 0.2 * most))
            for r in range(relations):
                u_ref[h, r] = spread(r, h) - bound
                w_ref[h, r] = 0.2 * spread(r, h) - bound
        least = jnp.full((rows, cols), jnp.inf, F32)
        for h in range(HEADS):
            for k in range(lists):
                source = score_ref[slots[k], pl.ds(rels[k] * HEADS + h, 1), :]
                logit = jnp.maximum(u_ref[h, rels[k]] + source, w_ref[h, rels[k]] + 0.2 * source)
                prob = jnp.exp2(logit).astype(BF16)
                prob_ref[h, :, k * cols : (k + 1) * cols] = jnp.minimum(prob, cap_ref[b, k])
        for h in range(HEADS):
            least = jnp.minimum(least, finish(h))

        @pl.when(jnp.logical_not(jnp.min(least) > 2.0**-90))
        def _():
            for h in range(HEADS):
                for r in range(relations):
                    u_ref[h, r] = spread(r, h)

                def raw(k):
                    r, slot = rel_ref[b, k], slot_ref[b, k]
                    x = u_ref[h, r] + score_ref[slot, pl.ds(r * HEADS + h, 1), :]
                    return jnp.where(cap_ref[b, k].astype(F32) > 0, jnp.maximum(x, 0.2 * x), -jnp.inf)

                w_ref[h, 0] = jnp.full((rows, cols), -jnp.inf, F32)

                def climb(k, carry):
                    w_ref[h, 0] = jnp.maximum(w_ref[h, 0], raw(k))
                    return carry

                lax.fori_loop(0, lists, climb, 0)
                w_ref[h, 0] = jnp.broadcast_to(jnp.max(w_ref[h, 0], axis=1, keepdims=True), (rows, cols))

                def weigh(k, carry):
                    at = pl.ds(pl.multiple_of(k * cols, cols), cols)
                    prob_ref[h, :, at] = jnp.exp2(raw(k) - w_ref[h, 0]).astype(BF16)
                    return carry

                lax.fori_loop(0, lists, weigh, 0)
                finish(h)

        return carry

    lax.fori_loop(0, blocks, body, 0)


def attend(hidden, cap, relation_ids, source_slots, values, scores, tgt_vectors):
    blocks, lists, rows, cols = cap.shape
    width = hidden.shape[1]
    relations = values.shape[1]
    scalars, inside = pl.BlockSpec(memory_space=pltpu.SMEM), pl.BlockSpec(memory_space=pltpu.VMEM)
    return pl.pallas_call(
        attend_kernel,
        in_specs=[scalars] * 2 + [inside] * 5,
        out_specs=inside,
        scratch_shapes=[
            pltpu.VMEM((HEADS, relations, rows, cols), F32),
            pltpu.VMEM((HEADS, relations, rows, cols), F32),
            pltpu.VMEM((HEADS, rows, lists * cols), BF16),
        ],
        out_shape=jax.ShapeDtypeStruct((blocks, rows, width), BF16),
        compiler_params=pltpu.CompilerParams(vmem_limit_bytes=24 * 1024 * 1024),
        name="attend",
    )(relation_ids, source_slots, hidden.reshape(blocks, rows, width), cap, tgt_vectors, values, scores).reshape(
        blocks * rows, width
    )


def score_vectors(relation_weight, att_source, att_target):
    relations, width = att_source.shape
    head_width = width // HEADS
    split = att_source.reshape(relations, HEADS, head_width)
    moved = jnp.einsum(
        "rche,rhe->rhc",
        relation_weight.astype(F32).reshape(relations, width, HEADS, head_width),
        split,
        precision=lax.Precision.HIGHEST,
        preferred_element_type=F32,
    ).reshape(relations * HEADS, width)
    src = jnp.concatenate(three_parts(moved * LOG2E) + (jnp.zeros((8, width), BF16),), axis=0)
    own_head = (jnp.arange(width)[:, None] // head_width) == (jnp.arange(relations * HEADS)[None, :] % HEADS)
    spread = jnp.repeat(att_target.T, HEADS, axis=1)
    tgt = jnp.where(own_head, spread, 0.0) * LOG2E
    tgt = jnp.pad(tgt, ((0, 0), (0, 128 - relations * HEADS)))
    return src, jnp.stack(three_parts(tgt))


def shards(
    node_features,
    proj_weight,
    relation_weight,
    att_source,
    att_target,
    edge_mask,
    relation_ids,
    send_blocks,
    source_slots,
):
    block_rows = edge_mask.shape[-1]
    local_blocks = edge_mask.shape[0]
    rows_local = local_blocks * block_rows
    depth, width = proj_weight.shape
    n_feat = lax.axis_size("feat")
    n_graph = lax.axis_size("graph")
    levels = n_graph // 2
    place = lax.axis_index("graph")
    core, level = lax.rem(place, 2), place // 2

    def send(x, up, cores=0):
        pairs = [(p, (p + 2 * up) % n_graph ^ cores) for p in range(n_graph)]
        return lax.ppermute(x, "graph", pairs)

    cut = local_blocks // 2
    rows_a, half = cut * block_rows, width // 2
    features = node_features.T
    first = arrange(features, proj_weight, core, n_feat, 0, rows_a, half)
    first, features = lax.optimization_barrier((first, features))
    got = lax.all_to_all(first, "feat", 0, 0, tiled=True).reshape(n_feat * depth, rows_a + half)
    outgoing = arrange(features, proj_weight, core, n_feat, rows_a, rows_local, 0)
    outgoing, send_blocks = lax.optimization_barrier((outgoing, send_blocks))

    tables = jnp.stack([send_blocks[0]] + [send(send_blocks[0], d) for d in range(1, levels)])
    tables = jnp.stack([tables, send(tables, 0, 1)], axis=1)
    order = jnp.array([0, 1, 3, 2])
    index = tables[order, :, place].reshape(n_graph, CAP)
    peer = source_slots // CAP
    distance = (level - peer // 2 + levels) % levels
    slots = (2 * (distance ^ (distance >> 1)) + (peer % 2 ^ core)) * CAP + source_slots % CAP
    src_vectors, tgt_vectors = score_vectors(relation_weight, att_source, att_target)

    got, outgoing, src_vectors, tgt_vectors, slots, index = lax.optimization_barrier(
        (got, outgoing, src_vectors, tgt_vectors, slots, index)
    )
    later = lax.all_to_all(outgoing, "feat", 0, 0, tiled=True).reshape(n_feat * depth, rows_local - rows_a)

    mine = got[:, rows_a:]
    other = send(mine, 0, 1)
    whole = jnp.where(core == 0, jnp.concatenate([mine, other], axis=1), jnp.concatenate([other, mine], axis=1))

    def project(x):
        return lax.dot_general(x, whole, (((0,), (0,)), ((), ())), preferred_element_type=F32).astype(BF16)

    def both(pieces):
        return [pieces, [(send(x, 0, 1), low, high) for x, low, high in pieces]]

    def spread(group, first, kept):
        return transform(group, first, index, relation_weight, src_vectors, block_rows, *kept)

    def ring(part):
        return send(part, 1), send(part, -1)

    def forward(up, down):
        middle = up.shape[0] // 2
        return send(up[:middle], 1), send(down[middle:], -1)

    a = project(got[:, :rows_a])
    up_a, down_a = ring(a)
    later, up_a, down_a = lax.optimization_barrier((later, up_a, down_a))
    far_a = forward(up_a, down_a)
    b = project(later)
    up_b, down_b = ring(b)
    done = spread(both([(a, 0, cut), (b, cut, local_blocks)]), 0, (None, None))
    edge_mask, done = lax.optimization_barrier((edge_mask, done))
    cap = caps(edge_mask)
    up_b, down_b, far_a, cap, done = lax.optimization_barrier((up_b, down_b, far_a, cap, done))
    far_b = forward(up_b, down_b)
    done = spread(
        both([(up_a, 0, cut), (up_b, cut, local_blocks)]) + both([(down_a, 0, cut), (down_b, cut, local_blocks)]), 2, done
    )
    far_b, done = lax.optimization_barrier((far_b, done))
    quarter = cut // 2
    far = [(x, n * quarter, (n + 1) * quarter) for n, x in enumerate(far_a + far_b)]
    values, scores = spread(both(far), 6, done)
    return attend(jnp.concatenate([a, b]), cap, relation_ids, slots, values, scores, tgt_vectors)


def solution(mesh):
    placed = (
        P("graph", "feat"),
        P("feat", None),
        P(),
        P(),
        P(),
        P(("graph", "feat"), None, None, None),
        P(("graph", "feat"), None),
        P(("graph", "feat"), None, None),
        P(("graph", "feat"), None),
    )
    return jax.shard_map(
        shards, mesh=mesh, in_specs=placed, out_specs=P(("graph", "feat"), None), check_vma=False
    )
```

```python
import functools

import jax
import jax.numpy as jnp
from jax import lax
from jax.experimental import pallas as pl
from jax.experimental.pallas import tpu as pltpu
from jax.sharding import PartitionSpec as P

HEADS = 4
CAP = 4
LOG2E = 1.4426950408889634
F32 = jnp.float32
BF16 = jnp.bfloat16


def arrange_kernel(low, high, core_ref, x_ref, w_ref, out_ref):
    peers, _, columns = out_ref.shape
    total = x_ref.shape[1] // peers
    rows = high - low
    for q in range(peers):
        out_ref[q, :, :rows] = x_ref[:, q * total + low : q * total + high]
        if columns > rows:
            out_ref[q, :, rows:] = w_ref[...]


def arrange(features, weight, core, peers, low, high, half):
    depth, columns = features.shape
    rows = columns // peers
    step = 4
    return pl.pallas_call(
        functools.partial(arrange_kernel, low, high),
        grid_spec=pltpu.PrefetchScalarGridSpec(
            num_scalar_prefetch=1,
            grid=(peers // step,),
            in_specs=[
                pl.BlockSpec((depth, step * rows), lambda i, core_ref: (0, i)),
                pl.BlockSpec((depth, weight.shape[1] // 2), lambda i, core_ref: (0, core_ref[0])),
            ],
            out_specs=pl.BlockSpec((step, depth, high - low + half), lambda i, core_ref: (i, 0, 0)),
        ),
        out_shape=jax.ShapeDtypeStruct((peers, depth, high - low + half), BF16),
        name="arrange",
    )(core.reshape(1), features, weight)


def three_parts(x):
    hi = lax.reduce_precision(x, 8, 7)
    rest = x - hi
    mid = lax.reduce_precision(rest, 8, 7)
    return hi.astype(BF16), mid.astype(BF16), (rest - mid).astype(BF16)


def transform_kernel(bounds, first, idx_ref, *refs):
    n_pieces = sum(len(p) for p in bounds)
    pieces = refs[:n_pieces]
    rw_ref, src_ref = refs[n_pieces : n_pieces + 2]
    val_ref, score_ref, hid_ref, sem = refs[-4:]
    relations, block = val_ref.shape[1:3]
    cap = sem.shape[1]

    def copy(piece, row, source, c):
        return pltpu.make_async_copy(
            piece.at[pl.ds(row, block)], hid_ref.at[source, pl.ds(c * block, block)], sem.at[source, c]
        )

    begin = 0
    for source in range(len(bounds)):
        for c in range(cap):
            wanted = idx_ref[first + source, c]
            for n, (low, high) in enumerate(bounds[source]):

                @pl.when((wanted >= low) & (wanted < high))
                def _():
                    copy(pieces[begin + n], pl.multiple_of((wanted - low) * block, block), source, c).start()

        begin += len(bounds[source])
    for source in range(len(bounds)):
        for c in range(cap):
            copy(pieces[0], 0, source, c).wait()
        hid = hid_ref[source]
        at = (first + source) * cap
        for r in range(relations):
            moved = jnp.dot(hid, rw_ref[r], preferred_element_type=F32).astype(BF16)
            for c in range(cap):
                val_ref[at + c, r] = moved[c * block : (c + 1) * block]
        raw = lax.dot_general(src_ref[...], hid, (((1,), (1,)), ((), ())), preferred_element_type=F32)
        score = raw[0:8] + raw[8:16] + raw[16:24]
        for c in range(cap):
            score_ref[at + c] = score[:, c * block : (c + 1) * block]

def transform(sources, first, index, relation_weight, src_vectors, block, values, scores):
    bounds = tuple(tuple((low, high) for _, low, high in pieces) for pieces in sources)
    arrays = [array for pieces in sources for array, _, _ in pieces]
    peers, cap = index.shape
    relations, width = relation_weight.shape[:2]
    anywhere, inside = pl.BlockSpec(memory_space=pl.ANY), pl.BlockSpec(memory_space=pltpu.VMEM)
    kept = () if values is None else (values, scores)
    at = 1 + len(arrays) + 2
    return pl.pallas_call(
        functools.partial(transform_kernel, bounds, first),
        in_specs=[pl.BlockSpec(memory_space=pltpu.SMEM)] + [anywhere] * len(arrays) + [inside] * (2 + len(kept)),
        out_specs=[inside, inside],
        scratch_shapes=[
            pltpu.VMEM((len(bounds), cap * block, width), BF16),
            pltpu.SemaphoreType.DMA((len(bounds), cap)),
        ],
        out_shape=[
            jax.ShapeDtypeStruct((peers * cap, relations, block, width), BF16),
            jax.ShapeDtypeStruct((peers * cap, 8, block), F32),
        ],
        input_output_aliases={at + n: n for n in range(len(kept))},
        compiler_params=pltpu.CompilerParams(vmem_limit_bytes=24 * 1024 * 1024),
        name="transform",
    )(index, *arrays, relation_weight, src_vectors, *kept)


def cap_kernel(mask_ref, cap_ref):
    cap_ref[...] = jnp.where(mask_ref[...] > 0, jnp.inf, 0.0).astype(BF16)


def caps(edge_mask):
    shape = edge_mask.shape
    spec = pl.BlockSpec((1,) + shape[1:], lambda b: (b, 0, 0, 0))
    return pl.pallas_call(
        cap_kernel,
        grid=shape[:1],
        in_specs=[spec],
        out_specs=spec,
        out_shape=jax.ShapeDtypeStruct(shape, BF16),
        name="caps",
    )(edge_mask)


def attend_kernel(
    rel_ref, slot_ref, own_ref, cap_ref, tgt_ref, val_ref, score_ref, out_ref, u_ref, w_ref, prob_ref
):
    blocks, lists, rows, cols = cap_ref.shape
    relations = u_ref.shape[1]
    ones = jnp.ones((lists * cols, cols), BF16)

    def body(b, carry):
        own = own_ref[b]
        target = jnp.dot(own, tgt_ref[0], preferred_element_type=F32)
        target += jnp.dot(own, tgt_ref[1], preferred_element_type=F32)
        target += jnp.dot(own, tgt_ref[2], preferred_element_type=F32)
        rels = [rel_ref[b, k] for k in range(lists)]
        slots = [slot_ref[b, k] for k in range(lists)]

        def spread(r, h):
            return jnp.broadcast_to(target[:, r * HEADS + h : r * HEADS + h + 1], (rows, cols))

        def finish(h):
            lanes = slice(h * cols, (h + 1) * cols)
            value = jnp.concatenate([val_ref[slots[k], rels[k], :, lanes] for k in range(lists)], axis=0)
            summed = jnp.dot(prob_ref[h], jnp.concatenate([value, ones], axis=1), preferred_element_type=F32)
            total = summed[:, cols:]
            mixed = summed[:, :cols] / total + own[:, lanes].astype(F32)
            out_ref[b, :, lanes] = jnp.where(mixed > 0, mixed, jnp.exp(jnp.minimum(mixed, 0.0)) - 1.0).astype(BF16)
            return total

        reach = [jnp.full((8, cols), -jnp.inf, F32) for _ in range(relations)]
        for k in range(lists):
            source = score_ref[slots[k]]
            for r in range(relations):
                reach[r] = jnp.maximum(reach[r], jnp.where(rels[k] == r, source, -jnp.inf))
        for h in range(HEADS):
            bound = jnp.full((rows, cols), -jnp.inf, F32)
            for r in range(relations):
                c = r * HEADS + h
                most = spread(r, h) + jnp.max(reach[r][c : c + 1, :], axis=1, keepdims=True)
                bound = jnp.maximum(bound, jnp.maximum(most, 0.2 * most))
            for r in range(relations):
                u_ref[h, r] = spread(r, h) - bound
                w_ref[h, r] = 0.2 * spread(r, h) - bound
        least = jnp.full((rows, cols), jnp.inf, F32)
        for h in range(HEADS):
            for k in range(lists):
                source = score_ref[slots[k], pl.ds(rels[k] * HEADS + h, 1), :]
                logit = jnp.maximum(u_ref[h, rels[k]] + source, w_ref[h, rels[k]] + 0.2 * source)
                prob = jnp.exp2(logit).astype(BF16)
                prob_ref[h, :, k * cols : (k + 1) * cols] = jnp.minimum(prob, cap_ref[b, k])
        for h in range(HEADS):
            least = jnp.minimum(least, finish(h))

        @pl.when(jnp.logical_not(jnp.min(least) > 2.0**-90))
        def _():
            for h in range(HEADS):
                for r in range(relations):
                    u_ref[h, r] = spread(r, h)

                def raw(k):
                    r, slot = rel_ref[b, k], slot_ref[b, k]
                    x = u_ref[h, r] + score_ref[slot, pl.ds(r * HEADS + h, 1), :]
                    return jnp.where(cap_ref[b, k].astype(F32) > 0, jnp.maximum(x, 0.2 * x), -jnp.inf)

                w_ref[h, 0] = jnp.full((rows, cols), -jnp.inf, F32)

                def climb(k, carry):
                    w_ref[h, 0] = jnp.maximum(w_ref[h, 0], raw(k))
                    return carry

                lax.fori_loop(0, lists, climb, 0)
                w_ref[h, 0] = jnp.broadcast_to(jnp.max(w_ref[h, 0], axis=1, keepdims=True), (rows, cols))

                def weigh(k, carry):
                    at = pl.ds(pl.multiple_of(k * cols, cols), cols)
                    prob_ref[h, :, at] = jnp.exp2(raw(k) - w_ref[h, 0]).astype(BF16)
                    return carry

                lax.fori_loop(0, lists, weigh, 0)
                finish(h)

        return carry

    lax.fori_loop(0, blocks, body, 0)


def attend(hidden, cap, relation_ids, source_slots, values, scores, tgt_vectors):
    blocks, lists, rows, cols = cap.shape
    width = hidden.shape[1]
    relations = values.shape[1]
    scalars, inside = pl.BlockSpec(memory_space=pltpu.SMEM), pl.BlockSpec(memory_space=pltpu.VMEM)
    return pl.pallas_call(
        attend_kernel,
        in_specs=[scalars] * 2 + [inside] * 5,
        out_specs=inside,
        scratch_shapes=[
            pltpu.VMEM((HEADS, relations, rows, cols), F32),
            pltpu.VMEM((HEADS, relations, rows, cols), F32),
            pltpu.VMEM((HEADS, rows, lists * cols), BF16),
        ],
        out_shape=jax.ShapeDtypeStruct((blocks, rows, width), BF16),
        compiler_params=pltpu.CompilerParams(vmem_limit_bytes=24 * 1024 * 1024),
        name="attend",
    )(relation_ids, source_slots, hidden.reshape(blocks, rows, width), cap, tgt_vectors, values, scores).reshape(
        blocks * rows, width
    )


def score_vectors(relation_weight, att_source, att_target):
    relations, width = att_source.shape
    head_width = width // HEADS
    split = att_source.reshape(relations, HEADS, head_width)
    moved = jnp.einsum(
        "rche,rhe->rhc",
        relation_weight.astype(F32).reshape(relations, width, HEADS, head_width),
        split,
        precision=lax.Precision.HIGHEST,
        preferred_element_type=F32,
    ).reshape(relations * HEADS, width)
    src = jnp.concatenate(three_parts(moved * LOG2E) + (jnp.zeros((8, width), BF16),), axis=0)
    own_head = (jnp.arange(width)[:, None] // head_width) == (jnp.arange(relations * HEADS)[None, :] % HEADS)
    spread = jnp.repeat(att_target.T, HEADS, axis=1)
    tgt = jnp.where(own_head, spread, 0.0) * LOG2E
    tgt = jnp.pad(tgt, ((0, 0), (0, 128 - relations * HEADS)))
    return src, jnp.stack(three_parts(tgt))


def shards(
    node_features,
    proj_weight,
    relation_weight,
    att_source,
    att_target,
    edge_mask,
    relation_ids,
    send_blocks,
    source_slots,
):
    block_rows = edge_mask.shape[-1]
    local_blocks = edge_mask.shape[0]
    rows_local = local_blocks * block_rows
    depth, width = proj_weight.shape
    n_feat = lax.axis_size("feat")
    n_graph = lax.axis_size("graph")
    levels = n_graph // 2
    place = lax.axis_index("graph")
    core, level = lax.rem(place, 2), place // 2

    def send(x, up, cores=0):
        pairs = [(p, (p + 2 * up) % n_graph ^ cores) for p in range(n_graph)]
        return lax.ppermute(x, "graph", pairs)

    cut = local_blocks // 2
    rows_a, half = cut * block_rows, width // 2
    features = node_features.T
    first = arrange(features, proj_weight, core, n_feat, 0, rows_a, half)
    first, features, send_blocks = lax.optimization_barrier((first, features, send_blocks))
    got = lax.all_to_all(first, "feat", 0, 0, tiled=True).reshape(n_feat * depth, rows_a + half)
    outgoing = arrange(features, proj_weight, core, n_feat, rows_a, rows_local, 0)

    tables = jnp.stack([send_blocks[0]] + [send(send_blocks[0], d) for d in range(1, levels)])
    tables = jnp.stack([tables, send(tables, 0, 1)], axis=1)
    order = jnp.array([0, 1, 3, 2])
    index = tables[order, :, place].reshape(n_graph, CAP)
    peer = source_slots // CAP
    distance = (level - peer // 2 + levels) % levels
    slots = (2 * (distance ^ (distance >> 1)) + (peer % 2 ^ core)) * CAP + source_slots % CAP
    src_vectors, tgt_vectors = score_vectors(relation_weight, att_source, att_target)

    got, outgoing, cap, src_vectors, tgt_vectors, slots, index = lax.optimization_barrier(
        (got, outgoing, caps(edge_mask), src_vectors, tgt_vectors, slots, index)
    )
    later = lax.all_to_all(outgoing, "feat", 0, 0, tiled=True).reshape(n_feat * depth, rows_local - rows_a)

    mine = got[:, rows_a:]
    other = send(mine, 0, 1)
    whole = jnp.where(core == 0, jnp.concatenate([mine, other], axis=1), jnp.concatenate([other, mine], axis=1))

    def project(x):
        return lax.dot_general(x, whole, (((0,), (0,)), ((), ())), preferred_element_type=F32).astype(BF16)

    def both(pieces):
        return [pieces, [(send(x, 0, 1), low, high) for x, low, high in pieces]]

    def spread(group, first, kept):
        return transform(group, first, index, relation_weight, src_vectors, block_rows, *kept)

    def ring(part):
        return send(part, 1), send(part, -1)

    def forward(up, down):
        middle = up.shape[0] // 2
        return send(up[:middle], 1), send(down[middle:], -1)

    a = project(got[:, :rows_a])
    up_a, down_a = ring(a)
    later, up_a, down_a = lax.optimization_barrier((later, up_a, down_a))
    far_a = forward(up_a, down_a)
    b = project(later)
    up_b, down_b = ring(b)
    done = spread(both([(a, 0, cut), (b, cut, local_blocks)]), 0, (None, None))
    up_b, down_b, far_a, done = lax.optimization_barrier((up_b, down_b, far_a, done))
    far_b = forward(up_b, down_b)
    done = spread(
        both([(up_a, 0, cut), (up_b, cut, local_blocks)]) + both([(down_a, 0, cut), (down_b, cut, local_blocks)]), 2, done
    )
    far_b, done = lax.optimization_barrier((far_b, done))
    quarter = cut // 2
    far = [(x, n * quarter, (n + 1) * quarter) for n, x in enumerate(far_a + far_b)]
    values, scores = spread(both(far), 6, done)
    return attend(jnp.concatenate([a, b]), cap, relation_ids, slots, values, scores, tgt_vectors)


def solution(mesh):
    placed = (
        P("graph", "feat"),
        P("feat", None),
        P(),
        P(),
        P(),
        P(("graph", "feat"), None, None, None),
        P(("graph", "feat"), None),
        P(("graph", "feat"), None, None),
        P(("graph", "feat"), None),
    )
    return jax.shard_map(
        shards, mesh=mesh, in_specs=placed, out_specs=P(("graph", "feat"), None), check_vma=False
    )
```

```python
import functools

import jax
import jax.numpy as jnp
from jax import lax
from jax.experimental import pallas as pl
from jax.experimental.pallas import tpu as pltpu
from jax.sharding import PartitionSpec as P

HEADS = 4
CAP = 4
LOG2E = 1.4426950408889634
F32 = jnp.float32
BF16 = jnp.bfloat16


def arrange_kernel(low, high, core_ref, x_ref, w_ref, out_ref):
    peers, _, columns = out_ref.shape
    total = x_ref.shape[1] // peers
    rows = high - low
    for q in range(peers):
        out_ref[q, :, :rows] = x_ref[:, q * total + low : q * total + high]
        if columns > rows:
            out_ref[q, :, rows:] = w_ref[...]


def arrange(features, weight, core, peers, low, high, half):
    depth, columns = features.shape
    rows = columns // peers
    step = 4
    return pl.pallas_call(
        functools.partial(arrange_kernel, low, high),
        grid_spec=pltpu.PrefetchScalarGridSpec(
            num_scalar_prefetch=1,
            grid=(peers // step,),
            in_specs=[
                pl.BlockSpec((depth, step * rows), lambda i, core_ref: (0, i)),
                pl.BlockSpec((depth, weight.shape[1] // 2), lambda i, core_ref: (0, core_ref[0])),
            ],
            out_specs=pl.BlockSpec((step, depth, high - low + half), lambda i, core_ref: (i, 0, 0)),
        ),
        out_shape=jax.ShapeDtypeStruct((peers, depth, high - low + half), BF16),
        name="arrange",
    )(core.reshape(1), features, weight)


def three_parts(x):
    hi = lax.reduce_precision(x, 8, 7)
    rest = x - hi
    mid = lax.reduce_precision(rest, 8, 7)
    return hi.astype(BF16), mid.astype(BF16), (rest - mid).astype(BF16)


def transform_kernel(bounds, first, idx_ref, *refs):
    n_pieces = sum(len(p) for p in bounds)
    pieces = refs[:n_pieces]
    rw_ref, src_ref = refs[n_pieces : n_pieces + 2]
    val_ref, score_ref, hid_ref, sem = refs[-4:]
    relations, block = val_ref.shape[1:3]
    cap = sem.shape[1]

    def copy(piece, row, source, c):
        return pltpu.make_async_copy(
            piece.at[pl.ds(row, block)], hid_ref.at[source, pl.ds(c * block, block)], sem.at[source, c]
        )

    begin = 0
    for source in range(len(bounds)):
        for c in range(cap):
            wanted = idx_ref[first + source, c]
            for n, (low, high) in enumerate(bounds[source]):

                @pl.when((wanted >= low) & (wanted < high))
                def _():
                    copy(pieces[begin + n], pl.multiple_of((wanted - low) * block, block), source, c).start()

        begin += len(bounds[source])
    for source in range(len(bounds)):
        for c in range(cap):
            copy(pieces[0], 0, source, c).wait()
        hid = hid_ref[source]
        at = (first + source) * cap
        for r in range(relations):
            moved = jnp.dot(hid, rw_ref[r], preferred_element_type=F32).astype(BF16)
            for c in range(cap):
                val_ref[at + c, r] = moved[c * block : (c + 1) * block]
        raw = lax.dot_general(src_ref[...], hid, (((1,), (1,)), ((), ())), preferred_element_type=F32)
        score = raw[0:8] + raw[8:16] + raw[16:24]
        for c in range(cap):
            score_ref[at + c] = score[:, c * block : (c + 1) * block]

def transform(sources, first, index, relation_weight, src_vectors, block, values, scores):
    bounds = tuple(tuple((low, high) for _, low, high in pieces) for pieces in sources)
    arrays = [array for pieces in sources for array, _, _ in pieces]
    peers, cap = index.shape
    relations, width = relation_weight.shape[:2]
    anywhere, inside = pl.BlockSpec(memory_space=pl.ANY), pl.BlockSpec(memory_space=pltpu.VMEM)
    kept = () if values is None else (values, scores)
    at = 1 + len(arrays) + 2
    return pl.pallas_call(
        functools.partial(transform_kernel, bounds, first),
        in_specs=[pl.BlockSpec(memory_space=pltpu.SMEM)] + [anywhere] * len(arrays) + [inside] * (2 + len(kept)),
        out_specs=[inside, inside],
        scratch_shapes=[
            pltpu.VMEM((len(bounds), cap * block, width), BF16),
            pltpu.SemaphoreType.DMA((len(bounds), cap)),
        ],
        out_shape=[
            jax.ShapeDtypeStruct((peers * cap, relations, block, width), BF16),
            jax.ShapeDtypeStruct((peers * cap, 8, block), F32),
        ],
        input_output_aliases={at + n: n for n in range(len(kept))},
        compiler_params=pltpu.CompilerParams(vmem_limit_bytes=24 * 1024 * 1024),
        name="transform",
    )(index, *arrays, relation_weight, src_vectors, *kept)


def cap_kernel(mask_ref, cap_ref):
    cap_ref[...] = jnp.where(mask_ref[...] > 0, jnp.inf, 0.0).astype(BF16)


def caps(edge_mask):
    shape = edge_mask.shape
    spec = pl.BlockSpec((1,) + shape[1:], lambda b: (b, 0, 0, 0))
    return pl.pallas_call(
        cap_kernel,
        grid=shape[:1],
        in_specs=[spec],
        out_specs=spec,
        out_shape=jax.ShapeDtypeStruct(shape, BF16),
        name="caps",
    )(edge_mask)


def attend_kernel(
    rel_ref, slot_ref, own_ref, cap_ref, tgt_ref, val_ref, score_ref, out_ref, u_ref, w_ref, prob_ref
):
    blocks, lists, rows, cols = cap_ref.shape
    relations = u_ref.shape[1]
    ones = jnp.ones((lists * cols, cols), BF16)

    def body(b, carry):
        own = own_ref[b]
        target = jnp.dot(own, tgt_ref[0], preferred_element_type=F32)
        target += jnp.dot(own, tgt_ref[1], preferred_element_type=F32)
        target += jnp.dot(own, tgt_ref[2], preferred_element_type=F32)
        rels = [rel_ref[b, k] for k in range(lists)]
        slots = [slot_ref[b, k] for k in range(lists)]

        def spread(r, h):
            return jnp.broadcast_to(target[:, r * HEADS + h : r * HEADS + h + 1], (rows, cols))

        def finish(h):
            lanes = slice(h * cols, (h + 1) * cols)
            value = jnp.concatenate([val_ref[slots[k], rels[k], :, lanes] for k in range(lists)], axis=0)
            summed = jnp.dot(prob_ref[h], jnp.concatenate([value, ones], axis=1), preferred_element_type=F32)
            total = summed[:, cols:]
            mixed = summed[:, :cols] / total + own[:, lanes].astype(F32)
            out_ref[b, :, lanes] = jnp.where(mixed > 0, mixed, jnp.exp(jnp.minimum(mixed, 0.0)) - 1.0).astype(BF16)
            return total

        reach = [jnp.full((8, cols), -jnp.inf, F32) for _ in range(relations)]
        for k in range(lists):
            source = score_ref[slots[k]]
            for r in range(relations):
                reach[r] = jnp.maximum(reach[r], jnp.where(rels[k] == r, source, -jnp.inf))
        for h in range(HEADS):
            bound = jnp.full((rows, cols), -jnp.inf, F32)
            for r in range(relations):
                c = r * HEADS + h
                most = spread(r, h) + jnp.max(reach[r][c : c + 1, :], axis=1, keepdims=True)
                bound = jnp.maximum(bound, jnp.maximum(most, 0.2 * most))
            for r in range(relations):
                u_ref[h, r] = spread(r, h) - bound
                w_ref[h, r] = 0.2 * spread(r, h) - bound
        least = jnp.full((rows, cols), jnp.inf, F32)
        for h in range(HEADS):
            for k in range(lists):
                source = score_ref[slots[k], pl.ds(rels[k] * HEADS + h, 1), :]
                logit = jnp.maximum(u_ref[h, rels[k]] + source, w_ref[h, rels[k]] + 0.2 * source)
                prob = jnp.exp2(logit).astype(BF16)
                prob_ref[h, :, k * cols : (k + 1) * cols] = jnp.minimum(prob, cap_ref[b, k])
        for h in range(HEADS):
            least = jnp.minimum(least, finish(h))

        @pl.when(jnp.logical_not(jnp.min(least) > 2.0**-90))
        def _():
            for h in range(HEADS):
                for r in range(relations):
                    u_ref[h, r] = spread(r, h)

                def raw(k):
                    r, slot = rel_ref[b, k], slot_ref[b, k]
                    x = u_ref[h, r] + score_ref[slot, pl.ds(r * HEADS + h, 1), :]
                    return jnp.where(cap_ref[b, k].astype(F32) > 0, jnp.maximum(x, 0.2 * x), -jnp.inf)

                w_ref[h, 0] = jnp.full((rows, cols), -jnp.inf, F32)

                def climb(k, carry):
                    w_ref[h, 0] = jnp.maximum(w_ref[h, 0], raw(k))
                    return carry

                lax.fori_loop(0, lists, climb, 0)
                w_ref[h, 0] = jnp.broadcast_to(jnp.max(w_ref[h, 0], axis=1, keepdims=True), (rows, cols))

                def weigh(k, carry):
                    at = pl.ds(pl.multiple_of(k * cols, cols), cols)
                    prob_ref[h, :, at] = jnp.exp2(raw(k) - w_ref[h, 0]).astype(BF16)
                    return carry

                lax.fori_loop(0, lists, weigh, 0)
                finish(h)

        return carry

    lax.fori_loop(0, blocks, body, 0)


def attend(hidden, cap, relation_ids, source_slots, values, scores, tgt_vectors):
    blocks, lists, rows, cols = cap.shape
    width = hidden.shape[1]
    relations = values.shape[1]
    scalars, inside = pl.BlockSpec(memory_space=pltpu.SMEM), pl.BlockSpec(memory_space=pltpu.VMEM)
    return pl.pallas_call(
        attend_kernel,
        in_specs=[scalars] * 2 + [inside] * 5,
        out_specs=inside,
        scratch_shapes=[
            pltpu.VMEM((HEADS, relations, rows, cols), F32),
            pltpu.VMEM((HEADS, relations, rows, cols), F32),
            pltpu.VMEM((HEADS, rows, lists * cols), BF16),
        ],
        out_shape=jax.ShapeDtypeStruct((blocks, rows, width), BF16),
        compiler_params=pltpu.CompilerParams(vmem_limit_bytes=24 * 1024 * 1024),
        name="attend",
    )(relation_ids, source_slots, hidden.reshape(blocks, rows, width), cap, tgt_vectors, values, scores).reshape(
        blocks * rows, width
    )


def score_vectors(relation_weight, att_source, att_target):
    relations, width = att_source.shape
    head_width = width // HEADS
    split = att_source.reshape(relations, HEADS, head_width)
    moved = jnp.einsum(
        "rche,rhe->rhc",
        relation_weight.astype(F32).reshape(relations, width, HEADS, head_width),
        split,
        precision=lax.Precision.HIGHEST,
        preferred_element_type=F32,
    ).reshape(relations * HEADS, width)
    src = jnp.concatenate(three_parts(moved * LOG2E) + (jnp.zeros((8, width), BF16),), axis=0)
    own_head = (jnp.arange(width)[:, None] // head_width) == (jnp.arange(relations * HEADS)[None, :] % HEADS)
    spread = jnp.repeat(att_target.T, HEADS, axis=1)
    tgt = jnp.where(own_head, spread, 0.0) * LOG2E
    tgt = jnp.pad(tgt, ((0, 0), (0, 128 - relations * HEADS)))
    return src, jnp.stack(three_parts(tgt))


def shards(
    node_features,
    proj_weight,
    relation_weight,
    att_source,
    att_target,
    edge_mask,
    relation_ids,
    send_blocks,
    source_slots,
):
    block_rows = edge_mask.shape[-1]
    local_blocks = edge_mask.shape[0]
    rows_local = local_blocks * block_rows
    depth, width = proj_weight.shape
    n_feat = lax.axis_size("feat")
    n_graph = lax.axis_size("graph")
    levels = n_graph // 2
    place = lax.axis_index("graph")
    core, level = lax.rem(place, 2), place // 2

    def send(x, up, cores=0):
        pairs = [(p, (p + 2 * up) % n_graph ^ cores) for p in range(n_graph)]
        return lax.ppermute(x, "graph", pairs)

    cut = local_blocks // 2 + 1
    rows_a, half = cut * block_rows, width // 2
    features = node_features.T
    first = arrange(features, proj_weight, core, n_feat, 0, rows_a, half)
    first, features, send_blocks = lax.optimization_barrier((first, features, send_blocks))
    got = lax.all_to_all(first, "feat", 0, 0, tiled=True).reshape(n_feat * depth, rows_a + half)
    outgoing = arrange(features, proj_weight, core, n_feat, rows_a, rows_local, 0)

    tables = jnp.stack([send_blocks[0]] + [send(send_blocks[0], d) for d in range(1, levels)])
    tables = jnp.stack([tables, send(tables, 0, 1)], axis=1)
    order = jnp.array([0, 1, 3, 2])
    index = tables[order, :, place].reshape(n_graph, CAP)
    peer = source_slots // CAP
    distance = (level - peer // 2 + levels) % levels
    slots = (2 * (distance ^ (distance >> 1)) + (peer % 2 ^ core)) * CAP + source_slots % CAP
    src_vectors, tgt_vectors = score_vectors(relation_weight, att_source, att_target)

    got, outgoing, cap, src_vectors, tgt_vectors, slots, index = lax.optimization_barrier(
        (got, outgoing, caps(edge_mask), src_vectors, tgt_vectors, slots, index)
    )
    mine = got[:, rows_a:]
    other = send(mine, 0, 1)
    whole = jnp.where(core == 0, jnp.concatenate([mine, other], axis=1), jnp.concatenate([other, mine], axis=1))

    def project(x):
        return lax.dot_general(x, whole, (((0,), (0,)), ((), ())), preferred_element_type=F32).astype(BF16)

    def both(pieces):
        return [pieces, [(send(x, 0, 1), low, high) for x, low, high in pieces]]

    def spread(group, first, kept):
        return transform(group, first, index, relation_weight, src_vectors, block_rows, *kept)

    def ring(part):
        return send(part, 1), send(part, -1)

    def forward(up, down, middle):
        return send(up[: middle * block_rows], 1), send(down[middle * block_rows :], -1)

    a = project(got[:, :rows_a])
    up_a, down_a = ring(a)
    swap_a = send(a, 0, 1)
    outgoing, swap_a = lax.optimization_barrier((outgoing, swap_a))
    later = lax.all_to_all(outgoing, "feat", 0, 0, tiled=True).reshape(n_feat * depth, rows_local - rows_a)
    middle_a = (cut + 1) // 2
    middle_b = local_blocks // 2 - middle_a
    later, up_a, down_a = lax.optimization_barrier((later, up_a, down_a))
    far_a = forward(up_a, down_a, middle_a)
    b = project(later)
    up_b, down_b = ring(b)
    own = [[(a, 0, cut), (b, cut, local_blocks)], [(swap_a, 0, cut), (send(b, 0, 1), cut, local_blocks)]]
    done = spread(own, 0, (None, None))
    up_b, down_b, far_a, done = lax.optimization_barrier((up_b, down_b, far_a, done))
    far_b = forward(up_b, down_b, middle_b)
    done = spread(
        both([(up_a, 0, cut), (up_b, cut, local_blocks)]) + both([(down_a, 0, cut), (down_b, cut, local_blocks)]), 2, done
    )
    far_b, done = lax.optimization_barrier((far_b, done))
    ends = (0, middle_a, cut, cut + middle_b, local_blocks)
    far = list(zip(far_a + far_b, ends[:-1], ends[1:]))
    values, scores = spread(both(far), 6, done)
    return attend(jnp.concatenate([a, b]), cap, relation_ids, slots, values, scores, tgt_vectors)


def solution(mesh):
    placed = (
        P("graph", "feat"),
        P("feat", None),
        P(),
        P(),
        P(),
        P(("graph", "feat"), None, None, None),
        P(("graph", "feat"), None),
        P(("graph", "feat"), None, None),
        P(("graph", "feat"), None),
    )
    return jax.shard_map(
        shards, mesh=mesh, in_specs=placed, out_specs=P(("graph", "feat"), None), check_vma=False
    )
```

```python
import functools

import jax
import jax.numpy as jnp
from jax import lax
from jax.experimental import pallas as pl
from jax.experimental.pallas import tpu as pltpu
from jax.sharding import PartitionSpec as P

HEADS = 4
CAP = 4
LOG2E = 1.4426950408889634
F32 = jnp.float32
BF16 = jnp.bfloat16


def arrange_kernel(low, high, core_ref, x_ref, w_ref, out_ref):
    peers, _, columns = out_ref.shape
    total = x_ref.shape[1] // peers
    rows = high - low
    for q in range(peers):
        out_ref[q, :, :rows] = x_ref[:, q * total + low : q * total + high]
        if columns > rows:
            out_ref[q, :, rows:] = w_ref[...]


def arrange(features, weight, core, peers, low, high, half):
    depth, columns = features.shape
    rows = columns // peers
    step = 4
    return pl.pallas_call(
        functools.partial(arrange_kernel, low, high),
        grid_spec=pltpu.PrefetchScalarGridSpec(
            num_scalar_prefetch=1,
            grid=(peers // step,),
            in_specs=[
                pl.BlockSpec((depth, step * rows), lambda i, core_ref: (0, i)),
                pl.BlockSpec((depth, weight.shape[1] // 2), lambda i, core_ref: (0, core_ref[0])),
            ],
            out_specs=pl.BlockSpec((step, depth, high - low + half), lambda i, core_ref: (i, 0, 0)),
        ),
        out_shape=jax.ShapeDtypeStruct((peers, depth, high - low + half), BF16),
        name="arrange",
    )(core.reshape(1), features, weight)


def three_parts(x):
    hi = lax.reduce_precision(x, 8, 7)
    rest = x - hi
    mid = lax.reduce_precision(rest, 8, 7)
    return hi.astype(BF16), mid.astype(BF16), (rest - mid).astype(BF16)


def transform_kernel(bounds, first, idx_ref, *refs):
    n_pieces = sum(len(p) for p in bounds)
    pieces = refs[:n_pieces]
    rw_ref, src_ref = refs[n_pieces : n_pieces + 2]
    val_ref, score_ref, hid_ref, sem = refs[-4:]
    relations, block = val_ref.shape[1:3]
    cap = sem.shape[1]

    def copy(piece, row, source, c):
        return pltpu.make_async_copy(
            piece.at[pl.ds(row, block)], hid_ref.at[source, pl.ds(c * block, block)], sem.at[source, c]
        )

    begin = 0
    for source in range(len(bounds)):
        for c in range(cap):
            wanted = idx_ref[first + source, c]
            for n, (low, high) in enumerate(bounds[source]):

                @pl.when((wanted >= low) & (wanted < high))
                def _():
                    copy(pieces[begin + n], pl.multiple_of((wanted - low) * block, block), source, c).start()

        begin += len(bounds[source])
    for source in range(len(bounds)):
        for c in range(cap):
            copy(pieces[0], 0, source, c).wait()
        hid = hid_ref[source]
        at = (first + source) * cap
        for r in range(relations):
            moved = jnp.dot(hid, rw_ref[r], preferred_element_type=F32).astype(BF16)
            for c in range(cap):
                val_ref[at + c, r] = moved[c * block : (c + 1) * block]
        raw = lax.dot_general(src_ref[...], hid, (((1,), (1,)), ((), ())), preferred_element_type=F32)
        score = raw[0:8] + raw[8:16] + raw[16:24]
        for c in range(cap):
            score_ref[at + c] = score[:, c * block : (c + 1) * block]

def transform(sources, first, index, relation_weight, src_vectors, block, values, scores):
    bounds = tuple(tuple((low, high) for _, low, high in pieces) for pieces in sources)
    arrays = [array for pieces in sources for array, _, _ in pieces]
    peers, cap = index.shape
    relations, width = relation_weight.shape[:2]
    anywhere, inside = pl.BlockSpec(memory_space=pl.ANY), pl.BlockSpec(memory_space=pltpu.VMEM)
    kept = () if values is None else (values, scores)
    at = 1 + len(arrays) + 2
    return pl.pallas_call(
        functools.partial(transform_kernel, bounds, first),
        in_specs=[pl.BlockSpec(memory_space=pltpu.SMEM)] + [anywhere] * len(arrays) + [inside] * (2 + len(kept)),
        out_specs=[inside, inside],
        scratch_shapes=[
            pltpu.VMEM((len(bounds), cap * block, width), BF16),
            pltpu.SemaphoreType.DMA((len(bounds), cap)),
        ],
        out_shape=[
            jax.ShapeDtypeStruct((peers * cap, relations, block, width), BF16),
            jax.ShapeDtypeStruct((peers * cap, 8, block), F32),
        ],
        input_output_aliases={at + n: n for n in range(len(kept))},
        compiler_params=pltpu.CompilerParams(vmem_limit_bytes=24 * 1024 * 1024),
        name="transform",
    )(index, *arrays, relation_weight, src_vectors, *kept)


def cap_kernel(mask_ref, cap_ref):
    cap_ref[...] = jnp.where(mask_ref[...] > 0, jnp.inf, 0.0).astype(BF16)


def caps(edge_mask):
    shape = edge_mask.shape
    spec = pl.BlockSpec((1,) + shape[1:], lambda b: (b, 0, 0, 0))
    return pl.pallas_call(
        cap_kernel,
        grid=shape[:1],
        in_specs=[spec],
        out_specs=spec,
        out_shape=jax.ShapeDtypeStruct(shape, BF16),
        name="caps",
    )(edge_mask)


def attend_kernel(
    rel_ref, slot_ref, own_ref, cap_ref, tgt_ref, val_ref, score_ref, out_ref, u_ref, w_ref, prob_ref
):
    blocks, lists, rows, cols = cap_ref.shape
    relations = u_ref.shape[1]
    ones = jnp.ones((lists * cols, cols), BF16)

    def body(b, carry):
        own = own_ref[b]
        target = jnp.dot(own, tgt_ref[0], preferred_element_type=F32)
        target += jnp.dot(own, tgt_ref[1], preferred_element_type=F32)
        target += jnp.dot(own, tgt_ref[2], preferred_element_type=F32)
        rels = [rel_ref[b, k] for k in range(lists)]
        slots = [slot_ref[b, k] for k in range(lists)]

        def spread(r, h):
            return jnp.broadcast_to(target[:, r * HEADS + h : r * HEADS + h + 1], (rows, cols))

        def finish(h):
            lanes = slice(h * cols, (h + 1) * cols)
            value = jnp.concatenate([val_ref[slots[k], rels[k], :, lanes] for k in range(lists)], axis=0)
            summed = jnp.dot(prob_ref[h], jnp.concatenate([value, ones], axis=1), preferred_element_type=F32)
            total = summed[:, cols:]
            mixed = summed[:, :cols] / total + own[:, lanes].astype(F32)
            out_ref[b, :, lanes] = jnp.where(mixed > 0, mixed, jnp.exp(jnp.minimum(mixed, 0.0)) - 1.0).astype(BF16)
            return total

        reach = [jnp.full((8, cols), -jnp.inf, F32) for _ in range(relations)]
        for k in range(lists):
            source = score_ref[slots[k]]
            for r in range(relations):
                reach[r] = jnp.maximum(reach[r], jnp.where(rels[k] == r, source, -jnp.inf))
        for h in range(HEADS):
            bound = jnp.full((rows, cols), -jnp.inf, F32)
            for r in range(relations):
                c = r * HEADS + h
                most = spread(r, h) + jnp.max(reach[r][c : c + 1, :], axis=1, keepdims=True)
                bound = jnp.maximum(bound, jnp.maximum(most, 0.2 * most))
            for r in range(relations):
                u_ref[h, r] = spread(r, h) - bound
                w_ref[h, r] = 0.2 * spread(r, h) - bound
        least = jnp.full((rows, cols), jnp.inf, F32)
        for h in range(HEADS):
            for k in range(lists):
                source = score_ref[slots[k], pl.ds(rels[k] * HEADS + h, 1), :]
                logit = jnp.maximum(u_ref[h, rels[k]] + source, w_ref[h, rels[k]] + 0.2 * source)
                prob = jnp.exp2(logit).astype(BF16)
                prob_ref[h, :, k * cols : (k + 1) * cols] = jnp.minimum(prob, cap_ref[b, k])
        for h in range(HEADS):
            least = jnp.minimum(least, finish(h))

        @pl.when(jnp.logical_not(jnp.min(least) > 2.0**-90))
        def _():
            for h in range(HEADS):
                for r in range(relations):
                    u_ref[h, r] = spread(r, h)

                def raw(k):
                    r, slot = rel_ref[b, k], slot_ref[b, k]
                    x = u_ref[h, r] + score_ref[slot, pl.ds(r * HEADS + h, 1), :]
                    return jnp.where(cap_ref[b, k].astype(F32) > 0, jnp.maximum(x, 0.2 * x), -jnp.inf)

                w_ref[h, 0] = jnp.full((rows, cols), -jnp.inf, F32)

                def climb(k, carry):
                    w_ref[h, 0] = jnp.maximum(w_ref[h, 0], raw(k))
                    return carry

                lax.fori_loop(0, lists, climb, 0)
                w_ref[h, 0] = jnp.broadcast_to(jnp.max(w_ref[h, 0], axis=1, keepdims=True), (rows, cols))

                def weigh(k, carry):
                    at = pl.ds(pl.multiple_of(k * cols, cols), cols)
                    prob_ref[h, :, at] = jnp.exp2(raw(k) - w_ref[h, 0]).astype(BF16)
                    return carry

                lax.fori_loop(0, lists, weigh, 0)
                finish(h)

        return carry

    lax.fori_loop(0, blocks, body, 0)


def attend(hidden, cap, relation_ids, source_slots, values, scores, tgt_vectors):
    blocks, lists, rows, cols = cap.shape
    width = hidden.shape[1]
    relations = values.shape[1]
    scalars, inside = pl.BlockSpec(memory_space=pltpu.SMEM), pl.BlockSpec(memory_space=pltpu.VMEM)
    return pl.pallas_call(
        attend_kernel,
        in_specs=[scalars] * 2 + [inside] * 5,
        out_specs=inside,
        scratch_shapes=[
            pltpu.VMEM((HEADS, relations, rows, cols), F32),
            pltpu.VMEM((HEADS, relations, rows, cols), F32),
            pltpu.VMEM((HEADS, rows, lists * cols), BF16),
        ],
        out_shape=jax.ShapeDtypeStruct((blocks, rows, width), BF16),
        compiler_params=pltpu.CompilerParams(vmem_limit_bytes=24 * 1024 * 1024),
        name="attend",
    )(relation_ids, source_slots, hidden.reshape(blocks, rows, width), cap, tgt_vectors, values, scores).reshape(
        blocks * rows, width
    )


def score_vectors(relation_weight, att_source, att_target):
    relations, width = att_source.shape
    head_width = width // HEADS
    split = att_source.reshape(relations, HEADS, head_width)
    moved = jnp.einsum(
        "rche,rhe->rhc",
        relation_weight.astype(F32).reshape(relations, width, HEADS, head_width),
        split,
        precision=lax.Precision.HIGHEST,
        preferred_element_type=F32,
    ).reshape(relations * HEADS, width)
    src = jnp.concatenate(three_parts(moved * LOG2E) + (jnp.zeros((8, width), BF16),), axis=0)
    own_head = (jnp.arange(width)[:, None] // head_width) == (jnp.arange(relations * HEADS)[None, :] % HEADS)
    spread = jnp.repeat(att_target.T, HEADS, axis=1)
    tgt = jnp.where(own_head, spread, 0.0) * LOG2E
    tgt = jnp.pad(tgt, ((0, 0), (0, 128 - relations * HEADS)))
    return src, jnp.stack(three_parts(tgt))


def shards(
    node_features,
    proj_weight,
    relation_weight,
    att_source,
    att_target,
    edge_mask,
    relation_ids,
    send_blocks,
    source_slots,
):
    block_rows = edge_mask.shape[-1]
    local_blocks = edge_mask.shape[0]
    rows_local = local_blocks * block_rows
    depth, width = proj_weight.shape
    n_feat = lax.axis_size("feat")
    n_graph = lax.axis_size("graph")
    levels = n_graph // 2
    place = lax.axis_index("graph")
    core, level = lax.rem(place, 2), place // 2

    def send(x, up, cores=0):
        pairs = [(p, (p + 2 * up) % n_graph ^ cores) for p in range(n_graph)]
        return lax.ppermute(x, "graph", pairs)

    cut = local_blocks // 2
    rows_a, half = cut * block_rows, width // 2
    features = node_features.T
    first = arrange(features, proj_weight, core, n_feat, 0, rows_a, half)
    first, features = lax.optimization_barrier((first, features))
    got = lax.all_to_all(first, "feat", 0, 0, tiled=True).reshape(n_feat * depth, rows_a + half)
    outgoing = arrange(features, proj_weight, core, n_feat, rows_a, rows_local, 0)

    table = jnp.broadcast_to(send_blocks.astype(BF16).reshape(1, n_graph * CAP, 1), (depth, n_graph * CAP, 16))
    tables = lax.all_gather(table.reshape(depth, n_graph * CAP * 16), "graph")
    tables = tables[:, 0].reshape(n_graph, n_graph, CAP, 16)[:, :, :, 0]
    steps = jnp.arange(n_graph) // 2
    sender = 2 * ((level - (steps ^ (steps >> 1)) + levels) % levels) + (jnp.arange(n_graph) % 2 ^ core)
    index = tables[sender, place].astype(jnp.int32)
    peer = source_slots // CAP
    distance = (level - peer // 2 + levels) % levels
    slots = (2 * (distance ^ (distance >> 1)) + (peer % 2 ^ core)) * CAP + source_slots % CAP
    src_vectors, tgt_vectors = score_vectors(relation_weight, att_source, att_target)

    got, outgoing, cap, src_vectors, tgt_vectors, slots = lax.optimization_barrier(
        (got, outgoing, caps(edge_mask), src_vectors, tgt_vectors, slots)
    )
    later = lax.all_to_all(outgoing, "feat", 0, 0, tiled=True).reshape(n_feat * depth, rows_local - rows_a)

    mine = got[:, rows_a:]
    other = send(mine, 0, 1)
    whole = jnp.where(core == 0, jnp.concatenate([mine, other], axis=1), jnp.concatenate([other, mine], axis=1))

    def project(x):
        return lax.dot_general(x, whole, (((0,), (0,)), ((), ())), preferred_element_type=F32).astype(BF16)

    def both(pieces):
        return [pieces, [(send(x, 0, 1), low, high) for x, low, high in pieces]]

    def spread(group, first, kept):
        return transform(group, first, index, relation_weight, src_vectors, block_rows, *kept)

    def ring(part):
        return send(part, 1), send(part, -1)

    def forward(up, down):
        middle = up.shape[0] // 2
        return send(up[:middle], 1), send(down[middle:], -1)

    a = project(got[:, :rows_a])
    up_a, down_a = ring(a)
    later, up_a, down_a = lax.optimization_barrier((later, up_a, down_a))
    far_a = forward(up_a, down_a)
    b = project(later)
    up_b, down_b = ring(b)
    done = spread(both([(a, 0, cut), (b, cut, local_blocks)]), 0, (None, None))
    up_b, down_b, far_a, done = lax.optimization_barrier((up_b, down_b, far_a, done))
    far_b = forward(up_b, down_b)
    done = spread(
        both([(up_a, 0, cut), (up_b, cut, local_blocks)]) + both([(down_a, 0, cut), (down_b, cut, local_blocks)]), 2, done
    )
    far_b, done = lax.optimization_barrier((far_b, done))
    quarter = cut // 2
    far = [(x, n * quarter, (n + 1) * quarter) for n, x in enumerate(far_a + far_b)]
    values, scores = spread(both(far), 6, done)
    return attend(jnp.concatenate([a, b]), cap, relation_ids, slots, values, scores, tgt_vectors)


def solution(mesh):
    placed = (
        P("graph", "feat"),
        P("feat", None),
        P(),
        P(),
        P(),
        P(("graph", "feat"), None, None, None),
        P(("graph", "feat"), None),
        P(("graph", "feat"), None, None),
        P(("graph", "feat"), None),
    )
    return jax.shard_map(
        shards, mesh=mesh, in_specs=placed, out_specs=P(("graph", "feat"), None), check_vma=False
    )
```

```python
import functools

import jax
import jax.numpy as jnp
from jax import lax
from jax.experimental import pallas as pl
from jax.experimental.pallas import tpu as pltpu
from jax.sharding import PartitionSpec as P

HEADS = 4
CAP = 4
LOG2E = 1.4426950408889634
F32 = jnp.float32
BF16 = jnp.bfloat16


def arrange_kernel(low, high, core_ref, x_ref, w_ref, out_ref):
    peers, _, columns = out_ref.shape
    total = x_ref.shape[1] // peers
    rows = high - low
    for q in range(peers):
        out_ref[q, :, :rows] = x_ref[:, q * total + low : q * total + high]
        if columns > rows:
            out_ref[q, :, rows:] = w_ref[...]


def arrange(features, weight, core, peers, low, high, half):
    depth, columns = features.shape
    rows = columns // peers
    step = 4
    return pl.pallas_call(
        functools.partial(arrange_kernel, low, high),
        grid_spec=pltpu.PrefetchScalarGridSpec(
            num_scalar_prefetch=1,
            grid=(peers // step,),
            in_specs=[
                pl.BlockSpec((depth, step * rows), lambda i, core_ref: (0, i)),
                pl.BlockSpec((depth, weight.shape[1] // 2), lambda i, core_ref: (0, core_ref[0])),
            ],
            out_specs=pl.BlockSpec((step, depth, high - low + half), lambda i, core_ref: (i, 0, 0)),
        ),
        out_shape=jax.ShapeDtypeStruct((peers, depth, high - low + half), BF16),
        name="arrange",
    )(core.reshape(1), features, weight)


def three_parts(x):
    hi = lax.reduce_precision(x, 8, 7)
    rest = x - hi
    mid = lax.reduce_precision(rest, 8, 7)
    return hi.astype(BF16), mid.astype(BF16), (rest - mid).astype(BF16)


def transform_kernel(bounds, first, *refs):
    index, refs = refs[: len(bounds) // 2], refs[len(bounds) // 2 :]
    n_pieces = sum(len(p) for p in bounds)
    pieces = refs[:n_pieces]
    rw_ref, src_ref = refs[n_pieces : n_pieces + 2]
    val_ref, score_ref, hid_ref, sem = refs[-4:]
    relations, block = val_ref.shape[1:3]
    cap = sem.shape[1]

    def copy(piece, row, source, c):
        return pltpu.make_async_copy(
            piece.at[pl.ds(row, block)], hid_ref.at[source, pl.ds(c * block, block)], sem.at[source, c]
        )

    begin = 0
    for source in range(len(bounds)):
        for c in range(cap):
            wanted = index[source // 2][source % 2, c]
            for n, (low, high) in enumerate(bounds[source]):

                @pl.when((wanted >= low) & (wanted < high))
                def _():
                    copy(pieces[begin + n], pl.multiple_of((wanted - low) * block, block), source, c).start()

        begin += len(bounds[source])
    for source in range(len(bounds)):
        for c in range(cap):
            copy(pieces[0], 0, source, c).wait()
        hid = hid_ref[source]
        at = (first + source) * cap
        for r in range(relations):
            moved = jnp.dot(hid, rw_ref[r], preferred_element_type=F32).astype(BF16)
            for c in range(cap):
                val_ref[at + c, r] = moved[c * block : (c + 1) * block]
        raw = lax.dot_general(src_ref[...], hid, (((1,), (1,)), ((), ())), preferred_element_type=F32)
        score = raw[0:8] + raw[8:16] + raw[16:24]
        for c in range(cap):
            score_ref[at + c] = score[:, c * block : (c + 1) * block]

def transform(sources, peers, first, index, relation_weight, src_vectors, block, values, scores):
    bounds = tuple(tuple((low, high) for _, low, high in pieces) for pieces in sources)
    arrays = [array for pieces in sources for array, _, _ in pieces]
    cap = index[0].shape[1]
    relations, width = relation_weight.shape[:2]
    anywhere, inside = pl.BlockSpec(memory_space=pl.ANY), pl.BlockSpec(memory_space=pltpu.VMEM)
    kept = () if values is None else (values, scores)
    at = len(index) + len(arrays) + 2
    return pl.pallas_call(
        functools.partial(transform_kernel, bounds, first),
        in_specs=[pl.BlockSpec(memory_space=pltpu.SMEM)] * len(index) + [anywhere] * len(arrays) + [inside] * (2 + len(kept)),
        out_specs=[inside, inside],
        scratch_shapes=[
            pltpu.VMEM((len(bounds), cap * block, width), BF16),
            pltpu.SemaphoreType.DMA((len(bounds), cap)),
        ],
        out_shape=[
            jax.ShapeDtypeStruct((peers * cap, relations, block, width), BF16),
            jax.ShapeDtypeStruct((peers * cap, 8, block), F32),
        ],
        input_output_aliases={at + n: n for n in range(len(kept))},
        compiler_params=pltpu.CompilerParams(vmem_limit_bytes=24 * 1024 * 1024),
        name="transform",
    )(*index, *arrays, relation_weight, src_vectors, *kept)


def cap_kernel(mask_ref, cap_ref):
    cap_ref[...] = jnp.where(mask_ref[...] > 0, jnp.inf, 0.0).astype(BF16)


def caps(edge_mask):
    shape = edge_mask.shape
    spec = pl.BlockSpec((1,) + shape[1:], lambda b: (b, 0, 0, 0))
    return pl.pallas_call(
        cap_kernel,
        grid=shape[:1],
        in_specs=[spec],
        out_specs=spec,
        out_shape=jax.ShapeDtypeStruct(shape, BF16),
        name="caps",
    )(edge_mask)


def attend_kernel(
    rel_ref, slot_ref, own_ref, cap_ref, tgt_ref, val_ref, score_ref, out_ref, u_ref, w_ref, prob_ref
):
    blocks, lists, rows, cols = cap_ref.shape
    relations = u_ref.shape[1]
    ones = jnp.ones((lists * cols, cols), BF16)

    def body(b, carry):
        own = own_ref[b]
        target = jnp.dot(own, tgt_ref[0], preferred_element_type=F32)
        target += jnp.dot(own, tgt_ref[1], preferred_element_type=F32)
        target += jnp.dot(own, tgt_ref[2], preferred_element_type=F32)
        rels = [rel_ref[b, k] for k in range(lists)]
        slots = [slot_ref[b, k] for k in range(lists)]

        def spread(r, h):
            return jnp.broadcast_to(target[:, r * HEADS + h : r * HEADS + h + 1], (rows, cols))

        def finish(h):
            lanes = slice(h * cols, (h + 1) * cols)
            value = jnp.concatenate([val_ref[slots[k], rels[k], :, lanes] for k in range(lists)], axis=0)
            summed = jnp.dot(prob_ref[h], jnp.concatenate([value, ones], axis=1), preferred_element_type=F32)
            total = summed[:, cols:]
            mixed = summed[:, :cols] / total + own[:, lanes].astype(F32)
            out_ref[b, :, lanes] = jnp.where(mixed > 0, mixed, jnp.exp(jnp.minimum(mixed, 0.0)) - 1.0).astype(BF16)
            return total

        reach = [jnp.full((8, cols), -jnp.inf, F32) for _ in range(relations)]
        for k in range(lists):
            source = score_ref[slots[k]]
            for r in range(relations):
                reach[r] = jnp.maximum(reach[r], jnp.where(rels[k] == r, source, -jnp.inf))
        for h in range(HEADS):
            bound = jnp.full((rows, cols), -jnp.inf, F32)
            for r in range(relations):
                c = r * HEADS + h
                most = spread(r, h) + jnp.max(reach[r][c : c + 1, :], axis=1, keepdims=True)
                bound = jnp.maximum(bound, jnp.maximum(most, 0.2 * most))
            for r in range(relations):
                u_ref[h, r] = spread(r, h) - bound
                w_ref[h, r] = 0.2 * spread(r, h) - bound
        least = jnp.full((rows, cols), jnp.inf, F32)
        for h in range(HEADS):
            for k in range(lists):
                source = score_ref[slots[k], pl.ds(rels[k] * HEADS + h, 1), :]
                logit = jnp.maximum(u_ref[h, rels[k]] + source, w_ref[h, rels[k]] + 0.2 * source)
                prob = jnp.exp2(logit).astype(BF16)
                prob_ref[h, :, k * cols : (k + 1) * cols] = jnp.minimum(prob, cap_ref[b, k])
        for h in range(HEADS):
            least = jnp.minimum(least, finish(h))

        @pl.when(jnp.logical_not(jnp.min(least) > 2.0**-90))
        def _():
            for h in range(HEADS):
                for r in range(relations):
                    u_ref[h, r] = spread(r, h)

                def raw(k):
                    r, slot = rel_ref[b, k], slot_ref[b, k]
                    x = u_ref[h, r] + score_ref[slot, pl.ds(r * HEADS + h, 1), :]
                    return jnp.where(cap_ref[b, k].astype(F32) > 0, jnp.maximum(x, 0.2 * x), -jnp.inf)

                w_ref[h, 0] = jnp.full((rows, cols), -jnp.inf, F32)

                def climb(k, carry):
                    w_ref[h, 0] = jnp.maximum(w_ref[h, 0], raw(k))
                    return carry

                lax.fori_loop(0, lists, climb, 0)
                w_ref[h, 0] = jnp.broadcast_to(jnp.max(w_ref[h, 0], axis=1, keepdims=True), (rows, cols))

                def weigh(k, carry):
                    at = pl.ds(pl.multiple_of(k * cols, cols), cols)
                    prob_ref[h, :, at] = jnp.exp2(raw(k) - w_ref[h, 0]).astype(BF16)
                    return carry

                lax.fori_loop(0, lists, weigh, 0)
                finish(h)

        return carry

    lax.fori_loop(0, blocks, body, 0)


def attend(hidden, cap, relation_ids, source_slots, values, scores, tgt_vectors):
    blocks, lists, rows, cols = cap.shape
    width = hidden.shape[1]
    relations = values.shape[1]
    scalars, inside = pl.BlockSpec(memory_space=pltpu.SMEM), pl.BlockSpec(memory_space=pltpu.VMEM)
    return pl.pallas_call(
        attend_kernel,
        in_specs=[scalars] * 2 + [inside] * 5,
        out_specs=inside,
        scratch_shapes=[
            pltpu.VMEM((HEADS, relations, rows, cols), F32),
            pltpu.VMEM((HEADS, relations, rows, cols), F32),
            pltpu.VMEM((HEADS, rows, lists * cols), BF16),
        ],
        out_shape=jax.ShapeDtypeStruct((blocks, rows, width), BF16),
        compiler_params=pltpu.CompilerParams(vmem_limit_bytes=24 * 1024 * 1024),
        name="attend",
    )(relation_ids, source_slots, hidden.reshape(blocks, rows, width), cap, tgt_vectors, values, scores).reshape(
        blocks * rows, width
    )


def score_vectors(relation_weight, att_source, att_target):
    relations, width = att_source.shape
    head_width = width // HEADS
    split = att_source.reshape(relations, HEADS, head_width)
    moved = jnp.einsum(
        "rche,rhe->rhc",
        relation_weight.astype(F32).reshape(relations, width, HEADS, head_width),
        split,
        precision=lax.Precision.HIGHEST,
        preferred_element_type=F32,
    ).reshape(relations * HEADS, width)
    src = jnp.concatenate(three_parts(moved * LOG2E) + (jnp.zeros((8, width), BF16),), axis=0)
    own_head = (jnp.arange(width)[:, None] // head_width) == (jnp.arange(relations * HEADS)[None, :] % HEADS)
    spread = jnp.repeat(att_target.T, HEADS, axis=1)
    tgt = jnp.where(own_head, spread, 0.0) * LOG2E
    tgt = jnp.pad(tgt, ((0, 0), (0, 128 - relations * HEADS)))
    return src, jnp.stack(three_parts(tgt))


def shards(
    node_features,
    proj_weight,
    relation_weight,
    att_source,
    att_target,
    edge_mask,
    relation_ids,
    send_blocks,
    source_slots,
):
    block_rows = edge_mask.shape[-1]
    local_blocks = edge_mask.shape[0]
    rows_local = local_blocks * block_rows
    depth, width = proj_weight.shape
    n_feat = lax.axis_size("feat")
    n_graph = lax.axis_size("graph")
    levels = n_graph // 2
    place = lax.axis_index("graph")
    core, level = lax.rem(place, 2), place // 2

    def send(x, up, cores=0):
        pairs = [(p, (p + 2 * up) % n_graph ^ cores) for p in range(n_graph)]
        return lax.ppermute(x, "graph", pairs)

    cut = local_blocks // 2
    rows_a, half = cut * block_rows, width // 2
    features = node_features.T
    first = arrange(features, proj_weight, core, n_feat, 0, rows_a, half)
    first, features, send_blocks = lax.optimization_barrier((first, features, send_blocks))
    got = lax.all_to_all(first, "feat", 0, 0, tiled=True).reshape(n_feat * depth, rows_a + half)
    outgoing = arrange(features, proj_weight, core, n_feat, rows_a, rows_local, 0)

    pair = jnp.stack([send_blocks[0], send(send_blocks[0], 0, 1)])
    lists = [pair[:, 2 * ((level + d) % levels) + core] for d in range(levels)]
    peer = source_slots // CAP
    distance = (level - peer // 2 + levels) % levels
    slots = (2 * (distance ^ (distance >> 1)) + (peer % 2 ^ core)) * CAP + source_slots % CAP
    src_vectors, tgt_vectors = score_vectors(relation_weight, att_source, att_target)

    got, outgoing, cap, src_vectors, tgt_vectors, slots, lists = lax.optimization_barrier(
        (got, outgoing, caps(edge_mask), src_vectors, tgt_vectors, slots, lists)
    )
    later = lax.all_to_all(outgoing, "feat", 0, 0, tiled=True).reshape(n_feat * depth, rows_local - rows_a)

    mine = got[:, rows_a:]
    other = send(mine, 0, 1)
    whole = jnp.where(core == 0, jnp.concatenate([mine, other], axis=1), jnp.concatenate([other, mine], axis=1))

    def project(x):
        return lax.dot_general(x, whole, (((0,), (0,)), ((), ())), preferred_element_type=F32).astype(BF16)

    def both(pieces):
        return [pieces, [(send(x, 0, 1), low, high) for x, low, high in pieces]]

    def spread(group, first, index, kept):
        return transform(group, n_graph, first, index, relation_weight, src_vectors, block_rows, *kept)

    def ring(part):
        return send(part, 1), send(part, -1)

    def forward(up, down):
        middle = up.shape[0] // 2
        return send(up[:middle], 1), send(down[middle:], -1)

    a = project(got[:, :rows_a])
    up_a, down_a = ring(a)
    later, up_a, down_a = lax.optimization_barrier((later, up_a, down_a))
    far_a = forward(up_a, down_a)
    b = project(later)
    up_b, down_b = ring(b)
    done = spread(both([(a, 0, cut), (b, cut, local_blocks)]), 0, lists[:1], (None, None))
    lists, done = lax.optimization_barrier((lists, done))
    lists = [send(lists[d], d) for d in range(1, levels)]
    up_b, down_b, far_a, lists, done = lax.optimization_barrier((up_b, down_b, far_a, lists, done))
    far_b = forward(up_b, down_b)
    done = spread(
        both([(up_a, 0, cut), (up_b, cut, local_blocks)]) + both([(down_a, 0, cut), (down_b, cut, local_blocks)]),
        2,
        (lists[0], lists[2]),
        done,
    )
    far_b, done = lax.optimization_barrier((far_b, done))
    quarter = cut // 2
    far = [(x, n * quarter, (n + 1) * quarter) for n, x in enumerate(far_a + far_b)]
    values, scores = spread(both(far), 6, lists[1:2], done)
    return attend(jnp.concatenate([a, b]), cap, relation_ids, slots, values, scores, tgt_vectors)


def solution(mesh):
    placed = (
        P("graph", "feat"),
        P("feat", None),
        P(),
        P(),
        P(),
        P(("graph", "feat"), None, None, None),
        P(("graph", "feat"), None),
        P(("graph", "feat"), None, None),
        P(("graph", "feat"), None),
    )
    return jax.shard_map(
        shards, mesh=mesh, in_specs=placed, out_specs=P(("graph", "feat"), None), check_vma=False
    )
```

```python
import functools

import jax
import jax.numpy as jnp
from jax import lax
from jax.experimental import pallas as pl
from jax.experimental.pallas import tpu as pltpu
from jax.sharding import PartitionSpec as P

HEADS = 4
CAP = 4
LOG2E = 1.4426950408889634
F32 = jnp.float32
BF16 = jnp.bfloat16


def arrange_kernel(low, high, core_ref, x_ref, w_ref, out_ref):
    peers, _, columns = out_ref.shape
    total = x_ref.shape[1] // peers
    rows = high - low
    for q in range(peers):
        out_ref[q, :, :rows] = x_ref[:, q * total + low : q * total + high]
        if columns > rows:
            out_ref[q, :, rows:] = w_ref[...]


def arrange(features, weight, core, peers, low, high, half):
    depth, columns = features.shape
    rows = columns // peers
    step = 4
    return pl.pallas_call(
        functools.partial(arrange_kernel, low, high),
        grid_spec=pltpu.PrefetchScalarGridSpec(
            num_scalar_prefetch=1,
            grid=(peers // step,),
            in_specs=[
                pl.BlockSpec((depth, step * rows), lambda i, core_ref: (0, i)),
                pl.BlockSpec((depth, weight.shape[1] // 2), lambda i, core_ref: (0, core_ref[0])),
            ],
            out_specs=pl.BlockSpec((step, depth, high - low + half), lambda i, core_ref: (i, 0, 0)),
        ),
        out_shape=jax.ShapeDtypeStruct((peers, depth, high - low + half), BF16),
        name="arrange",
    )(core.reshape(1), features, weight)


def three_parts(x):
    hi = lax.reduce_precision(x, 8, 7)
    rest = x - hi
    mid = lax.reduce_precision(rest, 8, 7)
    return hi.astype(BF16), mid.astype(BF16), (rest - mid).astype(BF16)


def transform_kernel(bounds, first, *refs):
    index, refs = refs[: len(bounds) // 2], refs[len(bounds) // 2 :]
    n_pieces = sum(len(p) for p in bounds)
    pieces = refs[:n_pieces]
    rw_ref, src_ref = refs[n_pieces : n_pieces + 2]
    val_ref, score_ref, hid_ref, sem = refs[-4:]
    relations, block = val_ref.shape[1:3]
    cap = sem.shape[1]

    def copy(piece, row, source, c):
        return pltpu.make_async_copy(
            piece.at[pl.ds(row, block)], hid_ref.at[source, pl.ds(c * block, block)], sem.at[source, c]
        )

    begin = 0
    for source in range(len(bounds)):
        for c in range(cap):
            wanted = index[source // 2][source % 2, c]
            for n, (low, high) in enumerate(bounds[source]):

                @pl.when((wanted >= low) & (wanted < high))
                def _():
                    copy(pieces[begin + n], pl.multiple_of((wanted - low) * block, block), source, c).start()

        begin += len(bounds[source])
    for source in range(len(bounds)):
        for c in range(cap):
            copy(pieces[0], 0, source, c).wait()
        hid = hid_ref[source]
        at = (first + source) * cap
        for r in range(relations):
            moved = jnp.dot(hid, rw_ref[r], preferred_element_type=F32).astype(BF16)
            for c in range(cap):
                val_ref[at + c, r] = moved[c * block : (c + 1) * block]
        raw = lax.dot_general(src_ref[...], hid, (((1,), (1,)), ((), ())), preferred_element_type=F32)
        score = raw[0:8] + raw[8:16] + raw[16:24]
        for c in range(cap):
            score_ref[at + c] = score[:, c * block : (c + 1) * block]

def transform(sources, peers, first, index, relation_weight, src_vectors, block, values, scores):
    bounds = tuple(tuple((low, high) for _, low, high in pieces) for pieces in sources)
    arrays = [array for pieces in sources for array, _, _ in pieces]
    cap = index[0].shape[1]
    relations, width = relation_weight.shape[:2]
    anywhere, inside = pl.BlockSpec(memory_space=pl.ANY), pl.BlockSpec(memory_space=pltpu.VMEM)
    kept = () if values is None else (values, scores)
    at = len(index) + len(arrays) + 2
    return pl.pallas_call(
        functools.partial(transform_kernel, bounds, first),
        in_specs=[pl.BlockSpec(memory_space=pltpu.SMEM)] * len(index) + [anywhere] * len(arrays) + [inside] * (2 + len(kept)),
        out_specs=[inside, inside],
        scratch_shapes=[
            pltpu.VMEM((len(bounds), cap * block, width), BF16),
            pltpu.SemaphoreType.DMA((len(bounds), cap)),
        ],
        out_shape=[
            jax.ShapeDtypeStruct((peers * cap, relations, block, width), BF16),
            jax.ShapeDtypeStruct((peers * cap, 8, block), F32),
        ],
        input_output_aliases={at + n: n for n in range(len(kept))},
        compiler_params=pltpu.CompilerParams(vmem_limit_bytes=24 * 1024 * 1024),
        name="transform",
    )(*index, *arrays, relation_weight, src_vectors, *kept)


def cap_kernel(mask_ref, cap_ref):
    cap_ref[...] = jnp.where(mask_ref[...] > 0, jnp.inf, 0.0).astype(BF16)


def caps(edge_mask):
    shape = edge_mask.shape
    spec = pl.BlockSpec((1,) + shape[1:], lambda b: (b, 0, 0, 0))
    return pl.pallas_call(
        cap_kernel,
        grid=shape[:1],
        in_specs=[spec],
        out_specs=spec,
        out_shape=jax.ShapeDtypeStruct(shape, BF16),
        name="caps",
    )(edge_mask)


def attend_kernel(
    rel_ref, slot_ref, own_ref, cap_ref, tgt_ref, val_ref, score_ref, out_ref, u_ref, w_ref, prob_ref
):
    blocks, lists, rows, cols = cap_ref.shape
    relations = u_ref.shape[1]
    ones = jnp.ones((lists * cols, cols), BF16)

    def body(b, carry):
        own = own_ref[b]
        target = jnp.dot(own, tgt_ref[0], preferred_element_type=F32)
        target += jnp.dot(own, tgt_ref[1], preferred_element_type=F32)
        target += jnp.dot(own, tgt_ref[2], preferred_element_type=F32)
        rels = [rel_ref[b, k] for k in range(lists)]
        slots = [slot_ref[b, k] for k in range(lists)]

        def spread(r, h):
            return jnp.broadcast_to(target[:, r * HEADS + h : r * HEADS + h + 1], (rows, cols))

        def finish(h):
            lanes = slice(h * cols, (h + 1) * cols)
            value = jnp.concatenate([val_ref[slots[k], rels[k], :, lanes] for k in range(lists)], axis=0)
            summed = jnp.dot(prob_ref[h], jnp.concatenate([value, ones], axis=1), preferred_element_type=F32)
            total = summed[:, cols:]
            mixed = summed[:, :cols] / total + own[:, lanes].astype(F32)
            out_ref[b, :, lanes] = jnp.where(mixed > 0, mixed, jnp.exp(jnp.minimum(mixed, 0.0)) - 1.0).astype(BF16)
            return total

        reach = [jnp.full((8, cols), -jnp.inf, F32) for _ in range(relations)]
        for k in range(lists):
            source = score_ref[slots[k]]
            for r in range(relations):
                reach[r] = jnp.maximum(reach[r], jnp.where(rels[k] == r, source, -jnp.inf))
        for h in range(HEADS):
            bound = jnp.full((rows, cols), -jnp.inf, F32)
            for r in range(relations):
                c = r * HEADS + h
                most = spread(r, h) + jnp.max(reach[r][c : c + 1, :], axis=1, keepdims=True)
                bound = jnp.maximum(bound, jnp.maximum(most, 0.2 * most))
            for r in range(relations):
                u_ref[h, r] = spread(r, h) - bound
                w_ref[h, r] = 0.2 * spread(r, h) - bound
        least = jnp.full((rows, cols), jnp.inf, F32)
        for h in range(HEADS):
            for k in range(lists):
                source = score_ref[slots[k], pl.ds(rels[k] * HEADS + h, 1), :]
                logit = jnp.maximum(u_ref[h, rels[k]] + source, w_ref[h, rels[k]] + 0.2 * source)
                prob = jnp.exp2(logit).astype(BF16)
                prob_ref[h, :, k * cols : (k + 1) * cols] = jnp.minimum(prob, cap_ref[b, k])
        for h in range(HEADS):
            least = jnp.minimum(least, finish(h))

        @pl.when(jnp.logical_not(jnp.min(least) > 2.0**-90))
        def _():
            for h in range(HEADS):
                for r in range(relations):
                    u_ref[h, r] = spread(r, h)

                def raw(k):
                    r, slot = rel_ref[b, k], slot_ref[b, k]
                    x = u_ref[h, r] + score_ref[slot, pl.ds(r * HEADS + h, 1), :]
                    return jnp.where(cap_ref[b, k].astype(F32) > 0, jnp.maximum(x, 0.2 * x), -jnp.inf)

                w_ref[h, 0] = jnp.full((rows, cols), -jnp.inf, F32)

                def climb(k, carry):
                    w_ref[h, 0] = jnp.maximum(w_ref[h, 0], raw(k))
                    return carry

                lax.fori_loop(0, lists, climb, 0)
                w_ref[h, 0] = jnp.broadcast_to(jnp.max(w_ref[h, 0], axis=1, keepdims=True), (rows, cols))

                def weigh(k, carry):
                    at = pl.ds(pl.multiple_of(k * cols, cols), cols)
                    prob_ref[h, :, at] = jnp.exp2(raw(k) - w_ref[h, 0]).astype(BF16)
                    return carry

                lax.fori_loop(0, lists, weigh, 0)
                finish(h)

        return carry

    lax.fori_loop(0, blocks, body, 0)


def attend(hidden, cap, relation_ids, source_slots, values, scores, tgt_vectors):
    blocks, lists, rows, cols = cap.shape
    width = hidden.shape[1]
    relations = values.shape[1]
    scalars, inside = pl.BlockSpec(memory_space=pltpu.SMEM), pl.BlockSpec(memory_space=pltpu.VMEM)
    return pl.pallas_call(
        attend_kernel,
        in_specs=[scalars] * 2 + [inside] * 5,
        out_specs=inside,
        scratch_shapes=[
            pltpu.VMEM((HEADS, relations, rows, cols), F32),
            pltpu.VMEM((HEADS, relations, rows, cols), F32),
            pltpu.VMEM((HEADS, rows, lists * cols), BF16),
        ],
        out_shape=jax.ShapeDtypeStruct((blocks, rows, width), BF16),
        compiler_params=pltpu.CompilerParams(vmem_limit_bytes=24 * 1024 * 1024),
        name="attend",
    )(relation_ids, source_slots, hidden.reshape(blocks, rows, width), cap, tgt_vectors, values, scores).reshape(
        blocks * rows, width
    )


def score_vectors(relation_weight, att_source, att_target):
    relations, width = att_source.shape
    head_width = width // HEADS
    split = att_source.reshape(relations, HEADS, head_width)
    moved = jnp.einsum(
        "rche,rhe->rhc",
        relation_weight.astype(F32).reshape(relations, width, HEADS, head_width),
        split,
        precision=lax.Precision.HIGHEST,
        preferred_element_type=F32,
    ).reshape(relations * HEADS, width)
    src = jnp.concatenate(three_parts(moved * LOG2E) + (jnp.zeros((8, width), BF16),), axis=0)
    own_head = (jnp.arange(width)[:, None] // head_width) == (jnp.arange(relations * HEADS)[None, :] % HEADS)
    spread = jnp.repeat(att_target.T, HEADS, axis=1)
    tgt = jnp.where(own_head, spread, 0.0) * LOG2E
    tgt = jnp.pad(tgt, ((0, 0), (0, 128 - relations * HEADS)))
    return src, jnp.stack(three_parts(tgt))


def shards(
    node_features,
    proj_weight,
    relation_weight,
    att_source,
    att_target,
    edge_mask,
    relation_ids,
    send_blocks,
    source_slots,
):
    block_rows = edge_mask.shape[-1]
    local_blocks = edge_mask.shape[0]
    rows_local = local_blocks * block_rows
    depth, width = proj_weight.shape
    n_feat = lax.axis_size("feat")
    n_graph = lax.axis_size("graph")
    levels = n_graph // 2
    place = lax.axis_index("graph")
    core, level = lax.rem(place, 2), place // 2

    def send(x, up, cores=0):
        pairs = [(p, (p + 2 * up) % n_graph ^ cores) for p in range(n_graph)]
        return lax.ppermute(x, "graph", pairs)

    cut = local_blocks // 2
    rows_a, half = cut * block_rows, width // 2
    features = node_features.T
    first = arrange(features, proj_weight, core, n_feat, 0, rows_a, half)
    first, features, send_blocks = lax.optimization_barrier((first, features, send_blocks))
    got = lax.all_to_all(first, "feat", 0, 0, tiled=True).reshape(n_feat * depth, rows_a + half)
    outgoing = arrange(features, proj_weight, core, n_feat, rows_a, rows_local, 0)

    pair = jnp.stack([send_blocks[0], send(send_blocks[0], 0, 1)])
    lists = [pair[:, 2 * ((level + d) % levels) + core] for d in range(levels)]
    peer = source_slots // CAP
    distance = (level - peer // 2 + levels) % levels
    slots = (2 * (distance ^ (distance >> 1)) + (peer % 2 ^ core)) * CAP + source_slots % CAP
    src_vectors, tgt_vectors = score_vectors(relation_weight, att_source, att_target)

    got, outgoing, cap, src_vectors, tgt_vectors, slots, lists = lax.optimization_barrier(
        (got, outgoing, caps(edge_mask), src_vectors, tgt_vectors, slots, lists)
    )
    later = lax.all_to_all(outgoing, "feat", 0, 0, tiled=True).reshape(n_feat * depth, rows_local - rows_a)

    mine = got[:, rows_a:]
    other = send(mine, 0, 1)
    whole = jnp.where(core == 0, jnp.concatenate([mine, other], axis=1), jnp.concatenate([other, mine], axis=1))

    def project(x):
        return lax.dot_general(x, whole, (((0,), (0,)), ((), ())), preferred_element_type=F32).astype(BF16)

    def both(pieces):
        return [pieces, [(send(x, 0, 1), low, high) for x, low, high in pieces]]

    def spread(group, first, index, kept):
        return transform(group, n_graph, first, index, relation_weight, src_vectors, block_rows, *kept)

    def ring(part):
        return send(part, 1), send(part, -1)

    def forward(up, down):
        middle = up.shape[0] // 2
        return send(up[:middle], 1), send(down[middle:], -1)

    a = project(got[:, :rows_a])
    up_a, down_a = ring(a)
    near, lists = lists[:1], [send(lists[d], d) for d in range(1, levels)]
    later, up_a, down_a, lists = lax.optimization_barrier((later, up_a, down_a, lists))
    far_a = forward(up_a, down_a)
    b = project(later)
    up_b, down_b = ring(b)
    done = spread(both([(a, 0, cut), (b, cut, local_blocks)]), 0, near, (None, None))
    up_b, down_b, far_a, done = lax.optimization_barrier((up_b, down_b, far_a, done))
    far_b = forward(up_b, down_b)
    done = spread(
        both([(up_a, 0, cut), (up_b, cut, local_blocks)]) + both([(down_a, 0, cut), (down_b, cut, local_blocks)]),
        2,
        (lists[0], lists[2]),
        done,
    )
    far_b, done = lax.optimization_barrier((far_b, done))
    quarter = cut // 2
    far = [(x, n * quarter, (n + 1) * quarter) for n, x in enumerate(far_a + far_b)]
    values, scores = spread(both(far), 6, lists[1:2], done)
    return attend(jnp.concatenate([a, b]), cap, relation_ids, slots, values, scores, tgt_vectors)


def solution(mesh):
    placed = (
        P("graph", "feat"),
        P("feat", None),
        P(),
        P(),
        P(),
        P(("graph", "feat"), None, None, None),
        P(("graph", "feat"), None),
        P(("graph", "feat"), None, None),
        P(("graph", "feat"), None),
    )
    return jax.shard_map(
        shards, mesh=mesh, in_specs=placed, out_specs=P(("graph", "feat"), None), check_vma=False
    )
```

```python
import functools

import jax
import jax.numpy as jnp
from jax import lax
from jax.experimental import pallas as pl
from jax.experimental.pallas import tpu as pltpu
from jax.sharding import PartitionSpec as P

HEADS = 4
CAP = 4
LOG2E = 1.4426950408889634
F32 = jnp.float32
BF16 = jnp.bfloat16


def arrange_kernel(low, high, core_ref, x_ref, w_ref, out_ref):
    peers, _, columns = out_ref.shape
    total = x_ref.shape[1] // peers
    rows = high - low
    for q in range(peers):
        out_ref[q, :, :rows] = x_ref[:, q * total + low : q * total + high]
        if columns > rows:
            out_ref[q, :, rows:] = w_ref[...]


def arrange(features, weight, core, peers, low, high, half):
    depth, columns = features.shape
    rows = columns // peers
    step = 4
    return pl.pallas_call(
        functools.partial(arrange_kernel, low, high),
        grid_spec=pltpu.PrefetchScalarGridSpec(
            num_scalar_prefetch=1,
            grid=(peers // step,),
            in_specs=[
                pl.BlockSpec((depth, step * rows), lambda i, core_ref: (0, i)),
                pl.BlockSpec((depth, weight.shape[1] // 2), lambda i, core_ref: (0, core_ref[0])),
            ],
            out_specs=pl.BlockSpec((step, depth, high - low + half), lambda i, core_ref: (i, 0, 0)),
        ),
        out_shape=jax.ShapeDtypeStruct((peers, depth, high - low + half), BF16),
        name="arrange",
    )(core.reshape(1), features, weight)


def three_parts(x):
    hi = lax.reduce_precision(x, 8, 7)
    rest = x - hi
    mid = lax.reduce_precision(rest, 8, 7)
    return hi.astype(BF16), mid.astype(BF16), (rest - mid).astype(BF16)


def transform_kernel(bounds, first, *refs):
    index, refs = refs[: len(bounds) // 2], refs[len(bounds) // 2 :]
    n_pieces = sum(len(p) for p in bounds)
    pieces = refs[:n_pieces]
    rw_ref, src_ref = refs[n_pieces : n_pieces + 2]
    val_ref, score_ref, hid_ref = refs[-3:]
    relations, block = val_ref.shape[1:3]
    cap = index[0].shape[1]
    begin = 0
    for source in range(len(bounds)):
        for c in range(cap):
            wanted = index[source // 2][source % 2, c]
            for n, (low, high) in enumerate(bounds[source]):

                @pl.when((wanted >= low) & (wanted < high))
                def _():
                    row = pl.multiple_of((wanted - low) * block, block)
                    hid_ref[source, c * block : (c + 1) * block] = pieces[begin + n][pl.ds(row, block), :]

        begin += len(bounds[source])
    for source in range(len(bounds)):
        hid = hid_ref[source]
        at = (first + source) * cap
        for r in range(relations):
            moved = jnp.dot(hid, rw_ref[r], preferred_element_type=F32).astype(BF16)
            for c in range(cap):
                val_ref[at + c, r] = moved[c * block : (c + 1) * block]
        raw = lax.dot_general(src_ref[...], hid, (((1,), (1,)), ((), ())), preferred_element_type=F32)
        score = raw[0:8] + raw[8:16] + raw[16:24]
        for c in range(cap):
            score_ref[at + c] = score[:, c * block : (c + 1) * block]


def transform(sources, peers, first, index, relation_weight, src_vectors, block, values, scores):
    bounds = tuple(tuple((low, high) for _, low, high in pieces) for pieces in sources)
    arrays = [array for pieces in sources for array, _, _ in pieces]
    cap = index[0].shape[1]
    relations, width = relation_weight.shape[:2]
    inside = pl.BlockSpec(memory_space=pltpu.VMEM)
    kept = () if values is None else (values, scores)
    at = len(index) + len(arrays) + 2
    return pl.pallas_call(
        functools.partial(transform_kernel, bounds, first),
        in_specs=[pl.BlockSpec(memory_space=pltpu.SMEM)] * len(index) + [inside] * (len(arrays) + 2 + len(kept)),
        out_specs=[inside, inside],
        scratch_shapes=[pltpu.VMEM((len(bounds), cap * block, width), BF16)],
        out_shape=[
            jax.ShapeDtypeStruct((peers * cap, relations, block, width), BF16),
            jax.ShapeDtypeStruct((peers * cap, 8, block), F32),
        ],
        input_output_aliases={at + n: n for n in range(len(kept))},
        compiler_params=pltpu.CompilerParams(vmem_limit_bytes=24 * 1024 * 1024),
        name="transform",
    )(*index, *arrays, relation_weight, src_vectors, *kept)


def cap_kernel(mask_ref, cap_ref):
    cap_ref[...] = jnp.where(mask_ref[...] > 0, jnp.inf, 0.0).astype(BF16)


def caps(edge_mask):
    shape = edge_mask.shape
    spec = pl.BlockSpec((1,) + shape[1:], lambda b: (b, 0, 0, 0))
    return pl.pallas_call(
        cap_kernel,
        grid=shape[:1],
        in_specs=[spec],
        out_specs=spec,
        out_shape=jax.ShapeDtypeStruct(shape, BF16),
        name="caps",
    )(edge_mask)


def attend_kernel(
    rel_ref, slot_ref, own_ref, cap_ref, tgt_ref, val_ref, score_ref, out_ref, u_ref, w_ref, prob_ref, least_ref
):
    blocks, lists, rows, cols = cap_ref.shape
    relations = u_ref.shape[1]
    ones = jnp.ones((lists * cols, cols), BF16)

    def parts(b):
        own = own_ref[b]
        target = jnp.dot(own, tgt_ref[0], preferred_element_type=F32)
        target += jnp.dot(own, tgt_ref[1], preferred_element_type=F32)
        target += jnp.dot(own, tgt_ref[2], preferred_element_type=F32)
        rels = [rel_ref[b, k] for k in range(lists)]
        slots = [slot_ref[b, k] for k in range(lists)]

        def spread(r, h):
            return jnp.broadcast_to(target[:, r * HEADS + h : r * HEADS + h + 1], (rows, cols))

        def finish(h, weights):
            lanes = slice(h * cols, (h + 1) * cols)
            value = jnp.concatenate([val_ref[slots[k], rels[k], :, lanes] for k in range(lists)], axis=0)
            summed = jnp.dot(weights, jnp.concatenate([value, ones], axis=1), preferred_element_type=F32)
            total = summed[:, cols:]
            mixed = summed[:, :cols] / total + own[:, lanes].astype(F32)
            out_ref[b, :, lanes] = jnp.where(mixed > 0, mixed, jnp.exp(jnp.minimum(mixed, 0.0)) - 1.0).astype(BF16)
            return total

        return rels, slots, spread, finish

    def body(b, carry):
        rels, slots, spread, finish = parts(b)
        reach = [jnp.full((8, cols), -jnp.inf, F32) for _ in range(relations)]
        for k in range(lists):
            source = score_ref[slots[k]]
            for r in range(relations):
                reach[r] = jnp.maximum(reach[r], jnp.where(rels[k] == r, source, -jnp.inf))
        for h in range(HEADS):
            bound = jnp.full((rows, cols), -jnp.inf, F32)
            for r in range(relations):
                c = r * HEADS + h
                most = spread(r, h) + jnp.max(reach[r][c : c + 1, :], axis=1, keepdims=True)
                bound = jnp.maximum(bound, jnp.maximum(most, 0.2 * most))
            for r in range(relations):
                u_ref[h, r] = spread(r, h) - bound
                w_ref[h, r] = 0.2 * spread(r, h) - bound
        least = jnp.full((rows, cols), jnp.inf, F32)
        for h in range(HEADS):
            probs = []
            for k in range(lists):
                source = score_ref[slots[k], pl.ds(rels[k] * HEADS + h, 1), :]
                logit = jnp.maximum(u_ref[h, rels[k]] + source, w_ref[h, rels[k]] + 0.2 * source)
                prob = jnp.exp2(logit).astype(BF16)
                probs.append(jnp.minimum(prob, cap_ref[b, k]))
            least = jnp.minimum(least, finish(h, jnp.concatenate(probs, axis=1)))

        least_ref[...] = jnp.minimum(least_ref[...], least)
        return carry

    least_ref[...] = jnp.full(least_ref.shape, jnp.inf, F32)
    lax.fori_loop(0, blocks, body, 0)

    def redo(b, carry):
        _, _, spread, finish = parts(b)
        for h in range(HEADS):
            for r in range(relations):
                u_ref[h, r] = spread(r, h)

            def raw(k):
                r, slot = rel_ref[b, k], slot_ref[b, k]
                x = u_ref[h, r] + score_ref[slot, pl.ds(r * HEADS + h, 1), :]
                return jnp.where(cap_ref[b, k].astype(F32) > 0, jnp.maximum(x, 0.2 * x), -jnp.inf)

            w_ref[h, 0] = jnp.full((rows, cols), -jnp.inf, F32)

            def climb(k, carry):
                w_ref[h, 0] = jnp.maximum(w_ref[h, 0], raw(k))
                return carry

            lax.fori_loop(0, lists, climb, 0)
            w_ref[h, 0] = jnp.broadcast_to(jnp.max(w_ref[h, 0], axis=1, keepdims=True), (rows, cols))

            def weigh(k, carry):
                at = pl.ds(pl.multiple_of(k * cols, cols), cols)
                prob_ref[h, :, at] = jnp.exp2(raw(k) - w_ref[h, 0]).astype(BF16)
                return carry

            lax.fori_loop(0, lists, weigh, 0)
            finish(h, prob_ref[h])
        return carry

    @pl.when(jnp.logical_not(jnp.min(least_ref[...]) > 2.0**-90))
    def _():
        lax.fori_loop(0, blocks, redo, 0)


def attend(hidden, cap, relation_ids, source_slots, values, scores, tgt_vectors):
    blocks, lists, rows, cols = cap.shape
    width = hidden.shape[1]
    relations = values.shape[1]
    scalars, inside = pl.BlockSpec(memory_space=pltpu.SMEM), pl.BlockSpec(memory_space=pltpu.VMEM)
    return pl.pallas_call(
        attend_kernel,
        in_specs=[scalars] * 2 + [inside] * 5,
        out_specs=inside,
        scratch_shapes=[
            pltpu.VMEM((HEADS, relations, rows, cols), F32),
            pltpu.VMEM((HEADS, relations, rows, cols), F32),
            pltpu.VMEM((HEADS, rows, lists * cols), BF16),
            pltpu.VMEM((rows, cols), F32),
        ],
        out_shape=jax.ShapeDtypeStruct((blocks, rows, width), BF16),
        compiler_params=pltpu.CompilerParams(vmem_limit_bytes=24 * 1024 * 1024),
        name="attend",
    )(relation_ids, source_slots, hidden.reshape(blocks, rows, width), cap, tgt_vectors, values, scores).reshape(
        blocks * rows, width
    )


def score_vectors(relation_weight, att_source, att_target):
    relations, width = att_source.shape
    head_width = width // HEADS
    split = att_source.reshape(relations, HEADS, head_width)
    moved = jnp.einsum(
        "rche,rhe->rhc",
        relation_weight.astype(F32).reshape(relations, width, HEADS, head_width),
        split,
        precision=lax.Precision.HIGHEST,
        preferred_element_type=F32,
    ).reshape(relations * HEADS, width)
    src = jnp.concatenate(three_parts(moved * LOG2E) + (jnp.zeros((8, width), BF16),), axis=0)
    own_head = (jnp.arange(width)[:, None] // head_width) == (jnp.arange(relations * HEADS)[None, :] % HEADS)
    spread = jnp.repeat(att_target.T, HEADS, axis=1)
    tgt = jnp.where(own_head, spread, 0.0) * LOG2E
    tgt = jnp.pad(tgt, ((0, 0), (0, 128 - relations * HEADS)))
    return src, jnp.stack(three_parts(tgt))


def shards(
    node_features,
    proj_weight,
    relation_weight,
    att_source,
    att_target,
    edge_mask,
    relation_ids,
    send_blocks,
    source_slots,
):
    block_rows = edge_mask.shape[-1]
    local_blocks = edge_mask.shape[0]
    rows_local = local_blocks * block_rows
    depth, width = proj_weight.shape
    n_feat = lax.axis_size("feat")
    n_graph = lax.axis_size("graph")
    levels = n_graph // 2
    place = lax.axis_index("graph")
    core, level = lax.rem(place, 2), place // 2

    def send(x, up, cores=0):
        pairs = [(p, (p + 2 * up) % n_graph ^ cores) for p in range(n_graph)]
        return lax.ppermute(x, "graph", pairs)

    cut = local_blocks // 2
    rows_a, half = cut * block_rows, width // 2
    features = node_features.T
    first = arrange(features, proj_weight, core, n_feat, 0, rows_a, half)
    first, features, send_blocks = lax.optimization_barrier((first, features, send_blocks))
    got = lax.all_to_all(first, "feat", 0, 0, tiled=True).reshape(n_feat * depth, rows_a + half)
    outgoing = arrange(features, proj_weight, core, n_feat, rows_a, rows_local, 0)

    pair = jnp.stack([send_blocks[0], send(send_blocks[0], 0, 1)])
    lists = [pair[:, 2 * ((level + d) % levels) + core] for d in range(levels)]
    peer = source_slots // CAP
    distance = (level - peer // 2 + levels) % levels
    slots = (2 * (distance ^ (distance >> 1)) + (peer % 2 ^ core)) * CAP + source_slots % CAP
    src_vectors, tgt_vectors = score_vectors(relation_weight, att_source, att_target)

    got, outgoing, cap, src_vectors, tgt_vectors, slots, lists = lax.optimization_barrier(
        (got, outgoing, caps(edge_mask), src_vectors, tgt_vectors, slots, lists)
    )
    later = lax.all_to_all(outgoing, "feat", 0, 0, tiled=True).reshape(n_feat * depth, rows_local - rows_a)

    mine = got[:, rows_a:]
    other = send(mine, 0, 1)
    whole = jnp.where(core == 0, jnp.concatenate([mine, other], axis=1), jnp.concatenate([other, mine], axis=1))

    def project(x):
        return lax.dot_general(x, whole, (((0,), (0,)), ((), ())), preferred_element_type=F32).astype(BF16)

    def both(pieces):
        return [pieces, [(send(x, 0, 1), low, high) for x, low, high in pieces]]

    def spread(group, first, index, kept):
        return transform(group, n_graph, first, index, relation_weight, src_vectors, block_rows, *kept)

    def ring(part):
        return send(part, 1), send(part, -1)

    def forward(up, down):
        middle = up.shape[0] // 2
        return send(up[:middle], 1), send(down[middle:], -1)

    a = project(got[:, :rows_a])
    up_a, down_a = ring(a)
    near, lists = lists[:1], [send(lists[d], d) for d in range(1, levels)]
    later, up_a, down_a, lists = lax.optimization_barrier((later, up_a, down_a, lists))
    far_a = forward(up_a, down_a)
    b = project(later)
    up_b, down_b = ring(b)
    done = spread(both([(a, 0, cut), (b, cut, local_blocks)]), 0, near, (None, None))
    up_b, down_b, far_a, done = lax.optimization_barrier((up_b, down_b, far_a, done))
    far_b = forward(up_b, down_b)
    done = spread(
        both([(up_a, 0, cut), (up_b, cut, local_blocks)]) + both([(down_a, 0, cut), (down_b, cut, local_blocks)]),
        2,
        (lists[0], lists[2]),
        done,
    )
    far_b, done = lax.optimization_barrier((far_b, done))
    quarter = cut // 2
    far = [(x, n * quarter, (n + 1) * quarter) for n, x in enumerate(far_a + far_b)]
    values, scores = spread(both(far), 6, lists[1:2], done)
    return attend(jnp.concatenate([a, b]), cap, relation_ids, slots, values, scores, tgt_vectors)


def solution(mesh):
    placed = (
        P("graph", "feat"),
        P("feat", None),
        P(),
        P(),
        P(),
        P(("graph", "feat"), None, None, None),
        P(("graph", "feat"), None),
        P(("graph", "feat"), None, None),
        P(("graph", "feat"), None),
    )
    return jax.shard_map(
        shards, mesh=mesh, in_specs=placed, out_specs=P(("graph", "feat"), None), check_vma=False
    )
```

```python
import functools

import jax
import jax.numpy as jnp
from jax import lax
from jax.experimental import pallas as pl
from jax.experimental.pallas import tpu as pltpu
from jax.sharding import PartitionSpec as P

HEADS = 4
CAP = 4
LOG2E = 1.4426950408889634
F32 = jnp.float32
BF16 = jnp.bfloat16


def arrange_kernel(low, high, core_ref, x_ref, w_ref, out_ref):
    peers, _, columns = out_ref.shape
    total = x_ref.shape[1] // peers
    rows = high - low
    for q in range(peers):
        out_ref[q, :, :rows] = x_ref[:, q * total + low : q * total + high]
        if columns > rows:
            out_ref[q, :, rows:] = w_ref[...]


def arrange(features, weight, core, peers, low, high, half):
    depth, columns = features.shape
    rows = columns // peers
    step = 4
    return pl.pallas_call(
        functools.partial(arrange_kernel, low, high),
        grid_spec=pltpu.PrefetchScalarGridSpec(
            num_scalar_prefetch=1,
            grid=(peers // step,),
            in_specs=[
                pl.BlockSpec((depth, step * rows), lambda i, core_ref: (0, i)),
                pl.BlockSpec((depth, weight.shape[1] // 2), lambda i, core_ref: (0, core_ref[0])),
            ],
            out_specs=pl.BlockSpec((step, depth, high - low + half), lambda i, core_ref: (i, 0, 0)),
        ),
        out_shape=jax.ShapeDtypeStruct((peers, depth, high - low + half), BF16),
        name="arrange",
    )(core.reshape(1), features, weight)


def three_parts(x):
    hi = lax.reduce_precision(x, 8, 7)
    rest = x - hi
    mid = lax.reduce_precision(rest, 8, 7)
    return hi.astype(BF16), mid.astype(BF16), (rest - mid).astype(BF16)


def transform_kernel(bounds, first, *refs):
    index, refs = refs[: len(bounds) // 2], refs[len(bounds) // 2 :]
    n_pieces = sum(len(p) for p in bounds)
    pieces = refs[:n_pieces]
    rw_ref, src_ref = refs[n_pieces : n_pieces + 2]
    val_ref, score_ref, hid_ref = refs[-3:]
    relations, block = val_ref.shape[1:3]
    cap = index[0].shape[1]
    begin = 0
    for source in range(len(bounds)):
        for c in range(cap):
            wanted = index[source // 2][source % 2, c]
            for n, (low, high) in enumerate(bounds[source]):

                @pl.when((wanted >= low) & (wanted < high))
                def _():
                    row = pl.multiple_of((wanted - low) * block, block)
                    hid_ref[source, c * block : (c + 1) * block] = pieces[begin + n][pl.ds(row, block), :]

        begin += len(bounds[source])
    for source in range(len(bounds)):
        hid = hid_ref[source]
        at = (first + source) * cap
        for r in range(relations):
            moved = jnp.dot(hid, rw_ref[r], preferred_element_type=F32).astype(BF16)
            for c in range(cap):
                val_ref[at + c, r] = moved[c * block : (c + 1) * block]
        raw = lax.dot_general(src_ref[...], hid, (((1,), (1,)), ((), ())), preferred_element_type=F32)
        score = raw[0:8] + raw[8:16] + raw[16:24]
        for c in range(cap):
            score_ref[at + c] = score[:, c * block : (c + 1) * block]


def transform(sources, peers, first, index, relation_weight, src_vectors, block, values, scores):
    bounds = tuple(tuple((low, high) for _, low, high in pieces) for pieces in sources)
    arrays = [array for pieces in sources for array, _, _ in pieces]
    cap = index[0].shape[1]
    relations, width = relation_weight.shape[:2]
    inside = pl.BlockSpec(memory_space=pltpu.VMEM)
    kept = () if values is None else (values, scores)
    at = len(index) + len(arrays) + 2
    return pl.pallas_call(
        functools.partial(transform_kernel, bounds, first),
        in_specs=[pl.BlockSpec(memory_space=pltpu.SMEM)] * len(index) + [inside] * (len(arrays) + 2 + len(kept)),
        out_specs=[inside, inside],
        scratch_shapes=[pltpu.VMEM((len(bounds), cap * block, width), BF16)],
        out_shape=[
            jax.ShapeDtypeStruct((peers * cap, relations, block, width), BF16),
            jax.ShapeDtypeStruct((peers * cap, 8, block), F32),
        ],
        input_output_aliases={at + n: n for n in range(len(kept))},
        compiler_params=pltpu.CompilerParams(vmem_limit_bytes=24 * 1024 * 1024),
        name="transform",
    )(*index, *arrays, relation_weight, src_vectors, *kept)


def cap_kernel(mask_ref, cap_ref):
    cap_ref[...] = jnp.where(mask_ref[...] > 0, jnp.inf, 0.0).astype(BF16)


def caps(edge_mask):
    shape = edge_mask.shape
    spec = pl.BlockSpec((1,) + shape[1:], lambda b: (b, 0, 0, 0))
    return pl.pallas_call(
        cap_kernel,
        grid=shape[:1],
        in_specs=[spec],
        out_specs=spec,
        out_shape=jax.ShapeDtypeStruct(shape, BF16),
        name="caps",
    )(edge_mask)


def target_kernel(own_ref, tgt_ref, tile_ref):
    blocks, relations, _, rows, cols = tile_ref.shape

    def body(b, carry):
        own = own_ref[b]
        target = jnp.dot(own, tgt_ref[0], preferred_element_type=F32)
        target += jnp.dot(own, tgt_ref[1], preferred_element_type=F32)
        target += jnp.dot(own, tgt_ref[2], preferred_element_type=F32)
        for r in range(relations):
            for h in range(HEADS):
                c = r * HEADS + h
                tile_ref[b, r, h] = jnp.broadcast_to(target[:, c : c + 1], (rows, cols))
        return carry

    lax.fori_loop(0, blocks, body, 0)


def target_tiles(hidden, tgt_vectors, blocks, relations):
    rows, width = hidden.shape[0] // blocks, hidden.shape[1]
    inside = pl.BlockSpec(memory_space=pltpu.VMEM)
    return pl.pallas_call(
        target_kernel,
        in_specs=[inside, inside],
        out_specs=inside,
        out_shape=jax.ShapeDtypeStruct((blocks, relations, HEADS, rows, rows), F32),
        compiler_params=pltpu.CompilerParams(vmem_limit_bytes=8 * 1024 * 1024),
        name="targets",
    )(hidden.reshape(blocks, rows, width), tgt_vectors)


def attend_kernel(
    rel_ref, slot_ref, own_ref, cap_ref, tile_ref, val_ref, score_ref, out_ref, u_ref, w_ref, prob_ref, least_ref
):
    blocks, lists, rows, cols = cap_ref.shape
    relations = u_ref.shape[1]
    ones = jnp.ones((lists * cols, cols), BF16)

    def parts(b):
        own = own_ref[b]
        rels = [rel_ref[b, k] for k in range(lists)]
        slots = [slot_ref[b, k] for k in range(lists)]

        def spread(r, h):
            return tile_ref[b, r, h]

        def finish(h, weights):
            lanes = slice(h * cols, (h + 1) * cols)
            value = jnp.concatenate([val_ref[slots[k], rels[k], :, lanes] for k in range(lists)], axis=0)
            summed = jnp.dot(weights, jnp.concatenate([value, ones], axis=1), preferred_element_type=F32)
            total = summed[:, cols:]
            mixed = summed[:, :cols] / total + own[:, lanes].astype(F32)
            out_ref[b, :, lanes] = jnp.where(mixed > 0, mixed, jnp.exp(jnp.minimum(mixed, 0.0)) - 1.0).astype(BF16)
            return total

        return rels, slots, spread, finish

    def body(b, carry):
        rels, slots, spread, finish = parts(b)
        reach = [jnp.full((8, cols), -jnp.inf, F32) for _ in range(relations)]
        for k in range(lists):
            source = score_ref[slots[k]]
            for r in range(relations):
                reach[r] = jnp.maximum(reach[r], jnp.where(rels[k] == r, source, -jnp.inf))
        for h in range(HEADS):
            bound = jnp.full((rows, cols), -jnp.inf, F32)
            for r in range(relations):
                c = r * HEADS + h
                most = spread(r, h) + jnp.max(reach[r][c : c + 1, :], axis=1, keepdims=True)
                bound = jnp.maximum(bound, jnp.maximum(most, 0.2 * most))
            for r in range(relations):
                u_ref[h, r] = spread(r, h) - bound
                w_ref[h, r] = 0.2 * spread(r, h) - bound
        least = jnp.full((rows, cols), jnp.inf, F32)
        for h in range(HEADS):
            probs = []
            for k in range(lists):
                source = score_ref[slots[k], pl.ds(rels[k] * HEADS + h, 1), :]
                logit = jnp.maximum(u_ref[h, rels[k]] + source, w_ref[h, rels[k]] + 0.2 * source)
                prob = jnp.exp2(logit).astype(BF16)
                probs.append(jnp.minimum(prob, cap_ref[b, k]))
            least = jnp.minimum(least, finish(h, jnp.concatenate(probs, axis=1)))

        least_ref[...] = jnp.minimum(least_ref[...], least)
        return carry

    least_ref[...] = jnp.full(least_ref.shape, jnp.inf, F32)
    lax.fori_loop(0, blocks, body, 0)

    def redo(b, carry):
        _, _, spread, finish = parts(b)
        for h in range(HEADS):
            for r in range(relations):
                u_ref[h, r] = spread(r, h)

            def raw(k):
                r, slot = rel_ref[b, k], slot_ref[b, k]
                x = u_ref[h, r] + score_ref[slot, pl.ds(r * HEADS + h, 1), :]
                return jnp.where(cap_ref[b, k].astype(F32) > 0, jnp.maximum(x, 0.2 * x), -jnp.inf)

            w_ref[h, 0] = jnp.full((rows, cols), -jnp.inf, F32)

            def climb(k, carry):
                w_ref[h, 0] = jnp.maximum(w_ref[h, 0], raw(k))
                return carry

            lax.fori_loop(0, lists, climb, 0)
            w_ref[h, 0] = jnp.broadcast_to(jnp.max(w_ref[h, 0], axis=1, keepdims=True), (rows, cols))

            def weigh(k, carry):
                at = pl.ds(pl.multiple_of(k * cols, cols), cols)
                prob_ref[h, :, at] = jnp.exp2(raw(k) - w_ref[h, 0]).astype(BF16)
                return carry

            lax.fori_loop(0, lists, weigh, 0)
            finish(h, prob_ref[h])
        return carry

    @pl.when(jnp.logical_not(jnp.min(least_ref[...]) > 2.0**-90))
    def _():
        lax.fori_loop(0, blocks, redo, 0)


def attend(hidden, cap, relation_ids, source_slots, values, scores, tiles):
    blocks, lists, rows, cols = cap.shape
    width = hidden.shape[1]
    relations = values.shape[1]
    scalars, inside = pl.BlockSpec(memory_space=pltpu.SMEM), pl.BlockSpec(memory_space=pltpu.VMEM)
    return pl.pallas_call(
        attend_kernel,
        in_specs=[scalars] * 2 + [inside] * 5,
        out_specs=inside,
        scratch_shapes=[
            pltpu.VMEM((HEADS, relations, rows, cols), F32),
            pltpu.VMEM((HEADS, relations, rows, cols), F32),
            pltpu.VMEM((HEADS, rows, lists * cols), BF16),
            pltpu.VMEM((rows, cols), F32),
        ],
        out_shape=jax.ShapeDtypeStruct((blocks, rows, width), BF16),
        compiler_params=pltpu.CompilerParams(vmem_limit_bytes=24 * 1024 * 1024),
        name="attend",
    )(relation_ids, source_slots, hidden.reshape(blocks, rows, width), cap, tiles, values, scores).reshape(
        blocks * rows, width
    )


def score_vectors(relation_weight, att_source, att_target):
    relations, width = att_source.shape
    head_width = width // HEADS
    split = att_source.reshape(relations, HEADS, head_width)
    moved = jnp.einsum(
        "rche,rhe->rhc",
        relation_weight.astype(F32).reshape(relations, width, HEADS, head_width),
        split,
        precision=lax.Precision.HIGHEST,
        preferred_element_type=F32,
    ).reshape(relations * HEADS, width)
    src = jnp.concatenate(three_parts(moved * LOG2E) + (jnp.zeros((8, width), BF16),), axis=0)
    own_head = (jnp.arange(width)[:, None] // head_width) == (jnp.arange(relations * HEADS)[None, :] % HEADS)
    spread = jnp.repeat(att_target.T, HEADS, axis=1)
    tgt = jnp.where(own_head, spread, 0.0) * LOG2E
    tgt = jnp.pad(tgt, ((0, 0), (0, 128 - relations * HEADS)))
    return src, jnp.stack(three_parts(tgt))


def shards(
    node_features,
    proj_weight,
    relation_weight,
    att_source,
    att_target,
    edge_mask,
    relation_ids,
    send_blocks,
    source_slots,
):
    block_rows = edge_mask.shape[-1]
    local_blocks = edge_mask.shape[0]
    rows_local = local_blocks * block_rows
    depth, width = proj_weight.shape
    n_feat = lax.axis_size("feat")
    n_graph = lax.axis_size("graph")
    levels = n_graph // 2
    place = lax.axis_index("graph")
    core, level = lax.rem(place, 2), place // 2

    def send(x, up, cores=0):
        pairs = [(p, (p + 2 * up) % n_graph ^ cores) for p in range(n_graph)]
        return lax.ppermute(x, "graph", pairs)

    cut = local_blocks // 2 + 1
    middle_a = (cut + 1) // 2
    middle_b = local_blocks // 2 - middle_a
    rows_a, half = cut * block_rows, width // 2
    features = node_features.T
    first = arrange(features, proj_weight, core, n_feat, 0, rows_a, half)
    first, features, send_blocks = lax.optimization_barrier((first, features, send_blocks))
    got = lax.all_to_all(first, "feat", 0, 0, tiled=True).reshape(n_feat * depth, rows_a + half)
    outgoing = arrange(features, proj_weight, core, n_feat, rows_a, rows_local, 0)

    pair = jnp.stack([send_blocks[0], send(send_blocks[0], 0, 1)])
    lists = [pair[:, 2 * ((level + d) % levels) + core] for d in range(levels)]
    peer = source_slots // CAP
    distance = (level - peer // 2 + levels) % levels
    slots = (2 * (distance ^ (distance >> 1)) + (peer % 2 ^ core)) * CAP + source_slots % CAP
    src_vectors, tgt_vectors = score_vectors(relation_weight, att_source, att_target)

    got, outgoing, cap, src_vectors, tgt_vectors, slots, lists = lax.optimization_barrier(
        (got, outgoing, caps(edge_mask), src_vectors, tgt_vectors, slots, lists)
    )
    later = lax.all_to_all(outgoing, "feat", 0, 0, tiled=True).reshape(n_feat * depth, rows_local - rows_a)

    mine = got[:, rows_a:]
    other = send(mine, 0, 1)
    whole = jnp.where(core == 0, jnp.concatenate([mine, other], axis=1), jnp.concatenate([other, mine], axis=1))

    def project(x):
        return lax.dot_general(x, whole, (((0,), (0,)), ((), ())), preferred_element_type=F32).astype(BF16)

    def both(pieces):
        return [pieces, [(send(x, 0, 1), low, high) for x, low, high in pieces]]

    def spread(group, first, index, kept):
        return transform(group, n_graph, first, index, relation_weight, src_vectors, block_rows, *kept)

    def ring(part):
        return send(part, 1), send(part, -1)

    def forward(up, down, middle):
        return send(up[: middle * block_rows], 1), send(down[middle * block_rows :], -1)

    a = project(got[:, :rows_a])
    up_a, down_a = ring(a)
    near, lists = lists[:1], [send(lists[d], d) for d in range(1, levels)]
    later, up_a, down_a, lists = lax.optimization_barrier((later, up_a, down_a, lists))
    far_a = forward(up_a, down_a, middle_a)
    b = project(later)
    up_b, down_b = ring(b)
    done = spread(both([(a, 0, cut), (b, cut, local_blocks)]), 0, near, (None, None))
    hidden = jnp.concatenate([a, b])
    tiles = target_tiles(hidden, tgt_vectors, local_blocks, relation_weight.shape[0])
    up_b, down_b, far_a, tiles, done = lax.optimization_barrier((up_b, down_b, far_a, tiles, done))
    far_b = forward(up_b, down_b, middle_b)
    done = spread(
        both([(up_a, 0, cut), (up_b, cut, local_blocks)]) + both([(down_a, 0, cut), (down_b, cut, local_blocks)]),
        2,
        (lists[0], lists[2]),
        done,
    )
    far_b, done = lax.optimization_barrier((far_b, done))
    ends = (0, middle_a, cut, cut + middle_b, local_blocks)
    far = list(zip(far_a + far_b, ends[:-1], ends[1:]))
    values, scores = spread(both(far), 6, lists[1:2], done)
    return attend(hidden, cap, relation_ids, slots, values, scores, tiles)


def solution(mesh):
    placed = (
        P("graph", "feat"),
        P("feat", None),
        P(),
        P(),
        P(),
        P(("graph", "feat"), None, None, None),
        P(("graph", "feat"), None),
        P(("graph", "feat"), None, None),
        P(("graph", "feat"), None),
    )
    return jax.shard_map(
        shards, mesh=mesh, in_specs=placed, out_specs=P(("graph", "feat"), None), check_vma=False
    )
```

```python
import functools

import jax
import jax.numpy as jnp
from jax import lax
from jax.experimental import pallas as pl
from jax.experimental.pallas import tpu as pltpu
from jax.sharding import PartitionSpec as P

HEADS = 4
CAP = 4
LOG2E = 1.4426950408889634
F32 = jnp.float32
BF16 = jnp.bfloat16


def arrange_kernel(low, high, core_ref, x_ref, w_ref, out_ref):
    peers, _, columns = out_ref.shape
    total = x_ref.shape[1] // peers
    rows = high - low
    for q in range(peers):
        out_ref[q, :, :rows] = x_ref[:, q * total + low : q * total + high]
        if columns > rows:
            out_ref[q, :, rows:] = w_ref[...]


def arrange(features, weight, core, peers, low, high, half):
    depth, columns = features.shape
    rows = columns // peers
    step = 4
    return pl.pallas_call(
        functools.partial(arrange_kernel, low, high),
        grid_spec=pltpu.PrefetchScalarGridSpec(
            num_scalar_prefetch=1,
            grid=(peers // step,),
            in_specs=[
                pl.BlockSpec((depth, step * rows), lambda i, core_ref: (0, i)),
                pl.BlockSpec((depth, weight.shape[1] // 2), lambda i, core_ref: (0, core_ref[0])),
            ],
            out_specs=pl.BlockSpec((step, depth, high - low + half), lambda i, core_ref: (i, 0, 0)),
        ),
        out_shape=jax.ShapeDtypeStruct((peers, depth, high - low + half), BF16),
        name="arrange",
    )(core.reshape(1), features, weight)


def three_parts(x):
    hi = lax.reduce_precision(x, 8, 7)
    rest = x - hi
    mid = lax.reduce_precision(rest, 8, 7)
    return hi.astype(BF16), mid.astype(BF16), (rest - mid).astype(BF16)


def transform_kernel(bounds, first, *refs):
    index, refs = refs[: len(bounds) // 2], refs[len(bounds) // 2 :]
    n_pieces = sum(len(p) for p in bounds)
    pieces = refs[:n_pieces]
    rw_ref, src_ref = refs[n_pieces : n_pieces + 2]
    val_ref, score_ref, hid_ref = refs[-3:]
    relations, block = val_ref.shape[1:3]
    cap = index[0].shape[1]
    begin = 0
    for source in range(len(bounds)):
        for c in range(cap):
            wanted = index[source // 2][source % 2, c]
            for n, (low, high) in enumerate(bounds[source]):

                @pl.when((wanted >= low) & (wanted < high))
                def _():
                    row = pl.multiple_of((wanted - low) * block, block)
                    hid_ref[source, c * block : (c + 1) * block] = pieces[begin + n][pl.ds(row, block), :]

        begin += len(bounds[source])
    for source in range(len(bounds)):
        hid = hid_ref[source]
        at = (first + source) * cap
        for r in range(relations):
            moved = jnp.dot(hid, rw_ref[r], preferred_element_type=F32).astype(BF16)
            for c in range(cap):
                val_ref[at + c, r] = moved[c * block : (c + 1) * block]
        raw = lax.dot_general(src_ref[...], hid, (((1,), (1,)), ((), ())), preferred_element_type=F32)
        score = raw[0:8] + raw[8:16] + raw[16:24]
        for c in range(cap):
            score_ref[at + c] = score[:, c * block : (c + 1) * block]


def transform(sources, peers, first, index, relation_weight, src_vectors, block, values, scores):
    bounds = tuple(tuple((low, high) for _, low, high in pieces) for pieces in sources)
    arrays = [array for pieces in sources for array, _, _ in pieces]
    cap = index[0].shape[1]
    relations, width = relation_weight.shape[:2]
    inside = pl.BlockSpec(memory_space=pltpu.VMEM)
    kept = () if values is None else (values, scores)
    at = len(index) + len(arrays) + 2
    return pl.pallas_call(
        functools.partial(transform_kernel, bounds, first),
        in_specs=[pl.BlockSpec(memory_space=pltpu.SMEM)] * len(index) + [inside] * (len(arrays) + 2 + len(kept)),
        out_specs=[inside, inside],
        scratch_shapes=[pltpu.VMEM((len(bounds), cap * block, width), BF16)],
        out_shape=[
            jax.ShapeDtypeStruct((peers * cap, relations, block, width), BF16),
            jax.ShapeDtypeStruct((peers * cap, 8, block), F32),
        ],
        input_output_aliases={at + n: n for n in range(len(kept))},
        compiler_params=pltpu.CompilerParams(vmem_limit_bytes=24 * 1024 * 1024),
        name="transform",
    )(*index, *arrays, relation_weight, src_vectors, *kept)


def cap_kernel(mask_ref, cap_ref):
    cap_ref[...] = jnp.where(mask_ref[...] > 0, jnp.inf, 0.0).astype(BF16)


def caps(edge_mask):
    shape = edge_mask.shape
    spec = pl.BlockSpec((1,) + shape[1:], lambda b: (b, 0, 0, 0))
    return pl.pallas_call(
        cap_kernel,
        grid=shape[:1],
        in_specs=[spec],
        out_specs=spec,
        out_shape=jax.ShapeDtypeStruct(shape, BF16),
        name="caps",
    )(edge_mask)


def target_kernel(own_ref, tgt_ref, tile_ref):
    blocks, relations, _, rows, cols = tile_ref.shape

    def body(b, carry):
        own = own_ref[b]
        target = jnp.dot(own, tgt_ref[0], preferred_element_type=F32)
        target += jnp.dot(own, tgt_ref[1], preferred_element_type=F32)
        target += jnp.dot(own, tgt_ref[2], preferred_element_type=F32)
        for r in range(relations):
            for h in range(HEADS):
                c = r * HEADS + h
                tile_ref[b, r, h] = jnp.broadcast_to(target[:, c : c + 1], (rows, cols))
        return carry

    lax.fori_loop(0, blocks, body, 0)


def target_tiles(hidden, tgt_vectors, blocks, relations):
    rows, width = hidden.shape[0] // blocks, hidden.shape[1]
    inside = pl.BlockSpec(memory_space=pltpu.VMEM)
    return pl.pallas_call(
        target_kernel,
        in_specs=[inside, inside],
        out_specs=inside,
        out_shape=jax.ShapeDtypeStruct((blocks, relations, HEADS, rows, rows), F32),
        compiler_params=pltpu.CompilerParams(vmem_limit_bytes=8 * 1024 * 1024),
        name="targets",
    )(hidden.reshape(blocks, rows, width), tgt_vectors)


def attend_kernel(
    rel_ref, slot_ref, own_ref, cap_ref, tile_ref, val_ref, score_ref, out_ref, u_ref, w_ref, prob_ref, least_ref
):
    blocks, lists, rows, cols = cap_ref.shape
    relations = u_ref.shape[1]
    ones = jnp.ones((lists * cols, cols), BF16)

    def parts(b):
        own = own_ref[b]
        rels = [rel_ref[b, k] for k in range(lists)]
        slots = [slot_ref[b, k] for k in range(lists)]

        def spread(r, h):
            return tile_ref[b, r, h]

        def finish(h, weights):
            lanes = slice(h * cols, (h + 1) * cols)
            value = jnp.concatenate([val_ref[slots[k], rels[k], :, lanes] for k in range(lists)], axis=0)
            summed = jnp.dot(weights, jnp.concatenate([value, ones], axis=1), preferred_element_type=F32)
            total = summed[:, cols:]
            mixed = summed[:, :cols] / total + own[:, lanes].astype(F32)
            out_ref[b, :, lanes] = jnp.where(mixed > 0, mixed, jnp.exp(jnp.minimum(mixed, 0.0)) - 1.0).astype(BF16)
            return total

        return rels, slots, spread, finish

    def body(b, carry):
        rels, slots, spread, finish = parts(b)
        reach = [jnp.full((8, cols), -jnp.inf, F32) for _ in range(relations)]
        for k in range(lists):
            source = score_ref[slots[k]]
            for r in range(relations):
                reach[r] = jnp.maximum(reach[r], jnp.where(rels[k] == r, source, -jnp.inf))
        for h in range(HEADS):
            bound = jnp.full((rows, cols), -jnp.inf, F32)
            for r in range(relations):
                c = r * HEADS + h
                most = spread(r, h) + jnp.max(reach[r][c : c + 1, :], axis=1, keepdims=True)
                bound = jnp.maximum(bound, jnp.maximum(most, 0.2 * most))
            for r in range(relations):
                u_ref[h, r] = spread(r, h) - bound
                w_ref[h, r] = 0.2 * spread(r, h) - bound
        least = jnp.full((rows, cols), jnp.inf, F32)
        for h in range(HEADS):
            probs = []
            for k in range(lists):
                source = score_ref[slots[k], pl.ds(rels[k] * HEADS + h, 1), :]
                logit = jnp.maximum(u_ref[h, rels[k]] + source, w_ref[h, rels[k]] + 0.2 * source)
                prob = jnp.exp2(logit).astype(BF16)
                probs.append(jnp.minimum(prob, cap_ref[b, k]))
            least = jnp.minimum(least, finish(h, jnp.concatenate(probs, axis=1)))

        least_ref[...] = jnp.minimum(least_ref[...], least)
        return carry

    least_ref[...] = jnp.full(least_ref.shape, jnp.inf, F32)
    lax.fori_loop(0, blocks, body, 0)

    def redo(b, carry):
        _, _, spread, finish = parts(b)
        for h in range(HEADS):
            for r in range(relations):
                u_ref[h, r] = spread(r, h)

            def raw(k):
                r, slot = rel_ref[b, k], slot_ref[b, k]
                x = u_ref[h, r] + score_ref[slot, pl.ds(r * HEADS + h, 1), :]
                return jnp.where(cap_ref[b, k].astype(F32) > 0, jnp.maximum(x, 0.2 * x), -jnp.inf)

            w_ref[h, 0] = jnp.full((rows, cols), -jnp.inf, F32)

            def climb(k, carry):
                w_ref[h, 0] = jnp.maximum(w_ref[h, 0], raw(k))
                return carry

            lax.fori_loop(0, lists, climb, 0)
            w_ref[h, 0] = jnp.broadcast_to(jnp.max(w_ref[h, 0], axis=1, keepdims=True), (rows, cols))

            def weigh(k, carry):
                at = pl.ds(pl.multiple_of(k * cols, cols), cols)
                prob_ref[h, :, at] = jnp.exp2(raw(k) - w_ref[h, 0]).astype(BF16)
                return carry

            lax.fori_loop(0, lists, weigh, 0)
            finish(h, prob_ref[h])
        return carry

    @pl.when(jnp.logical_not(jnp.min(least_ref[...]) > 2.0**-90))
    def _():
        lax.fori_loop(0, blocks, redo, 0)


def attend(hidden, cap, relation_ids, source_slots, values, scores, tiles):
    blocks, lists, rows, cols = cap.shape
    width = hidden.shape[1]
    relations = values.shape[1]
    scalars, inside = pl.BlockSpec(memory_space=pltpu.SMEM), pl.BlockSpec(memory_space=pltpu.VMEM)
    return pl.pallas_call(
        attend_kernel,
        in_specs=[scalars] * 2 + [inside] * 5,
        out_specs=inside,
        scratch_shapes=[
            pltpu.VMEM((HEADS, relations, rows, cols), F32),
            pltpu.VMEM((HEADS, relations, rows, cols), F32),
            pltpu.VMEM((HEADS, rows, lists * cols), BF16),
            pltpu.VMEM((rows, cols), F32),
        ],
        out_shape=jax.ShapeDtypeStruct((blocks, rows, width), BF16),
        compiler_params=pltpu.CompilerParams(vmem_limit_bytes=24 * 1024 * 1024),
        name="attend",
    )(relation_ids, source_slots, hidden.reshape(blocks, rows, width), cap, tiles, values, scores).reshape(
        blocks * rows, width
    )


def score_vectors(relation_weight, att_source, att_target):
    relations, width = att_source.shape
    head_width = width // HEADS
    split = att_source.reshape(relations, HEADS, head_width)
    moved = jnp.einsum(
        "rche,rhe->rhc",
        relation_weight.astype(F32).reshape(relations, width, HEADS, head_width),
        split,
        precision=lax.Precision.HIGHEST,
        preferred_element_type=F32,
    ).reshape(relations * HEADS, width)
    src = jnp.concatenate(three_parts(moved * LOG2E) + (jnp.zeros((8, width), BF16),), axis=0)
    own_head = (jnp.arange(width)[:, None] // head_width) == (jnp.arange(relations * HEADS)[None, :] % HEADS)
    spread = jnp.repeat(att_target.T, HEADS, axis=1)
    tgt = jnp.where(own_head, spread, 0.0) * LOG2E
    tgt = jnp.pad(tgt, ((0, 0), (0, 128 - relations * HEADS)))
    return src, jnp.stack(three_parts(tgt))


def shards(
    node_features,
    proj_weight,
    relation_weight,
    att_source,
    att_target,
    edge_mask,
    relation_ids,
    send_blocks,
    source_slots,
):
    block_rows = edge_mask.shape[-1]
    local_blocks = edge_mask.shape[0]
    rows_local = local_blocks * block_rows
    depth, width = proj_weight.shape
    n_feat = lax.axis_size("feat")
    n_graph = lax.axis_size("graph")
    levels = n_graph // 2
    place = lax.axis_index("graph")
    core, level = lax.rem(place, 2), place // 2

    def send(x, up, cores=0):
        pairs = [(p, (p + 2 * up) % n_graph ^ cores) for p in range(n_graph)]
        return lax.ppermute(x, "graph", pairs)

    cut = local_blocks // 2
    rows_a, half = cut * block_rows, width // 2
    features = node_features.T
    first = arrange(features, proj_weight, core, n_feat, 0, rows_a, half)
    first, features, send_blocks = lax.optimization_barrier((first, features, send_blocks))
    got = lax.all_to_all(first, "feat", 0, 0, tiled=True).reshape(n_feat * depth, rows_a + half)
    outgoing = arrange(features, proj_weight, core, n_feat, rows_a, rows_local, 0)

    pair = jnp.stack([send_blocks[0], send(send_blocks[0], 0, 1)])
    lists = [pair[:, 2 * ((level + d) % levels) + core] for d in range(levels)]
    peer = source_slots // CAP
    distance = (level - peer // 2 + levels) % levels
    slots = (2 * (distance ^ (distance >> 1)) + (peer % 2 ^ core)) * CAP + source_slots % CAP
    src_vectors, tgt_vectors = score_vectors(relation_weight, att_source, att_target)

    got, outgoing, cap, src_vectors, tgt_vectors, slots, lists = lax.optimization_barrier(
        (got, outgoing, caps(edge_mask), src_vectors, tgt_vectors, slots, lists)
    )
    later = lax.all_to_all(outgoing, "feat", 0, 0, tiled=True).reshape(n_feat * depth, rows_local - rows_a)

    mine = got[:, rows_a:]
    other = send(mine, 0, 1)
    whole = jnp.where(core == 0, jnp.concatenate([mine, other], axis=1), jnp.concatenate([other, mine], axis=1))

    def project(x):
        return lax.dot_general(x, whole, (((0,), (0,)), ((), ())), preferred_element_type=F32).astype(BF16)

    def both(pieces):
        return [pieces, [(send(x, 0, 1), low, high) for x, low, high in pieces]]

    def spread(group, first, index, kept):
        return transform(group, n_graph, first, index, relation_weight, src_vectors, block_rows, *kept)

    def ring(part):
        return send(part, 1), send(part, -1)

    def forward(up, down):
        middle = up.shape[0] // 2
        return send(up[:middle], 1), send(down[middle:], -1)

    a = project(got[:, :rows_a])
    up_a, down_a = ring(a)
    near, lists = lists[:1], [send(lists[d], d) for d in range(1, levels)]
    later, up_a, down_a, lists = lax.optimization_barrier((later, up_a, down_a, lists))
    far_a = forward(up_a, down_a)
    b = project(later)
    up_b, down_b = ring(b)
    done = spread(both([(a, 0, cut), (b, cut, local_blocks)]), 0, near, (None, None))
    hidden = jnp.concatenate([a, b])
    tiles = target_tiles(hidden, tgt_vectors, local_blocks, relation_weight.shape[0])
    up_b, down_b, far_a, tiles, done = lax.optimization_barrier((up_b, down_b, far_a, tiles, done))
    far_b = forward(up_b, down_b)
    done = spread(
        both([(up_a, 0, cut), (up_b, cut, local_blocks)]) + both([(down_a, 0, cut), (down_b, cut, local_blocks)]),
        2,
        (lists[0], lists[2]),
        done,
    )
    far_b, done = lax.optimization_barrier((far_b, done))
    quarter = cut // 2
    far = [(x, n * quarter, (n + 1) * quarter) for n, x in enumerate(far_a + far_b)]
    values, scores = spread(both(far), 6, lists[1:2], done)
    return attend(hidden, cap, relation_ids, slots, values, scores, tiles)


def solution(mesh):
    placed = (
        P("graph", "feat"),
        P("feat", None),
        P(),
        P(),
        P(),
        P(("graph", "feat"), None, None, None),
        P(("graph", "feat"), None),
        P(("graph", "feat"), None, None),
        P(("graph", "feat"), None),
    )
    return jax.shard_map(
        shards, mesh=mesh, in_specs=placed, out_specs=P(("graph", "feat"), None), check_vma=False
    )
```

```python
import functools

import jax
import jax.numpy as jnp
from jax import lax
from jax.experimental import pallas as pl
from jax.experimental.pallas import tpu as pltpu
from jax.sharding import PartitionSpec as P

HEADS = 4
CAP = 4
LOG2E = 1.4426950408889634
F32 = jnp.float32
BF16 = jnp.bfloat16


def arrange_kernel(low, high, core_ref, x_ref, w_ref, out_ref):
    peers, _, columns = out_ref.shape
    total = x_ref.shape[1] // peers
    rows = high - low
    for q in range(peers):
        out_ref[q, :, :rows] = x_ref[:, q * total + low : q * total + high]
        if columns > rows:
            out_ref[q, :, rows:] = w_ref[...]


def arrange(features, weight, core, peers, low, high, half):
    depth, columns = features.shape
    rows = columns // peers
    step = 4
    return pl.pallas_call(
        functools.partial(arrange_kernel, low, high),
        grid_spec=pltpu.PrefetchScalarGridSpec(
            num_scalar_prefetch=1,
            grid=(peers // step,),
            in_specs=[
                pl.BlockSpec((depth, step * rows), lambda i, core_ref: (0, i)),
                pl.BlockSpec((depth, weight.shape[1] // 2), lambda i, core_ref: (0, core_ref[0])),
            ],
            out_specs=pl.BlockSpec((step, depth, high - low + half), lambda i, core_ref: (i, 0, 0)),
        ),
        out_shape=jax.ShapeDtypeStruct((peers, depth, high - low + half), BF16),
        name="arrange",
    )(core.reshape(1), features, weight)


def three_parts(x):
    hi = lax.reduce_precision(x, 8, 7)
    rest = x - hi
    mid = lax.reduce_precision(rest, 8, 7)
    return hi.astype(BF16), mid.astype(BF16), (rest - mid).astype(BF16)


def transform_kernel(bounds, first, *refs):
    index, refs = refs[: len(bounds) // 2], refs[len(bounds) // 2 :]
    n_pieces = sum(len(p) for p in bounds)
    pieces = refs[:n_pieces]
    rw_ref, src_ref = refs[n_pieces : n_pieces + 2]
    val_ref, score_ref, hid_ref = refs[-3:]
    relations, block = val_ref.shape[1:3]
    cap = index[0].shape[1]
    begin = 0
    for source in range(len(bounds)):
        for c in range(cap):
            wanted = index[source // 2][source % 2, c]
            for n, (low, high) in enumerate(bounds[source]):

                @pl.when((wanted >= low) & (wanted < high))
                def _():
                    row = pl.multiple_of((wanted - low) * block, block)
                    hid_ref[source, c * block : (c + 1) * block] = pieces[begin + n][pl.ds(row, block), :]

        begin += len(bounds[source])
    for source in range(len(bounds)):
        hid = hid_ref[source]
        at = (first + source) * cap
        for r in range(relations):
            moved = jnp.dot(hid, rw_ref[r], preferred_element_type=F32).astype(BF16)
            for c in range(cap):
                val_ref[at + c, r] = moved[c * block : (c + 1) * block]
        raw = lax.dot_general(src_ref[...], hid, (((1,), (1,)), ((), ())), preferred_element_type=F32)
        score = raw[0:8] + raw[8:16] + raw[16:24]
        for c in range(cap):
            score_ref[at + c] = score[:, c * block : (c + 1) * block]


def transform(sources, peers, first, index, relation_weight, src_vectors, block, values, scores):
    bounds = tuple(tuple((low, high) for _, low, high in pieces) for pieces in sources)
    arrays = [array for pieces in sources for array, _, _ in pieces]
    cap = index[0].shape[1]
    relations, width = relation_weight.shape[:2]
    inside = pl.BlockSpec(memory_space=pltpu.VMEM)
    kept = () if values is None else (values, scores)
    at = len(index) + len(arrays) + 2
    return pl.pallas_call(
        functools.partial(transform_kernel, bounds, first),
        in_specs=[pl.BlockSpec(memory_space=pltpu.SMEM)] * len(index) + [inside] * (len(arrays) + 2 + len(kept)),
        out_specs=[inside, inside],
        scratch_shapes=[pltpu.VMEM((len(bounds), cap * block, width), BF16)],
        out_shape=[
            jax.ShapeDtypeStruct((peers * cap, relations, block, width), BF16),
            jax.ShapeDtypeStruct((peers * cap, 8, block), F32),
        ],
        input_output_aliases={at + n: n for n in range(len(kept))},
        compiler_params=pltpu.CompilerParams(vmem_limit_bytes=24 * 1024 * 1024),
        name="transform",
    )(*index, *arrays, relation_weight, src_vectors, *kept)


def cap_kernel(mask_ref, cap_ref):
    cap_ref[...] = jnp.where(mask_ref[...] > 0, jnp.inf, 0.0).astype(BF16)


def caps(edge_mask):
    shape = edge_mask.shape
    spec = pl.BlockSpec((1,) + shape[1:], lambda b: (b, 0, 0, 0))
    return pl.pallas_call(
        cap_kernel,
        grid=shape[:1],
        in_specs=[spec],
        out_specs=spec,
        out_shape=jax.ShapeDtypeStruct(shape, BF16),
        name="caps",
    )(edge_mask)


def target_kernel(own_ref, tgt_ref, tile_ref):
    blocks, relations, _, rows, cols = tile_ref.shape

    def body(b, carry):
        own = own_ref[b]
        target = jnp.dot(own, tgt_ref[0], preferred_element_type=F32)
        target += jnp.dot(own, tgt_ref[1], preferred_element_type=F32)
        target += jnp.dot(own, tgt_ref[2], preferred_element_type=F32)
        for r in range(relations):
            for h in range(HEADS):
                c = r * HEADS + h
                tile_ref[b, r, h] = jnp.broadcast_to(target[:, c : c + 1], (rows, cols))
        return carry

    lax.fori_loop(0, blocks, body, 0)


def target_tiles(hidden, tgt_vectors, blocks, relations):
    rows, width = hidden.shape[0] // blocks, hidden.shape[1]
    inside = pl.BlockSpec(memory_space=pltpu.VMEM)
    return pl.pallas_call(
        target_kernel,
        in_specs=[inside, inside],
        out_specs=inside,
        out_shape=jax.ShapeDtypeStruct((blocks, relations, HEADS, rows, rows), F32),
        compiler_params=pltpu.CompilerParams(vmem_limit_bytes=8 * 1024 * 1024),
        name="targets",
    )(hidden.reshape(blocks, rows, width), tgt_vectors)


def attend_kernel(
    rel_ref, slot_ref, own_ref, cap_ref, tile_ref, val_ref, score_ref, out_ref, u_ref, w_ref, prob_ref, least_ref
):
    blocks, lists, rows, cols = cap_ref.shape
    relations = u_ref.shape[1]
    ones = jnp.ones((lists * cols, cols), BF16)

    def parts(b):
        own = own_ref[b]
        rels = [rel_ref[b, k] for k in range(lists)]
        slots = [slot_ref[b, k] for k in range(lists)]

        def spread(r, h):
            return tile_ref[b, r, h]

        def finish(h, weights):
            lanes = slice(h * cols, (h + 1) * cols)
            value = jnp.concatenate([val_ref[slots[k], rels[k], :, lanes] for k in range(lists)], axis=0)
            summed = jnp.dot(weights, jnp.concatenate([value, ones], axis=1), preferred_element_type=F32)
            total = summed[:, cols:]
            mixed = summed[:, :cols] / total + own[:, lanes].astype(F32)
            out_ref[b, :, lanes] = jnp.where(mixed > 0, mixed, jnp.exp(jnp.minimum(mixed, 0.0)) - 1.0).astype(BF16)
            return total

        return rels, slots, spread, finish

    def body(b, carry):
        rels, slots, spread, finish = parts(b)
        reach = [jnp.full((8, cols), -jnp.inf, F32) for _ in range(relations)]
        for k in range(lists):
            source = score_ref[slots[k]]
            for r in range(relations):
                reach[r] = jnp.maximum(reach[r], jnp.where(rels[k] == r, source, -jnp.inf))
        for h in range(HEADS):
            bound = jnp.full((rows, cols), -jnp.inf, F32)
            for r in range(relations):
                c = r * HEADS + h
                most = spread(r, h) + jnp.max(reach[r][c : c + 1, :], axis=1, keepdims=True)
                bound = jnp.maximum(bound, jnp.maximum(most, 0.2 * most))
            for r in range(relations):
                u_ref[h, r] = spread(r, h) - bound
                w_ref[h, r] = 0.2 * spread(r, h) - bound
        least = jnp.full((rows, cols), jnp.inf, F32)
        for h in range(HEADS):
            probs = []
            for k in range(lists):
                source = score_ref[slots[k], pl.ds(rels[k] * HEADS + h, 1), :]
                logit = jnp.maximum(u_ref[h, rels[k]] + source, w_ref[h, rels[k]] + 0.2 * source)
                prob = jnp.exp2(logit).astype(BF16)
                probs.append(jnp.minimum(prob, cap_ref[b, k]))
            least = jnp.minimum(least, finish(h, jnp.concatenate(probs, axis=1)))

        least_ref[...] = jnp.minimum(least_ref[...], least)
        return carry

    least_ref[...] = jnp.full(least_ref.shape, jnp.inf, F32)
    lax.fori_loop(0, blocks, body, 0)

    def redo(b, carry):
        _, _, spread, finish = parts(b)
        for h in range(HEADS):
            for r in range(relations):
                u_ref[h, r] = spread(r, h)

            def raw(k):
                r, slot = rel_ref[b, k], slot_ref[b, k]
                x = u_ref[h, r] + score_ref[slot, pl.ds(r * HEADS + h, 1), :]
                return jnp.where(cap_ref[b, k].astype(F32) > 0, jnp.maximum(x, 0.2 * x), -jnp.inf)

            w_ref[h, 0] = jnp.full((rows, cols), -jnp.inf, F32)

            def climb(k, carry):
                w_ref[h, 0] = jnp.maximum(w_ref[h, 0], raw(k))
                return carry

            lax.fori_loop(0, lists, climb, 0)
            w_ref[h, 0] = jnp.broadcast_to(jnp.max(w_ref[h, 0], axis=1, keepdims=True), (rows, cols))

            def weigh(k, carry):
                at = pl.ds(pl.multiple_of(k * cols, cols), cols)
                prob_ref[h, :, at] = jnp.exp2(raw(k) - w_ref[h, 0]).astype(BF16)
                return carry

            lax.fori_loop(0, lists, weigh, 0)
            finish(h, prob_ref[h])
        return carry

    @pl.when(jnp.logical_not(jnp.min(least_ref[...]) > 2.0**-90))
    def _():
        lax.fori_loop(0, blocks, redo, 0)


def attend(hidden, cap, relation_ids, source_slots, values, scores, tiles):
    blocks, lists, rows, cols = cap.shape
    width = hidden.shape[1]
    relations = values.shape[1]
    scalars, inside = pl.BlockSpec(memory_space=pltpu.SMEM), pl.BlockSpec(memory_space=pltpu.VMEM)
    return pl.pallas_call(
        attend_kernel,
        in_specs=[scalars] * 2 + [inside] * 5,
        out_specs=inside,
        scratch_shapes=[
            pltpu.VMEM((HEADS, relations, rows, cols), F32),
            pltpu.VMEM((HEADS, relations, rows, cols), F32),
            pltpu.VMEM((HEADS, rows, lists * cols), BF16),
            pltpu.VMEM((rows, cols), F32),
        ],
        out_shape=jax.ShapeDtypeStruct((blocks, rows, width), BF16),
        compiler_params=pltpu.CompilerParams(vmem_limit_bytes=24 * 1024 * 1024),
        name="attend",
    )(relation_ids, source_slots, hidden.reshape(blocks, rows, width), cap, tiles, values, scores).reshape(
        blocks * rows, width
    )


def score_vectors(relation_weight, att_source, att_target):
    relations, width = att_source.shape
    head_width = width // HEADS
    split = att_source.reshape(relations, HEADS, head_width)
    moved = jnp.einsum(
        "rche,rhe->rhc",
        relation_weight.astype(F32).reshape(relations, width, HEADS, head_width),
        split,
        precision=lax.Precision.HIGHEST,
        preferred_element_type=F32,
    ).reshape(relations * HEADS, width)
    src = jnp.concatenate(three_parts(moved * LOG2E) + (jnp.zeros((8, width), BF16),), axis=0)
    own_head = (jnp.arange(width)[:, None] // head_width) == (jnp.arange(relations * HEADS)[None, :] % HEADS)
    spread = jnp.repeat(att_target.T, HEADS, axis=1)
    tgt = jnp.where(own_head, spread, 0.0) * LOG2E
    tgt = jnp.pad(tgt, ((0, 0), (0, 128 - relations * HEADS)))
    return src, jnp.stack(three_parts(tgt))


def shards(
    node_features,
    proj_weight,
    relation_weight,
    att_source,
    att_target,
    edge_mask,
    relation_ids,
    send_blocks,
    source_slots,
):
    block_rows = edge_mask.shape[-1]
    local_blocks = edge_mask.shape[0]
    rows_local = local_blocks * block_rows
    depth, width = proj_weight.shape
    n_feat = lax.axis_size("feat")
    n_graph = lax.axis_size("graph")
    levels = n_graph // 2
    place = lax.axis_index("graph")
    core, level = lax.rem(place, 2), place // 2

    def send(x, up, cores=0):
        pairs = [(p, (p + 2 * up) % n_graph ^ cores) for p in range(n_graph)]
        return lax.ppermute(x, "graph", pairs)

    cut = local_blocks // 2
    rows_a, half = cut * block_rows, width // 2
    features = node_features.T
    first = arrange(features, proj_weight, core, n_feat, 0, rows_a, half)
    first, features, send_blocks = lax.optimization_barrier((first, features, send_blocks))
    got = lax.all_to_all(first, "feat", 0, 0, tiled=True).reshape(n_feat * depth, rows_a + half)
    outgoing = arrange(features, proj_weight, core, n_feat, rows_a, rows_local, 0)

    pair = jnp.stack([send_blocks[0], send(send_blocks[0], 0, 1)])
    lists = [pair[:, 2 * ((level + d) % levels) + core] for d in range(levels)]
    peer = source_slots // CAP
    distance = (level - peer // 2 + levels) % levels
    slots = (2 * (distance ^ (distance >> 1)) + (peer % 2 ^ core)) * CAP + source_slots % CAP
    src_vectors, tgt_vectors = score_vectors(relation_weight, att_source, att_target)

    got, outgoing, cap, src_vectors, tgt_vectors, slots, lists = lax.optimization_barrier(
        (got, outgoing, caps(edge_mask), src_vectors, tgt_vectors, slots, lists)
    )
    later = lax.all_to_all(outgoing, "feat", 0, 0, tiled=True).reshape(n_feat * depth, rows_local - rows_a)

    mine = got[:, rows_a:]
    other = send(mine, 0, 1)
    whole = jnp.where(core == 0, jnp.concatenate([mine, other], axis=1), jnp.concatenate([other, mine], axis=1))

    def project(x):
        return lax.dot_general(x, whole, (((0,), (0,)), ((), ())), preferred_element_type=F32).astype(BF16)

    def both(pieces):
        return [pieces, [(send(x, 0, 1), low, high) for x, low, high in pieces]]

    def spread(group, first, index, kept):
        return transform(group, n_graph, first, index, relation_weight, src_vectors, block_rows, *kept)

    def ring(part):
        return send(part, 1), send(part, -1)

    def forward(up, down):
        middle = up.shape[0] // 2
        return send(up[:middle], 1), send(down[middle:], -1)

    a = project(got[:, :rows_a])
    up_a, down_a = ring(a)
    near, lists = lists[:1], [send(lists[d], d) for d in range(1, levels)]
    later, up_a, down_a, lists = lax.optimization_barrier((later, up_a, down_a, lists))
    far_a = forward(up_a, down_a)
    b = project(later)
    up_b, down_b = ring(b)
    hidden = jnp.concatenate([a, b])
    tiles = target_tiles(hidden, tgt_vectors, local_blocks, relation_weight.shape[0])
    later_a, later_b, tiles = lax.optimization_barrier((a, b, tiles))
    front, back = (0, cut), (cut, local_blocks)
    own = [[(a, *front), (b, *back)], [(send(later_a, 0, 1), *front), (send(later_b, 0, 1), *back)]]
    done = spread(own, 0, near, (None, None))
    swap_up, swap_down = send(up_a, 0, 1), send(down_a, 0, 1)
    up_b, down_b, far_a, tiles, done, swap_up, swap_down = lax.optimization_barrier(
        (up_b, down_b, far_a, tiles, done, swap_up, swap_down)
    )
    far_b = forward(up_b, down_b)
    rows = [[(up_a, *front), (up_b, *back)], [(swap_up, *front), (send(up_b, 0, 1), *back)]]
    rows += [[(down_a, *front), (down_b, *back)], [(swap_down, *front), (send(down_b, 0, 1), *back)]]
    done = spread(rows, 2, (lists[0], lists[2]), done)
    far_b, done = lax.optimization_barrier((far_b, done))
    quarter = cut // 2
    far = [(x, n * quarter, (n + 1) * quarter) for n, x in enumerate(far_a + far_b)]
    values, scores = spread(both(far), 6, lists[1:2], done)
    return attend(hidden, cap, relation_ids, slots, values, scores, tiles)


def solution(mesh):
    placed = (
        P("graph", "feat"),
        P("feat", None),
        P(),
        P(),
        P(),
        P(("graph", "feat"), None, None, None),
        P(("graph", "feat"), None),
        P(("graph", "feat"), None, None),
        P(("graph", "feat"), None),
    )
    return jax.shard_map(
        shards, mesh=mesh, in_specs=placed, out_specs=P(("graph", "feat"), None), check_vma=False
    )
```

```python
import functools

import jax
import jax.numpy as jnp
from jax import lax
from jax.experimental import pallas as pl
from jax.experimental.pallas import tpu as pltpu
from jax.sharding import PartitionSpec as P

HEADS = 4
CAP = 4
LOG2E = 1.4426950408889634
F32 = jnp.float32
BF16 = jnp.bfloat16


def arrange_kernel(low, high, core_ref, x_ref, w_ref, out_ref):
    peers, _, columns = out_ref.shape
    total = x_ref.shape[1] // peers
    rows = high - low
    for q in range(peers):
        out_ref[q, :, :rows] = x_ref[:, q * total + low : q * total + high]
        if columns > rows:
            out_ref[q, :, rows:] = w_ref[...]


def arrange(features, weight, core, peers, low, high, half):
    depth, columns = features.shape
    rows = columns // peers
    step = 4
    return pl.pallas_call(
        functools.partial(arrange_kernel, low, high),
        grid_spec=pltpu.PrefetchScalarGridSpec(
            num_scalar_prefetch=1,
            grid=(peers // step,),
            in_specs=[
                pl.BlockSpec((depth, step * rows), lambda i, core_ref: (0, i)),
                pl.BlockSpec((depth, weight.shape[1] // 2), lambda i, core_ref: (0, core_ref[0])),
            ],
            out_specs=pl.BlockSpec((step, depth, high - low + half), lambda i, core_ref: (i, 0, 0)),
        ),
        out_shape=jax.ShapeDtypeStruct((peers, depth, high - low + half), BF16),
        name="arrange",
    )(core.reshape(1), features, weight)


def three_parts(x):
    hi = lax.reduce_precision(x, 8, 7)
    rest = x - hi
    mid = lax.reduce_precision(rest, 8, 7)
    return hi.astype(BF16), mid.astype(BF16), (rest - mid).astype(BF16)


def transform_kernel(bounds, first, *refs):
    index, refs = refs[: len(bounds) // 2], refs[len(bounds) // 2 :]
    n_pieces = sum(len(p) for p in bounds)
    pieces = refs[:n_pieces]
    rw_ref, src_ref = refs[n_pieces : n_pieces + 2]
    val_ref, score_ref, hid_ref = refs[-3:]
    relations, block = val_ref.shape[1:3]
    cap = index[0].shape[1]
    begin = 0
    for source in range(len(bounds)):
        for c in range(cap):
            wanted = index[source // 2][source % 2, c]
            for n, (low, high) in enumerate(bounds[source]):

                @pl.when((wanted >= low) & (wanted < high))
                def _():
                    row = pl.multiple_of((wanted - low) * block, block)
                    hid_ref[source, c * block : (c + 1) * block] = pieces[begin + n][pl.ds(row, block), :]

        begin += len(bounds[source])
    for source in range(len(bounds)):
        hid = hid_ref[source]
        at = (first + source) * cap
        for r in range(relations):
            moved = jnp.dot(hid, rw_ref[r], preferred_element_type=F32).astype(BF16)
            for c in range(cap):
                val_ref[at + c, r] = moved[c * block : (c + 1) * block]
        raw = lax.dot_general(src_ref[...], hid, (((1,), (1,)), ((), ())), preferred_element_type=F32)
        score = raw[0:8] + raw[8:16] + raw[16:24]
        for c in range(cap):
            score_ref[at + c] = score[:, c * block : (c + 1) * block]


def transform(sources, peers, first, index, relation_weight, src_vectors, block, values, scores):
    bounds = tuple(tuple((low, high) for _, low, high in pieces) for pieces in sources)
    arrays = [array for pieces in sources for array, _, _ in pieces]
    cap = index[0].shape[1]
    relations, width = relation_weight.shape[:2]
    inside = pl.BlockSpec(memory_space=pltpu.VMEM)
    kept = () if values is None else (values, scores)
    at = len(index) + len(arrays) + 2
    return pl.pallas_call(
        functools.partial(transform_kernel, bounds, first),
        in_specs=[pl.BlockSpec(memory_space=pltpu.SMEM)] * len(index) + [inside] * (len(arrays) + 2 + len(kept)),
        out_specs=[inside, inside],
        scratch_shapes=[pltpu.VMEM((len(bounds), cap * block, width), BF16)],
        out_shape=[
            jax.ShapeDtypeStruct((peers * cap, relations, block, width), BF16),
            jax.ShapeDtypeStruct((peers * cap, 8, block), F32),
        ],
        input_output_aliases={at + n: n for n in range(len(kept))},
        compiler_params=pltpu.CompilerParams(vmem_limit_bytes=24 * 1024 * 1024),
        name="transform",
    )(*index, *arrays, relation_weight, src_vectors, *kept)


def cap_kernel(mask_ref, cap_ref):
    cap_ref[...] = jnp.where(mask_ref[...] > 0, jnp.inf, 0.0).astype(BF16)


def caps(edge_mask):
    shape = edge_mask.shape
    spec = pl.BlockSpec((1,) + shape[1:], lambda b: (b, 0, 0, 0))
    return pl.pallas_call(
        cap_kernel,
        grid=shape[:1],
        in_specs=[spec],
        out_specs=spec,
        out_shape=jax.ShapeDtypeStruct(shape, BF16),
        name="caps",
    )(edge_mask)


def target_kernel(own_ref, tgt_ref, tile_ref):
    blocks, relations, _, rows, cols = tile_ref.shape

    def body(b, carry):
        own = own_ref[b]
        target = jnp.dot(own, tgt_ref[0], preferred_element_type=F32)
        target += jnp.dot(own, tgt_ref[1], preferred_element_type=F32)
        target += jnp.dot(own, tgt_ref[2], preferred_element_type=F32)
        for r in range(relations):
            for h in range(HEADS):
                c = r * HEADS + h
                tile_ref[b, r, h] = jnp.broadcast_to(target[:, c : c + 1], (rows, cols))
        return carry

    lax.fori_loop(0, blocks, body, 0)


def target_tiles(hidden, tgt_vectors, blocks, relations):
    rows, width = hidden.shape[0] // blocks, hidden.shape[1]
    inside = pl.BlockSpec(memory_space=pltpu.VMEM)
    return pl.pallas_call(
        target_kernel,
        in_specs=[inside, inside],
        out_specs=inside,
        out_shape=jax.ShapeDtypeStruct((blocks, relations, HEADS, rows, rows), F32),
        compiler_params=pltpu.CompilerParams(vmem_limit_bytes=8 * 1024 * 1024),
        name="targets",
    )(hidden.reshape(blocks, rows, width), tgt_vectors)


def attend_kernel(
    rel_ref, slot_ref, own_ref, cap_ref, tile_ref, val_ref, score_ref, out_ref, u_ref, w_ref, prob_ref, least_ref
):
    blocks, lists, rows, cols = cap_ref.shape
    relations = u_ref.shape[1]
    ones = jnp.ones((lists * cols, cols), BF16)

    def parts(b):
        own = own_ref[b]
        rels = [rel_ref[b, k] for k in range(lists)]
        slots = [slot_ref[b, k] for k in range(lists)]

        def spread(r, h):
            return tile_ref[b, r, h]

        def finish(h, weights):
            lanes = slice(h * cols, (h + 1) * cols)
            value = jnp.concatenate([val_ref[slots[k], rels[k], :, lanes] for k in range(lists)], axis=0)
            summed = jnp.dot(weights, jnp.concatenate([value, ones], axis=1), preferred_element_type=F32)
            total = summed[:, cols:]
            mixed = summed[:, :cols] / total + own[:, lanes].astype(F32)
            out_ref[b, :, lanes] = jnp.where(mixed > 0, mixed, jnp.exp(jnp.minimum(mixed, 0.0)) - 1.0).astype(BF16)
            return total

        return rels, slots, spread, finish

    def body(b, carry):
        rels, slots, spread, finish = parts(b)
        reach = [jnp.full((8, cols), -jnp.inf, F32) for _ in range(relations)]
        for k in range(lists):
            source = score_ref[slots[k]]
            for r in range(relations):
                reach[r] = jnp.maximum(reach[r], jnp.where(rels[k] == r, source, -jnp.inf))
        for h in range(HEADS):
            bound = jnp.full((rows, cols), -jnp.inf, F32)
            for r in range(relations):
                c = r * HEADS + h
                most = spread(r, h) + jnp.max(reach[r][c : c + 1, :], axis=1, keepdims=True)
                bound = jnp.maximum(bound, jnp.maximum(most, 0.2 * most))
            for r in range(relations):
                u_ref[h, r] = spread(r, h) - bound
                w_ref[h, r] = 0.2 * spread(r, h) - bound
        least = jnp.full((rows, cols), jnp.inf, F32)
        for h in range(HEADS):
            probs = []
            for k in range(lists):
                source = score_ref[slots[k], pl.ds(rels[k] * HEADS + h, 1), :]
                logit = jnp.maximum(u_ref[h, rels[k]] + source, w_ref[h, rels[k]] + 0.2 * source)
                prob = jnp.exp2(logit).astype(BF16)
                probs.append(jnp.minimum(prob, cap_ref[b, k]))
            least = jnp.minimum(least, finish(h, jnp.concatenate(probs, axis=1)))

        least_ref[...] = jnp.minimum(least_ref[...], least)
        return carry

    least_ref[...] = jnp.full(least_ref.shape, jnp.inf, F32)
    lax.fori_loop(0, blocks, body, 0)

    def redo(b, carry):
        _, _, spread, finish = parts(b)
        for h in range(HEADS):
            for r in range(relations):
                u_ref[h, r] = spread(r, h)

            def raw(k):
                r, slot = rel_ref[b, k], slot_ref[b, k]
                x = u_ref[h, r] + score_ref[slot, pl.ds(r * HEADS + h, 1), :]
                return jnp.where(cap_ref[b, k].astype(F32) > 0, jnp.maximum(x, 0.2 * x), -jnp.inf)

            w_ref[h, 0] = jnp.full((rows, cols), -jnp.inf, F32)

            def climb(k, carry):
                w_ref[h, 0] = jnp.maximum(w_ref[h, 0], raw(k))
                return carry

            lax.fori_loop(0, lists, climb, 0)
            w_ref[h, 0] = jnp.broadcast_to(jnp.max(w_ref[h, 0], axis=1, keepdims=True), (rows, cols))

            def weigh(k, carry):
                at = pl.ds(pl.multiple_of(k * cols, cols), cols)
                prob_ref[h, :, at] = jnp.exp2(raw(k) - w_ref[h, 0]).astype(BF16)
                return carry

            lax.fori_loop(0, lists, weigh, 0)
            finish(h, prob_ref[h])
        return carry

    @pl.when(jnp.logical_not(jnp.min(least_ref[...]) > 2.0**-90))
    def _():
        lax.fori_loop(0, blocks, redo, 0)


def attend(hidden, cap, relation_ids, source_slots, values, scores, tiles):
    blocks, lists, rows, cols = cap.shape
    width = hidden.shape[1]
    relations = values.shape[1]
    scalars, inside = pl.BlockSpec(memory_space=pltpu.SMEM), pl.BlockSpec(memory_space=pltpu.VMEM)
    return pl.pallas_call(
        attend_kernel,
        in_specs=[scalars] * 2 + [inside] * 5,
        out_specs=inside,
        scratch_shapes=[
            pltpu.VMEM((HEADS, relations, rows, cols), F32),
            pltpu.VMEM((HEADS, relations, rows, cols), F32),
            pltpu.VMEM((HEADS, rows, lists * cols), BF16),
            pltpu.VMEM((rows, cols), F32),
        ],
        out_shape=jax.ShapeDtypeStruct((blocks, rows, width), BF16),
        compiler_params=pltpu.CompilerParams(vmem_limit_bytes=24 * 1024 * 1024),
        name="attend",
    )(relation_ids, source_slots, hidden.reshape(blocks, rows, width), cap, tiles, values, scores).reshape(
        blocks * rows, width
    )


def score_vectors(relation_weight, att_source, att_target):
    relations, width = att_source.shape
    head_width = width // HEADS
    split = att_source.reshape(relations, HEADS, head_width)
    moved = jnp.einsum(
        "rche,rhe->rhc",
        relation_weight.astype(F32).reshape(relations, width, HEADS, head_width),
        split,
        precision=lax.Precision.HIGHEST,
        preferred_element_type=F32,
    ).reshape(relations * HEADS, width)
    src = jnp.concatenate(three_parts(moved * LOG2E) + (jnp.zeros((8, width), BF16),), axis=0)
    own_head = (jnp.arange(width)[:, None] // head_width) == (jnp.arange(relations * HEADS)[None, :] % HEADS)
    spread = jnp.repeat(att_target.T, HEADS, axis=1)
    tgt = jnp.where(own_head, spread, 0.0) * LOG2E
    tgt = jnp.pad(tgt, ((0, 0), (0, 128 - relations * HEADS)))
    return src, jnp.stack(three_parts(tgt))


def shards(
    node_features,
    proj_weight,
    relation_weight,
    att_source,
    att_target,
    edge_mask,
    relation_ids,
    send_blocks,
    source_slots,
):
    block_rows = edge_mask.shape[-1]
    local_blocks = edge_mask.shape[0]
    rows_local = local_blocks * block_rows
    depth, width = proj_weight.shape
    n_feat = lax.axis_size("feat")
    n_graph = lax.axis_size("graph")
    levels = n_graph // 2
    place = lax.axis_index("graph")
    core, level = lax.rem(place, 2), place // 2

    def send(x, up, cores=0):
        pairs = [(p, (p + 2 * up) % n_graph ^ cores) for p in range(n_graph)]
        return lax.ppermute(x, "graph", pairs)

    cut = local_blocks // 2
    rows_a, half = cut * block_rows, width // 2
    features = node_features.T
    first = arrange(features, proj_weight, core, n_feat, 0, rows_a, half)
    first, features, send_blocks = lax.optimization_barrier((first, features, send_blocks))
    got = lax.all_to_all(first, "feat", 0, 0, tiled=True).reshape(n_feat * depth, rows_a + half)
    outgoing = arrange(features, proj_weight, core, n_feat, rows_a, rows_local, 0)

    pair = jnp.stack([send_blocks[0], send(send_blocks[0], 0, 1)])
    lists = [pair[:, 2 * ((level + d) % levels) + core] for d in range(levels)]
    peer = source_slots // CAP
    distance = (level - peer // 2 + levels) % levels
    slots = (2 * (distance ^ (distance >> 1)) + (peer % 2 ^ core)) * CAP + source_slots % CAP
    src_vectors, tgt_vectors = score_vectors(relation_weight, att_source, att_target)

    got, outgoing, cap, src_vectors, tgt_vectors, slots, lists = lax.optimization_barrier(
        (got, outgoing, caps(edge_mask), src_vectors, tgt_vectors, slots, lists)
    )
    later = lax.all_to_all(outgoing, "feat", 0, 0, tiled=True).reshape(n_feat * depth, rows_local - rows_a)

    mine = got[:, rows_a:]
    other = send(mine, 0, 1)
    whole = jnp.where(core == 0, jnp.concatenate([mine, other], axis=1), jnp.concatenate([other, mine], axis=1))

    def project(x):
        return lax.dot_general(x, whole, (((0,), (0,)), ((), ())), preferred_element_type=F32).astype(BF16)

    def both(pieces):
        return [pieces, [(send(x, 0, 1), low, high) for x, low, high in pieces]]

    def spread(group, first, index, kept):
        return transform(group, n_graph, first, index, relation_weight, src_vectors, block_rows, *kept)

    def ring(part):
        return send(part, 1), send(part, -1)

    def forward(up, down):
        middle = up.shape[0] // 2
        return send(up[:middle], 1), send(down[middle:], -1)

    a = project(got[:, :rows_a])
    up_a, down_a = ring(a)
    near, lists = lists[:1], [send(lists[d], d) for d in range(1, levels)]
    later, up_a, down_a, lists = lax.optimization_barrier((later, up_a, down_a, lists))
    far_a = forward(up_a, down_a)
    b = project(later)
    up_b, down_b = ring(b)
    done = spread(both([(a, 0, cut), (b, cut, local_blocks)]), 0, near, (None, None))
    hidden = jnp.concatenate([a, b])
    tiles = target_tiles(hidden, tgt_vectors, local_blocks, relation_weight.shape[0])
    swap_up, swap_down = send(up_a, 0, 1), send(down_a, 0, 1)
    up_b, down_b, far_a, tiles, done, swap_up, swap_down = lax.optimization_barrier(
        (up_b, down_b, far_a, tiles, done, swap_up, swap_down)
    )
    far_b = forward(up_b, down_b)
    front, back = (0, cut), (cut, local_blocks)
    rows = [[(up_a, *front), (up_b, *back)], [(swap_up, *front), (send(up_b, 0, 1), *back)]]
    rows += [[(down_a, *front), (down_b, *back)], [(swap_down, *front), (send(down_b, 0, 1), *back)]]
    done = spread(rows, 2, (lists[0], lists[2]), done)
    far_b, done = lax.optimization_barrier((far_b, done))
    quarter = cut // 2
    far = [(x, n * quarter, (n + 1) * quarter) for n, x in enumerate(far_a + far_b)]
    values, scores = spread(both(far), 6, lists[1:2], done)
    return attend(hidden, cap, relation_ids, slots, values, scores, tiles)


def solution(mesh):
    placed = (
        P("graph", "feat"),
        P("feat", None),
        P(),
        P(),
        P(),
        P(("graph", "feat"), None, None, None),
        P(("graph", "feat"), None),
        P(("graph", "feat"), None, None),
        P(("graph", "feat"), None),
    )
    return jax.shard_map(
        shards, mesh=mesh, in_specs=placed, out_specs=P(("graph", "feat"), None), check_vma=False
    )
```

```python
import functools

import jax
import jax.numpy as jnp
from jax import lax
from jax.experimental import pallas as pl
from jax.experimental.pallas import tpu as pltpu
from jax.sharding import PartitionSpec as P

HEADS = 4
CAP = 4
LOG2E = 1.4426950408889634
F32 = jnp.float32
BF16 = jnp.bfloat16


def arrange_kernel(low, high, core_ref, x_ref, w_ref, out_ref):
    peers, _, columns = out_ref.shape
    total = x_ref.shape[1] // peers
    rows = high - low
    for q in range(peers):
        out_ref[q, :, :rows] = x_ref[:, q * total + low : q * total + high]
        if columns > rows:
            out_ref[q, :, rows:] = w_ref[...]


def arrange(features, weight, core, peers, low, high, half):
    depth, columns = features.shape
    rows = columns // peers
    step = 4
    return pl.pallas_call(
        functools.partial(arrange_kernel, low, high),
        grid_spec=pltpu.PrefetchScalarGridSpec(
            num_scalar_prefetch=1,
            grid=(peers // step,),
            in_specs=[
                pl.BlockSpec((depth, step * rows), lambda i, core_ref: (0, i)),
                pl.BlockSpec((depth, weight.shape[1] // 2), lambda i, core_ref: (0, core_ref[0])),
            ],
            out_specs=pl.BlockSpec((step, depth, high - low + half), lambda i, core_ref: (i, 0, 0)),
        ),
        out_shape=jax.ShapeDtypeStruct((peers, depth, high - low + half), BF16),
        name="arrange",
    )(core.reshape(1), features, weight)


def three_parts(x):
    hi = lax.reduce_precision(x, 8, 7)
    rest = x - hi
    mid = lax.reduce_precision(rest, 8, 7)
    return hi.astype(BF16), mid.astype(BF16), (rest - mid).astype(BF16)


def transform_kernel(bounds, first, *refs):
    index, refs = refs[: len(bounds) // 2], refs[len(bounds) // 2 :]
    n_pieces = sum(len(p) for p in bounds)
    pieces = refs[:n_pieces]
    rw_ref, src_ref = refs[n_pieces : n_pieces + 2]
    val_ref, score_ref, hid_ref = refs[-3:]
    relations, block = val_ref.shape[1:3]
    cap = index[0].shape[1]
    begin = 0
    for source in range(len(bounds)):
        for c in range(cap):
            wanted = index[source // 2][source % 2, c]
            for n, (low, high) in enumerate(bounds[source]):

                @pl.when((wanted >= low) & (wanted < high))
                def _():
                    row = pl.multiple_of((wanted - low) * block, block)
                    hid_ref[source, c * block : (c + 1) * block] = pieces[begin + n][pl.ds(row, block), :]

        begin += len(bounds[source])
    for source in range(len(bounds)):
        hid = hid_ref[source]
        at = (first + source) * cap
        for r in range(relations):
            moved = jnp.dot(hid, rw_ref[r], preferred_element_type=F32).astype(BF16)
            for c in range(cap):
                val_ref[at + c, r] = moved[c * block : (c + 1) * block]
        raw = lax.dot_general(src_ref[...], hid, (((1,), (1,)), ((), ())), preferred_element_type=F32)
        score = raw[0:8] + raw[8:16] + raw[16:24]
        for c in range(cap):
            score_ref[at + c] = score[:, c * block : (c + 1) * block]


def transform(sources, peers, first, index, relation_weight, src_vectors, block, values, scores):
    bounds = tuple(tuple((low, high) for _, low, high in pieces) for pieces in sources)
    arrays = [array for pieces in sources for array, _, _ in pieces]
    cap = index[0].shape[1]
    relations, width = relation_weight.shape[:2]
    inside = pl.BlockSpec(memory_space=pltpu.VMEM)
    kept = () if values is None else (values, scores)
    at = len(index) + len(arrays) + 2
    return pl.pallas_call(
        functools.partial(transform_kernel, bounds, first),
        in_specs=[pl.BlockSpec(memory_space=pltpu.SMEM)] * len(index) + [inside] * (len(arrays) + 2 + len(kept)),
        out_specs=[inside, inside],
        scratch_shapes=[pltpu.VMEM((len(bounds), cap * block, width), BF16)],
        out_shape=[
            jax.ShapeDtypeStruct((peers * cap, relations, block, width), BF16),
            jax.ShapeDtypeStruct((peers * cap, 8, block), F32),
        ],
        input_output_aliases={at + n: n for n in range(len(kept))},
        compiler_params=pltpu.CompilerParams(vmem_limit_bytes=24 * 1024 * 1024),
        name="transform",
    )(*index, *arrays, relation_weight, src_vectors, *kept)


def cap_kernel(mask_ref, cap_ref):
    cap_ref[...] = jnp.where(mask_ref[...] > 0, jnp.inf, 0.0).astype(BF16)


def caps(edge_mask):
    shape = edge_mask.shape
    spec = pl.BlockSpec((1,) + shape[1:], lambda b: (b, 0, 0, 0))
    return pl.pallas_call(
        cap_kernel,
        grid=shape[:1],
        in_specs=[spec],
        out_specs=spec,
        out_shape=jax.ShapeDtypeStruct(shape, BF16),
        name="caps",
    )(edge_mask)


def target_kernel(own_ref, tgt_ref, tile_ref):
    blocks, relations, _, rows, cols = tile_ref.shape

    def body(b, carry):
        own = own_ref[b]
        target = jnp.dot(own, tgt_ref[0], preferred_element_type=F32)
        target += jnp.dot(own, tgt_ref[1], preferred_element_type=F32)
        target += jnp.dot(own, tgt_ref[2], preferred_element_type=F32)
        for r in range(relations):
            for h in range(HEADS):
                c = r * HEADS + h
                tile_ref[b, r, h] = jnp.broadcast_to(target[:, c : c + 1], (rows, cols))
        return carry

    lax.fori_loop(0, blocks, body, 0)


def target_tiles(hidden, tgt_vectors, blocks, relations):
    rows, width = hidden.shape[0] // blocks, hidden.shape[1]
    inside = pl.BlockSpec(memory_space=pltpu.VMEM)
    return pl.pallas_call(
        target_kernel,
        in_specs=[inside, inside],
        out_specs=inside,
        out_shape=jax.ShapeDtypeStruct((blocks, relations, HEADS, rows, rows), F32),
        compiler_params=pltpu.CompilerParams(vmem_limit_bytes=8 * 1024 * 1024),
        name="targets",
    )(hidden.reshape(blocks, rows, width), tgt_vectors)


def attend_kernel(
    rel_ref, slot_ref, own_ref, cap_ref, tile_ref, val_ref, score_ref, out_ref, u_ref, w_ref, prob_ref, least_ref
):
    blocks, lists, rows, cols = cap_ref.shape
    relations = u_ref.shape[1]
    ones = jnp.ones((lists * cols, cols), BF16)

    def parts(b):
        own = own_ref[b]
        rels = [rel_ref[b, k] for k in range(lists)]
        slots = [slot_ref[b, k] for k in range(lists)]

        def spread(r, h):
            return tile_ref[b, r, h]

        def finish(h, weights):
            lanes = slice(h * cols, (h + 1) * cols)
            value = jnp.concatenate([val_ref[slots[k], rels[k], :, lanes] for k in range(lists)], axis=0)
            summed = jnp.dot(weights, jnp.concatenate([value, ones], axis=1), preferred_element_type=F32)
            total = summed[:, cols:]
            mixed = summed[:, :cols] / total + own[:, lanes].astype(F32)
            out_ref[b, :, lanes] = jnp.where(mixed > 0, mixed, jnp.exp(jnp.minimum(mixed, 0.0)) - 1.0).astype(BF16)
            return total

        return rels, slots, spread, finish

    def body(b, carry):
        rels, slots, spread, finish = parts(b)
        reach = [jnp.full((8, cols), -jnp.inf, F32) for _ in range(relations)]
        for k in range(lists):
            source = score_ref[slots[k]]
            for r in range(relations):
                reach[r] = jnp.maximum(reach[r], jnp.where(rels[k] == r, source, -jnp.inf))
        for h in range(HEADS):
            bound = jnp.full((rows, cols), -jnp.inf, F32)
            for r in range(relations):
                c = r * HEADS + h
                most = spread(r, h) + jnp.max(reach[r][c : c + 1, :], axis=1, keepdims=True)
                bound = jnp.maximum(bound, jnp.maximum(most, 0.2 * most))
            for r in range(relations):
                u_ref[h, r] = spread(r, h) - bound
                w_ref[h, r] = 0.2 * spread(r, h) - bound
        least = jnp.full((rows, cols), jnp.inf, F32)
        for h in range(HEADS):
            probs = []
            for k in range(lists):
                source = score_ref[slots[k], pl.ds(rels[k] * HEADS + h, 1), :]
                logit = jnp.maximum(u_ref[h, rels[k]] + source, w_ref[h, rels[k]] + 0.2 * source)
                prob = jnp.exp2(logit).astype(BF16)
                probs.append(jnp.minimum(prob, cap_ref[b, k]))
            least = jnp.minimum(least, finish(h, jnp.concatenate(probs, axis=1)))

        least_ref[...] = jnp.minimum(least_ref[...], least)
        return carry

    least_ref[...] = jnp.full(least_ref.shape, jnp.inf, F32)
    lax.fori_loop(0, blocks, body, 0, unroll=2)

    def redo(b, carry):
        _, _, spread, finish = parts(b)
        for h in range(HEADS):
            for r in range(relations):
                u_ref[h, r] = spread(r, h)

            def raw(k):
                r, slot = rel_ref[b, k], slot_ref[b, k]
                x = u_ref[h, r] + score_ref[slot, pl.ds(r * HEADS + h, 1), :]
                return jnp.where(cap_ref[b, k].astype(F32) > 0, jnp.maximum(x, 0.2 * x), -jnp.inf)

            w_ref[h, 0] = jnp.full((rows, cols), -jnp.inf, F32)

            def climb(k, carry):
                w_ref[h, 0] = jnp.maximum(w_ref[h, 0], raw(k))
                return carry

            lax.fori_loop(0, lists, climb, 0)
            w_ref[h, 0] = jnp.broadcast_to(jnp.max(w_ref[h, 0], axis=1, keepdims=True), (rows, cols))

            def weigh(k, carry):
                at = pl.ds(pl.multiple_of(k * cols, cols), cols)
                prob_ref[h, :, at] = jnp.exp2(raw(k) - w_ref[h, 0]).astype(BF16)
                return carry

            lax.fori_loop(0, lists, weigh, 0)
            finish(h, prob_ref[h])
        return carry

    @pl.when(jnp.logical_not(jnp.min(least_ref[...]) > 2.0**-90))
    def _():
        lax.fori_loop(0, blocks, redo, 0)


def finale_kernel(bounds, first, rel_ref, slot_ref, *refs):
    moved = 1 + sum(len(p) for p in bounds) + 2
    own_ref, cap_ref, tile_ref = refs[moved : moved + 3]
    out_ref, val_ref, score_ref, hid_ref, *scratch = refs[moved + 5 :]
    transform_kernel(bounds, first, *refs[:moved], val_ref, score_ref, hid_ref)
    attend_kernel(rel_ref, slot_ref, own_ref, cap_ref, tile_ref, val_ref, score_ref, out_ref, *scratch)


def finale(sources, first, index, relation_weight, src_vectors, hidden, cap, relation_ids, source_slots, values, scores, tiles):
    bounds = tuple(tuple((low, high) for _, low, high in pieces) for pieces in sources)
    arrays = [array for pieces in sources for array, _, _ in pieces]
    blocks, lists, rows, cols = cap.shape
    width = hidden.shape[1]
    relations = values.shape[1]
    scalars, inside = pl.BlockSpec(memory_space=pltpu.SMEM), pl.BlockSpec(memory_space=pltpu.VMEM)
    at = 3 + len(arrays) + 2 + 3
    return pl.pallas_call(
        functools.partial(finale_kernel, bounds, first),
        in_specs=[scalars] * 3 + [inside] * (len(arrays) + 7),
        out_specs=[inside] * 3,
        scratch_shapes=[
            pltpu.VMEM((len(bounds), index.shape[1] * rows, width), BF16),
            pltpu.VMEM((HEADS, relations, rows, cols), F32),
            pltpu.VMEM((HEADS, relations, rows, cols), F32),
            pltpu.VMEM((HEADS, rows, lists * cols), BF16),
            pltpu.VMEM((rows, cols), F32),
        ],
        out_shape=[
            jax.ShapeDtypeStruct((blocks, rows, width), BF16),
            jax.ShapeDtypeStruct(values.shape, BF16),
            jax.ShapeDtypeStruct(scores.shape, F32),
        ],
        input_output_aliases={at: 1, at + 1: 2},
        compiler_params=pltpu.CompilerParams(vmem_limit_bytes=24 * 1024 * 1024),
        name="finale",
    )(
        relation_ids, source_slots, index, *arrays, relation_weight, src_vectors,
        hidden.reshape(blocks, rows, width), cap, tiles, values, scores,
    )[0].reshape(blocks * rows, width)


def score_vectors(relation_weight, att_source, att_target):
    relations, width = att_source.shape
    head_width = width // HEADS
    split = att_source.reshape(relations, HEADS, head_width)
    moved = jnp.einsum(
        "rche,rhe->rhc",
        relation_weight.astype(F32).reshape(relations, width, HEADS, head_width),
        split,
        precision=lax.Precision.HIGHEST,
        preferred_element_type=F32,
    ).reshape(relations * HEADS, width)
    src = jnp.concatenate(three_parts(moved * LOG2E) + (jnp.zeros((8, width), BF16),), axis=0)
    own_head = (jnp.arange(width)[:, None] // head_width) == (jnp.arange(relations * HEADS)[None, :] % HEADS)
    spread = jnp.repeat(att_target.T, HEADS, axis=1)
    tgt = jnp.where(own_head, spread, 0.0) * LOG2E
    tgt = jnp.pad(tgt, ((0, 0), (0, 128 - relations * HEADS)))
    return src, jnp.stack(three_parts(tgt))


def shards(
    node_features,
    proj_weight,
    relation_weight,
    att_source,
    att_target,
    edge_mask,
    relation_ids,
    send_blocks,
    source_slots,
):
    block_rows = edge_mask.shape[-1]
    local_blocks = edge_mask.shape[0]
    rows_local = local_blocks * block_rows
    depth, width = proj_weight.shape
    n_feat = lax.axis_size("feat")
    n_graph = lax.axis_size("graph")
    levels = n_graph // 2
    place = lax.axis_index("graph")
    core, level = lax.rem(place, 2), place // 2

    def send(x, up, cores=0):
        pairs = [(p, (p + 2 * up) % n_graph ^ cores) for p in range(n_graph)]
        return lax.ppermute(x, "graph", pairs)

    cut = local_blocks // 2
    rows_a, half = cut * block_rows, width // 2
    features = node_features.T
    first = arrange(features, proj_weight, core, n_feat, 0, rows_a, half)
    first, features, send_blocks = lax.optimization_barrier((first, features, send_blocks))
    got = lax.all_to_all(first, "feat", 0, 0, tiled=True).reshape(n_feat * depth, rows_a + half)
    outgoing = arrange(features, proj_weight, core, n_feat, rows_a, rows_local, 0)

    pair = jnp.stack([send_blocks[0], send(send_blocks[0], 0, 1)])
    lists = [pair[:, 2 * ((level + d) % levels) + core] for d in range(levels)]
    peer = source_slots // CAP
    distance = (level - peer // 2 + levels) % levels
    slots = (2 * (distance ^ (distance >> 1)) + (peer % 2 ^ core)) * CAP + source_slots % CAP
    src_vectors, tgt_vectors = score_vectors(relation_weight, att_source, att_target)

    got, outgoing, cap, src_vectors, tgt_vectors, slots, lists = lax.optimization_barrier(
        (got, outgoing, caps(edge_mask), src_vectors, tgt_vectors, slots, lists)
    )
    later = lax.all_to_all(outgoing, "feat", 0, 0, tiled=True).reshape(n_feat * depth, rows_local - rows_a)

    mine = got[:, rows_a:]
    other = send(mine, 0, 1)
    whole = jnp.where(core == 0, jnp.concatenate([mine, other], axis=1), jnp.concatenate([other, mine], axis=1))

    def project(x):
        return lax.dot_general(x, whole, (((0,), (0,)), ((), ())), preferred_element_type=F32).astype(BF16)

    def both(pieces):
        return [pieces, [(send(x, 0, 1), low, high) for x, low, high in pieces]]

    def spread(group, first, index, kept):
        return transform(group, n_graph, first, index, relation_weight, src_vectors, block_rows, *kept)

    def ring(part):
        return send(part, 1), send(part, -1)

    def forward(up, down):
        middle = up.shape[0] // 2
        return send(up[:middle], 1), send(down[middle:], -1)

    a = project(got[:, :rows_a])
    up_a, down_a = ring(a)
    near, lists = lists[:1], [send(lists[d], d) for d in range(1, levels)]
    later, up_a, down_a, lists = lax.optimization_barrier((later, up_a, down_a, lists))
    far_a = forward(up_a, down_a)
    b = project(later)
    up_b, down_b = ring(b)
    done = spread(both([(a, 0, cut), (b, cut, local_blocks)]), 0, near, (None, None))
    hidden = jnp.concatenate([a, b])
    tiles = target_tiles(hidden, tgt_vectors, local_blocks, relation_weight.shape[0])
    up_b, down_b, far_a, tiles, done = lax.optimization_barrier((up_b, down_b, far_a, tiles, done))
    far_b = forward(up_b, down_b)
    done = spread(
        both([(up_a, 0, cut), (up_b, cut, local_blocks)]) + both([(down_a, 0, cut), (down_b, cut, local_blocks)]),
        2,
        (lists[0], lists[2]),
        done,
    )
    far_b, done = lax.optimization_barrier((far_b, done))
    quarter = cut // 2
    far = [(x, n * quarter, (n + 1) * quarter) for n, x in enumerate(far_a + far_b)]
    return finale(
        both(far), 6, lists[1], relation_weight, src_vectors, hidden, cap, relation_ids, slots, *done, tiles
    )


def solution(mesh):
    placed = (
        P("graph", "feat"),
        P("feat", None),
        P(),
        P(),
        P(),
        P(("graph", "feat"), None, None, None),
        P(("graph", "feat"), None),
        P(("graph", "feat"), None, None),
        P(("graph", "feat"), None),
    )
    return jax.shard_map(
        shards, mesh=mesh, in_specs=placed, out_specs=P(("graph", "feat"), None), check_vma=False
    )
```

```python
import functools

import jax
import jax.numpy as jnp
from jax import lax
from jax.experimental import pallas as pl
from jax.experimental.pallas import tpu as pltpu
from jax.sharding import PartitionSpec as P

HEADS = 4
CAP = 4
LOG2E = 1.4426950408889634
F32 = jnp.float32
BF16 = jnp.bfloat16


def arrange_kernel(low, high, core_ref, x_ref, w_ref, out_ref, sem):
    peers, _, columns = out_ref.shape
    total = x_ref.shape[1] // peers
    rows = high - low
    copies = [
        pltpu.make_async_copy(
            x_ref.at[:, pl.ds(q * total + low, rows)], out_ref.at[q, :, pl.ds(0, rows)], sem.at[q]
        )
        for q in range(peers)
    ]
    for c in copies:
        c.start()
    if columns > rows:
        half = columns - rows
        share = w_ref[:, pl.ds(pl.multiple_of(core_ref[0] * half, half), half)]
        for q in range(peers):
            out_ref[q, :, rows:] = share
    for c in copies:
        c.wait()


def arrange(features, weight, core, peers, low, high, half):
    depth = features.shape[0]
    inside = pl.BlockSpec(memory_space=pltpu.VMEM)
    return pl.pallas_call(
        functools.partial(arrange_kernel, low, high),
        in_specs=[pl.BlockSpec(memory_space=pltpu.SMEM), pl.BlockSpec(memory_space=pl.ANY), inside],
        out_specs=inside,
        out_shape=jax.ShapeDtypeStruct((peers, depth, high - low + half), BF16),
        scratch_shapes=[pltpu.SemaphoreType.DMA((peers,))],
        name="arrange",
    )(core.reshape(1), features, weight)


def three_parts(x):
    hi = lax.reduce_precision(x, 8, 7)
    rest = x - hi
    mid = lax.reduce_precision(rest, 8, 7)
    return hi.astype(BF16), mid.astype(BF16), (rest - mid).astype(BF16)


def transform_kernel(bounds, first, *refs):
    index, refs = refs[: len(bounds) // 2], refs[len(bounds) // 2 :]
    n_pieces = sum(len(p) for p in bounds)
    pieces = refs[:n_pieces]
    rw_ref, src_ref = refs[n_pieces : n_pieces + 2]
    val_ref, score_ref, hid_ref = refs[-3:]
    relations, block = val_ref.shape[1:3]
    cap = index[0].shape[1]
    begin = 0
    for source in range(len(bounds)):
        for c in range(cap):
            wanted = index[source // 2][source % 2, c]
            for n, (low, high) in enumerate(bounds[source]):

                @pl.when((wanted >= low) & (wanted < high))
                def _():
                    row = pl.multiple_of((wanted - low) * block, block)
                    hid_ref[source, c * block : (c + 1) * block] = pieces[begin + n][pl.ds(row, block), :]

        begin += len(bounds[source])
    for source in range(len(bounds)):
        hid = hid_ref[source]
        at = (first + source) * cap
        for r in range(relations):
            moved = jnp.dot(hid, rw_ref[r], preferred_element_type=F32).astype(BF16)
            for c in range(cap):
                val_ref[at + c, r] = moved[c * block : (c + 1) * block]
        raw = lax.dot_general(src_ref[...], hid, (((1,), (1,)), ((), ())), preferred_element_type=F32)
        score = raw[0:8] + raw[8:16] + raw[16:24]
        for c in range(cap):
            score_ref[at + c] = score[:, c * block : (c + 1) * block]


def transform(sources, peers, first, index, relation_weight, src_vectors, block, values, scores):
    bounds = tuple(tuple((low, high) for _, low, high in pieces) for pieces in sources)
    arrays = [array for pieces in sources for array, _, _ in pieces]
    cap = index[0].shape[1]
    relations, width = relation_weight.shape[:2]
    inside = pl.BlockSpec(memory_space=pltpu.VMEM)
    kept = () if values is None else (values, scores)
    at = len(index) + len(arrays) + 2
    return pl.pallas_call(
        functools.partial(transform_kernel, bounds, first),
        in_specs=[pl.BlockSpec(memory_space=pltpu.SMEM)] * len(index) + [inside] * (len(arrays) + 2 + len(kept)),
        out_specs=[inside, inside],
        scratch_shapes=[pltpu.VMEM((len(bounds), cap * block, width), BF16)],
        out_shape=[
            jax.ShapeDtypeStruct((peers * cap, relations, block, width), BF16),
            jax.ShapeDtypeStruct((peers * cap, 8, block), F32),
        ],
        input_output_aliases={at + n: n for n in range(len(kept))},
        compiler_params=pltpu.CompilerParams(vmem_limit_bytes=24 * 1024 * 1024),
        name="transform",
    )(*index, *arrays, relation_weight, src_vectors, *kept)


def cap_kernel(mask_ref, cap_ref):
    cap_ref[...] = jnp.where(mask_ref[...] > 0, jnp.inf, 0.0).astype(BF16)


def caps(edge_mask):
    shape = edge_mask.shape
    spec = pl.BlockSpec((1,) + shape[1:], lambda b: (b, 0, 0, 0))
    return pl.pallas_call(
        cap_kernel,
        grid=shape[:1],
        in_specs=[spec],
        out_specs=spec,
        out_shape=jax.ShapeDtypeStruct(shape, BF16),
        name="caps",
    )(edge_mask)


def target_kernel(own_ref, tgt_ref, tile_ref):
    blocks, relations, _, rows, cols = tile_ref.shape

    def body(b, carry):
        own = own_ref[b]
        target = jnp.dot(own, tgt_ref[0], preferred_element_type=F32)
        target += jnp.dot(own, tgt_ref[1], preferred_element_type=F32)
        target += jnp.dot(own, tgt_ref[2], preferred_element_type=F32)
        for r in range(relations):
            for h in range(HEADS):
                c = r * HEADS + h
                tile_ref[b, r, h] = jnp.broadcast_to(target[:, c : c + 1], (rows, cols))
        return carry

    lax.fori_loop(0, blocks, body, 0)


def target_tiles(hidden, tgt_vectors, blocks, relations):
    rows, width = hidden.shape[0] // blocks, hidden.shape[1]
    inside = pl.BlockSpec(memory_space=pltpu.VMEM)
    return pl.pallas_call(
        target_kernel,
        in_specs=[inside, inside],
        out_specs=inside,
        out_shape=jax.ShapeDtypeStruct((blocks, relations, HEADS, rows, rows), F32),
        compiler_params=pltpu.CompilerParams(vmem_limit_bytes=8 * 1024 * 1024),
        name="targets",
    )(hidden.reshape(blocks, rows, width), tgt_vectors)


def attend_kernel(
    rel_ref, slot_ref, own_ref, cap_ref, tile_ref, val_ref, score_ref, out_ref, u_ref, w_ref, prob_ref, least_ref
):
    blocks, lists, rows, cols = cap_ref.shape
    relations = u_ref.shape[1]
    ones = jnp.ones((lists * cols, cols), BF16)

    def parts(b):
        own = own_ref[b]
        rels = [rel_ref[b, k] for k in range(lists)]
        slots = [slot_ref[b, k] for k in range(lists)]

        def spread(r, h):
            return tile_ref[b, r, h]

        def finish(h, weights):
            lanes = slice(h * cols, (h + 1) * cols)
            value = jnp.concatenate([val_ref[slots[k], rels[k], :, lanes] for k in range(lists)], axis=0)
            summed = jnp.dot(weights, jnp.concatenate([value, ones], axis=1), preferred_element_type=F32)
            total = summed[:, cols:]
            mixed = summed[:, :cols] / total + own[:, lanes].astype(F32)
            out_ref[b, :, lanes] = jnp.where(mixed > 0, mixed, jnp.exp(jnp.minimum(mixed, 0.0)) - 1.0).astype(BF16)
            return total

        return rels, slots, spread, finish

    def body(b, carry):
        rels, slots, spread, finish = parts(b)
        reach = [jnp.full((8, cols), -jnp.inf, F32) for _ in range(relations)]
        for k in range(lists):
            source = score_ref[slots[k]]
            for r in range(relations):
                reach[r] = jnp.maximum(reach[r], jnp.where(rels[k] == r, source, -jnp.inf))
        for h in range(HEADS):
            bound = jnp.full((rows, cols), -jnp.inf, F32)
            for r in range(relations):
                c = r * HEADS + h
                most = spread(r, h) + jnp.max(reach[r][c : c + 1, :], axis=1, keepdims=True)
                bound = jnp.maximum(bound, jnp.maximum(most, 0.2 * most))
            for r in range(relations):
                u_ref[h, r] = spread(r, h) - bound
                w_ref[h, r] = 0.2 * spread(r, h) - bound
        least = jnp.full((rows, cols), jnp.inf, F32)
        for h in range(HEADS):
            probs = []
            for k in range(lists):
                source = score_ref[slots[k], pl.ds(rels[k] * HEADS + h, 1), :]
                logit = jnp.maximum(u_ref[h, rels[k]] + source, w_ref[h, rels[k]] + 0.2 * source)
                prob = jnp.exp2(logit).astype(BF16)
                probs.append(jnp.minimum(prob, cap_ref[b, k]))
            least = jnp.minimum(least, finish(h, jnp.concatenate(probs, axis=1)))

        least_ref[...] = jnp.minimum(least_ref[...], least)
        return carry

    least_ref[...] = jnp.full(least_ref.shape, jnp.inf, F32)
    lax.fori_loop(0, blocks, body, 0, unroll=2)

    def redo(b, carry):
        _, _, spread, finish = parts(b)
        for h in range(HEADS):
            for r in range(relations):
                u_ref[h, r] = spread(r, h)

            def raw(k):
                r, slot = rel_ref[b, k], slot_ref[b, k]
                x = u_ref[h, r] + score_ref[slot, pl.ds(r * HEADS + h, 1), :]
                return jnp.where(cap_ref[b, k].astype(F32) > 0, jnp.maximum(x, 0.2 * x), -jnp.inf)

            w_ref[h, 0] = jnp.full((rows, cols), -jnp.inf, F32)

            def climb(k, carry):
                w_ref[h, 0] = jnp.maximum(w_ref[h, 0], raw(k))
                return carry

            lax.fori_loop(0, lists, climb, 0)
            w_ref[h, 0] = jnp.broadcast_to(jnp.max(w_ref[h, 0], axis=1, keepdims=True), (rows, cols))

            def weigh(k, carry):
                at = pl.ds(pl.multiple_of(k * cols, cols), cols)
                prob_ref[h, :, at] = jnp.exp2(raw(k) - w_ref[h, 0]).astype(BF16)
                return carry

            lax.fori_loop(0, lists, weigh, 0)
            finish(h, prob_ref[h])
        return carry

    @pl.when(jnp.logical_not(jnp.min(least_ref[...]) > 2.0**-90))
    def _():
        lax.fori_loop(0, blocks, redo, 0)


def finale_kernel(bounds, first, rel_ref, slot_ref, *refs):
    moved = 1 + sum(len(p) for p in bounds) + 2
    own_ref, cap_ref, tile_ref = refs[moved : moved + 3]
    out_ref, val_ref, score_ref, hid_ref, *scratch = refs[moved + 5 :]
    transform_kernel(bounds, first, *refs[:moved], val_ref, score_ref, hid_ref)
    attend_kernel(rel_ref, slot_ref, own_ref, cap_ref, tile_ref, val_ref, score_ref, out_ref, *scratch)


def finale(sources, first, index, relation_weight, src_vectors, hidden, cap, relation_ids, source_slots, values, scores, tiles):
    bounds = tuple(tuple((low, high) for _, low, high in pieces) for pieces in sources)
    arrays = [array for pieces in sources for array, _, _ in pieces]
    blocks, lists, rows, cols = cap.shape
    width = hidden.shape[1]
    relations = values.shape[1]
    scalars, inside = pl.BlockSpec(memory_space=pltpu.SMEM), pl.BlockSpec(memory_space=pltpu.VMEM)
    at = 3 + len(arrays) + 2 + 3
    return pl.pallas_call(
        functools.partial(finale_kernel, bounds, first),
        in_specs=[scalars] * 3 + [inside] * (len(arrays) + 7),
        out_specs=[inside] * 3,
        scratch_shapes=[
            pltpu.VMEM((len(bounds), index.shape[1] * rows, width), BF16),
            pltpu.VMEM((HEADS, relations, rows, cols), F32),
            pltpu.VMEM((HEADS, relations, rows, cols), F32),
            pltpu.VMEM((HEADS, rows, lists * cols), BF16),
            pltpu.VMEM((rows, cols), F32),
        ],
        out_shape=[
            jax.ShapeDtypeStruct((blocks, rows, width), BF16),
            jax.ShapeDtypeStruct(values.shape, BF16),
            jax.ShapeDtypeStruct(scores.shape, F32),
        ],
        input_output_aliases={at: 1, at + 1: 2},
        compiler_params=pltpu.CompilerParams(vmem_limit_bytes=24 * 1024 * 1024),
        name="finale",
    )(
        relation_ids, source_slots, index, *arrays, relation_weight, src_vectors,
        hidden.reshape(blocks, rows, width), cap, tiles, values, scores,
    )[0].reshape(blocks * rows, width)


def score_vectors(relation_weight, att_source, att_target):
    relations, width = att_source.shape
    head_width = width // HEADS
    split = att_source.reshape(relations, HEADS, head_width)
    moved = jnp.einsum(
        "rche,rhe->rhc",
        relation_weight.astype(F32).reshape(relations, width, HEADS, head_width),
        split,
        precision=lax.Precision.HIGHEST,
        preferred_element_type=F32,
    ).reshape(relations * HEADS, width)
    src = jnp.concatenate(three_parts(moved * LOG2E) + (jnp.zeros((8, width), BF16),), axis=0)
    own_head = (jnp.arange(width)[:, None] // head_width) == (jnp.arange(relations * HEADS)[None, :] % HEADS)
    spread = jnp.repeat(att_target.T, HEADS, axis=1)
    tgt = jnp.where(own_head, spread, 0.0) * LOG2E
    tgt = jnp.pad(tgt, ((0, 0), (0, 128 - relations * HEADS)))
    return src, jnp.stack(three_parts(tgt))


def shards(
    node_features,
    proj_weight,
    relation_weight,
    att_source,
    att_target,
    edge_mask,
    relation_ids,
    send_blocks,
    source_slots,
):
    block_rows = edge_mask.shape[-1]
    local_blocks = edge_mask.shape[0]
    rows_local = local_blocks * block_rows
    depth, width = proj_weight.shape
    n_feat = lax.axis_size("feat")
    n_graph = lax.axis_size("graph")
    levels = n_graph // 2
    place = lax.axis_index("graph")
    core, level = lax.rem(place, 2), place // 2

    def send(x, up, cores=0):
        pairs = [(p, (p + 2 * up) % n_graph ^ cores) for p in range(n_graph)]
        return lax.ppermute(x, "graph", pairs)

    cut = local_blocks // 2
    rows_a, half = cut * block_rows, width // 2
    features = node_features.T
    first = arrange(features, proj_weight, core, n_feat, 0, rows_a, half)
    first, features, send_blocks = lax.optimization_barrier((first, features, send_blocks))
    got = lax.all_to_all(first, "feat", 0, 0, tiled=True).reshape(n_feat * depth, rows_a + half)
    outgoing = arrange(features, proj_weight, core, n_feat, rows_a, rows_local, 0)

    pair = jnp.stack([send_blocks[0], send(send_blocks[0], 0, 1)])
    lists = [pair[:, 2 * ((level + d) % levels) + core] for d in range(levels)]
    peer = source_slots // CAP
    distance = (level - peer // 2 + levels) % levels
    slots = (2 * (distance ^ (distance >> 1)) + (peer % 2 ^ core)) * CAP + source_slots % CAP
    src_vectors, tgt_vectors = score_vectors(relation_weight, att_source, att_target)

    got, outgoing, cap, src_vectors, tgt_vectors, slots, lists = lax.optimization_barrier(
        (got, outgoing, caps(edge_mask), src_vectors, tgt_vectors, slots, lists)
    )
    later = lax.all_to_all(outgoing, "feat", 0, 0, tiled=True).reshape(n_feat * depth, rows_local - rows_a)

    mine = got[:, rows_a:]
    other = send(mine, 0, 1)
    whole = jnp.where(core == 0, jnp.concatenate([mine, other], axis=1), jnp.concatenate([other, mine], axis=1))

    def project(x):
        return lax.dot_general(x, whole, (((0,), (0,)), ((), ())), preferred_element_type=F32).astype(BF16)

    def both(pieces):
        return [pieces, [(send(x, 0, 1), low, high) for x, low, high in pieces]]

    def spread(group, first, index, kept):
        return transform(group, n_graph, first, index, relation_weight, src_vectors, block_rows, *kept)

    def ring(part):
        return send(part, 1), send(part, -1)

    def forward(up, down):
        middle = up.shape[0] // 2
        return send(up[:middle], 1), send(down[middle:], -1)

    a = project(got[:, :rows_a])
    up_a, down_a = ring(a)
    near, lists = lists[:1], [send(lists[d], d) for d in range(1, levels)]
    later, up_a, down_a, lists = lax.optimization_barrier((later, up_a, down_a, lists))
    far_a = forward(up_a, down_a)
    b = project(later)
    up_b, down_b = ring(b)
    done = spread(both([(a, 0, cut), (b, cut, local_blocks)]), 0, near, (None, None))
    hidden = jnp.concatenate([a, b])
    tiles = target_tiles(hidden, tgt_vectors, local_blocks, relation_weight.shape[0])
    up_b, down_b, far_a, tiles, done = lax.optimization_barrier((up_b, down_b, far_a, tiles, done))
    far_b = forward(up_b, down_b)
    done = spread(
        both([(up_a, 0, cut), (up_b, cut, local_blocks)]) + both([(down_a, 0, cut), (down_b, cut, local_blocks)]),
        2,
        (lists[0], lists[2]),
        done,
    )
    far_b, done = lax.optimization_barrier((far_b, done))
    quarter = cut // 2
    far = [(x, n * quarter, (n + 1) * quarter) for n, x in enumerate(far_a + far_b)]
    return finale(
        both(far), 6, lists[1], relation_weight, src_vectors, hidden, cap, relation_ids, slots, *done, tiles
    )


def solution(mesh):
    placed = (
        P("graph", "feat"),
        P("feat", None),
        P(),
        P(),
        P(),
        P(("graph", "feat"), None, None, None),
        P(("graph", "feat"), None),
        P(("graph", "feat"), None, None),
        P(("graph", "feat"), None),
    )
    return jax.shard_map(
        shards, mesh=mesh, in_specs=placed, out_specs=P(("graph", "feat"), None), check_vma=False
    )
```
